32 devices in a mesh: dp: 8 (over y, x, core), mp: 4 (over z).
Axes of the slice: x: 2, y: 2, z: 4, core: 2. Of those that a mesh axis runs over, the one named last changes fastest.
Arguments:
- tokens: bfloat16 [4, 3136, 768], P(None, ('dp', 'mp')), may hold values from -6 to 6
- cotangent: bfloat16 [4, 3136, 768], P(None, ('dp', 'mp')), may hold values from -6 to 6
- clip_adapter: int32 [4], replicated, may hold values from 0 to 7
- gain_one: float32 [768], replicated, may hold values from 0.1 to 1.9
- gain_two: float32 [768], replicated, may hold values from 0.1 to 1.9
- w_qkv: bfloat16 [768, 3, 768], P('dp', None, 'mp'), may hold values from -0.21875 to 0.21875
- w_out: bfloat16 [768, 768], P('mp', 'dp'), may hold values from -1.75 to 1.75
- w_up: bfloat16 [768, 3072], P('dp', 'mp'), may hold values from -0.21875 to 0.21875
- w_down: bfloat16 [3072, 768], P('mp', 'dp'), may hold values from -0.109375 to 0.109375
- adapters: float32 [128, 12288], P(None, ('dp', 'mp'))
- moment_one: float32 [128, 12288], P(None, ('dp', 'mp')), may hold values from -128 to 128
- moment_two: float32 [128, 12288], P(None, ('dp', 'mp')), may hold values from 392 to 1568
Outputs:
- activations: bfloat16 [4, 3136, 768], P(None, ('dp', 'mp'))
- input_grad: bfloat16 [4, 3136, 768], P(None, ('dp', 'mp'))
- adapter_grad: float32 [128, 12288], P(None, ('dp', 'mp'))
- new_adapters: float32 [128, 12288], P(None, ('dp', 'mp'))
- new_moment_one: float32 [128, 12288], P(None, ('dp', 'mp'))
- new_moment_two: float32 [128, 12288], P(None, ('dp', 'mp'))
- adapter_copy: bfloat16 [128, 12288], P(None, ('dp', 'mp'))
The draws below stay inside these ranges and needn't reach their ends.
All inputs are finite; a program needn't handle non-finite values.
Results may differ from the reference program's by a relative error of at most 0.017.
Values may be sent and summed in bfloat16 or wider, within the bound.
A program may use at most 192 MiB of HBM per device.

```python
import math
import jax
import jax.numpy as jnp
from jax import lax

D = 768
HEADS = 12
FF = 3072
HEAD = 64
FRAME = 196
ADAPTERS = 8
RANK = 16
MICRO = 4
FPM = 2
CLIP_FRAMES = 16
STEP = 5
AR = 128
WIDE = 12288
TOKM = 3136
CLIPS = 4
N_DP = 8


def draw_adapters(key, part):
    key = jax.random.fold_in(key, 7)
    total_width = 8 * D + 2 * FF
    column = jnp.arange(total_width)
    spread = jnp.full((total_width,), 0.075, jnp.float32)
    spread = jnp.where(column < D, D ** (-0.5), spread)
    spread = jnp.where((column >= 4 * D) & (column < 5 * D), 4.0 * D ** (-0.5), spread)
    spread = jnp.where((column >= 5 * D) & (column < 6 * D), 0.13, spread)
    spread = jnp.where((column >= 6 * D) & (column < 7 * D), D ** (-0.5), spread)
    spread = jnp.where((column >= 7 * D + FF) & (column < 7 * D + 2 * FF), 2.0 * FF ** (-0.5), spread)
    values = jax.random.normal(key, (ADAPTERS * RANK, total_width), jnp.float32)
    return values * spread[None, :]


def plant(result, stream_key, smallest, top_value):
    longest = result.shape.index(max(result.shape))
    spots = []
    for shift in (0, 1):
        where = [jax.random.randint(jax.random.fold_in(stream_key, axis), (), 0, length) for axis, length in enumerate(result.shape)]
        where[longest] = (where[longest] + shift) % result.shape[longest]
        spots.append(tuple(where))
    return result.at[spots[0]].set(smallest).at[spots[1]].set(top_value)


def block_levels(key, extent, cuts, least, top_value):
    def one(position, parts):
        draws = jax.random.uniform(jax.random.fold_in(jax.random.fold_in(key, 6), position), (parts,), jnp.float32, least / len(cuts), top_value / len(cuts))
        return jnp.repeat(jnp.exp(draws), extent[position] // parts).reshape((-1,) + (1,) * (len(extent) - position - 1))

    level = one(*cuts[0])
    for cut in cuts[1:]:
        level = level * one(*cut)
    return level


def gaussian(stream_key, shape, deviation, limit, cuts=(), held_as=jnp.bfloat16):
    level = block_levels(stream_key, shape, cuts, -0.22, 0.18) if cuts else 1.0
    entries = jax.random.normal(stream_key, shape, jnp.float32) * deviation * level
    return jnp.minimum(jnp.maximum(entries, -limit), limit).astype(held_as)


def setup_inputs(seed: int = 0) -> dict:
    keys = jax.random.split(jax.random.key(seed), 13)
    tokens = gaussian(keys[0], (MICRO, TOKM, D), 1.0, 6.0, ((1, 32),))
    cotangent = gaussian(keys[1], (MICRO, TOKM, D), 1.0, 6.0, ((1, 32),))
    clip_adapter = plant(jax.random.randint(keys[2], (CLIPS,), 0, ADAPTERS), jax.random.fold_in(keys[2], 1), 0, ADAPTERS - 1).astype(jnp.int32)
    gain_one = jnp.clip(1.0 + 0.18 * jax.random.normal(keys[3], (D,), jnp.float32), 0.1, 1.9)
    gain_two = jnp.clip(1.0 + 0.18 * jax.random.normal(keys[4], (D,), jnp.float32), 0.1, 1.9)
    w_qkv = gaussian(keys[5], (D, 3, D), D ** -0.5, 0.21875, ((0, 8), (2, 4)))
    w_out = gaussian(keys[6], (D, D), (3 * D // FRAME) ** -0.5, 1.75, ((0, 4), (1, 8)))
    w_up = gaussian(keys[7], (D, FF), D ** -0.5, 0.21875, ((0, 8), (1, 4)))
    w_down = gaussian(keys[8], (FF, D), FF ** -0.5, 0.109375, ((0, 4), (1, 8)))
    adapters = draw_adapters(jax.random.fold_in(keys[12], 71), 0)
    moment_one = gaussian(keys[10], (AR, WIDE), (0.5 * (MICRO * N_DP * FPM * FRAME // ADAPTERS) ** 0.5), 128.0, ((1, 32),), jnp.float32)
    moment_two = jnp.clip(jnp.exp(math.log(1568.0) - 1.3862944 * jax.random.uniform(keys[11], (AR, WIDE), jnp.float32) ** block_levels(keys[11], (AR, WIDE), ((1, 32),), -0.2, 0.2)), 392.0, 1568.0)
    return {"tokens": tokens, "cotangent": cotangent, "clip_adapter": clip_adapter, "gain_one": gain_one, "gain_two": gain_two, "w_qkv": w_qkv, "w_out": w_out, "w_up": w_up, "w_down": w_down, "adapters": adapters, "moment_one": moment_one, "moment_two": moment_two}


@jax.custom_vjp
def low(v):
    return lax.optimization_barrier(v.astype(jnp.bfloat16)).astype(jnp.float32)

@jax.custom_vjp
def low_back(v):
    return v

def low_keep(v):
    return (low(v), None)

def low_pass(kept, grad):
    return (grad,)

def back_keep(v):
    return (v, None)

def back_low(kept, grad):
    return (low(grad),)
low.defvjp(low_keep, low_pass)
low_back.defvjp(back_keep, back_low)
norm_epsilon = 1e-06
beta_first = 0.5
beta_second = 0.5
learn_rate = 0.05
weight_decay = 0.01
adam_epsilon = 1e-08
block_frames = 16
highest = lax.Precision.HIGHEST

def product(left_side, right_side):
    return jnp.dot(left_side, right_side, precision=highest, preferred_element_type=jnp.float32)

def normalize(values_in, gain):
    center = values_in - lax.optimization_barrier(jnp.mean(values_in, axis=-1, keepdims=True))
    spread = lax.optimization_barrier(jnp.mean(center * center, axis=-1, keepdims=True))
    return center * lax.rsqrt(spread + norm_epsilon) * gain

def block_layer(inputs, adapter_values, selector, qkv_weight, out_weight, up_weight, down_weight, gain_one, gain_two):
    a_qkv = adapter_values[:, 0:D]
    b_qkv = adapter_values[:, D:4 * D]
    a_out = adapter_values[:, 4 * D:5 * D]
    b_out = adapter_values[:, 5 * D:6 * D]
    a_up = adapter_values[:, 6 * D:7 * D]
    b_up = adapter_values[:, 7 * D:7 * D + FF]
    a_down = adapter_values[:, 7 * D + FF:7 * D + 2 * FF]
    b_down = adapter_values[:, 7 * D + 2 * FF:]
    frames = inputs.shape[0] // FRAME
    score_scale = 1.0 / math.sqrt(HEAD)
    normed_one = low(normalize(inputs, gain_one))
    low_qkv = product(normed_one, a_qkv.T) * selector
    projected = product(normed_one, qkv_weight.reshape(D, 3 * D)) + product(low_qkv, b_qkv)
    projected = low_back(low(projected))
    queries = projected[:, 0:D].reshape(frames, FRAME, HEADS, HEAD)
    key_rows = projected[:, D:2 * D].reshape(frames, FRAME, HEADS, HEAD)
    value_rows = projected[:, 2 * D:].reshape(frames, FRAME, HEADS, HEAD)
    scores = low_back(jnp.einsum('fqhd,fkhd->fhqk', queries, key_rows, precision=highest) * score_scale)
    soft_weights = jax.nn.softmax(scores, axis=-1)
    attended = jnp.einsum('fhqk,fkhd->fqhd', low(soft_weights), value_rows, precision=highest).reshape(-1, D)
    attended = low_back(low(attended))
    branch = product(attended, out_weight) + product(product(attended, a_out.T) * selector, b_out)
    branch = low_back(branch)
    middle = inputs + branch
    normed_two = low(normalize(middle, gain_two))
    hidden = product(normed_two, up_weight) + product(product(normed_two, a_up.T) * selector, b_up)
    hidden = low_back(hidden)
    active = low(jax.nn.gelu(hidden, approximate=False))
    feed = product(active, down_weight) + product(product(active, a_down.T) * selector, b_down)
    return middle + feed

def reference(tokens, cotangent, clip_adapter, gain_one, gain_two, w_qkv, w_out, w_up, w_down, adapters, moment_one, moment_two):
    frame_total = MICRO * TOKM // FRAME
    block_count = frame_total // block_frames
    rows_block = block_frames * FRAME
    inputs = tokens.astype(jnp.float32).reshape(block_count, rows_block, D)
    grads_in = cotangent.astype(jnp.float32).reshape(block_count, rows_block, D)
    frame_index = jnp.arange(frame_total, dtype=jnp.int32)
    frame_adapter = clip_adapter[frame_index // CLIP_FRAMES].reshape(block_count, block_frames)
    rounded = adapters.astype(jnp.bfloat16).astype(jnp.float32)
    qkv_float = w_qkv.astype(jnp.float32)
    out_float = w_out.astype(jnp.float32)
    up_float = w_up.astype(jnp.float32)
    down_float = w_down.astype(jnp.float32)
    column_adapter = jnp.arange(ADAPTERS * RANK, dtype=jnp.int32) // RANK

    def one_block(running, block_item):
        block_inputs, block_grads, block_adapter = block_item
        row_adapter = jnp.repeat(block_adapter, FRAME)
        selector = (row_adapter[:, None] == column_adapter[None, :]).astype(jnp.float32)

        def forward(inputs_here, adapter_here):
            return block_layer(inputs_here, adapter_here, selector, qkv_float, out_float, up_float, down_float, gain_one, gain_two)
        outputs, pullback = jax.vjp(forward, block_inputs, rounded)
        input_grad, adapter_grad = pullback(block_grads)
        return (running + adapter_grad, (outputs.astype(jnp.bfloat16), input_grad.astype(jnp.bfloat16)))
    start = jnp.zeros((ADAPTERS * RANK, 8 * D + 2 * FF), jnp.float32)
    gradient, (outputs, input_grads) = lax.scan(one_block, start, (inputs, grads_in, frame_adapter))
    first_moment = beta_first * moment_one + (1.0 - beta_first) * gradient
    second_moment = beta_second * moment_two + (1.0 - beta_second) * gradient * gradient
    first_hat = first_moment / (1.0 - beta_first ** STEP)
    second_hat = second_moment / (1.0 - beta_second ** STEP)
    updated = adapters - learn_rate * (first_hat / (jnp.sqrt(second_hat) + adam_epsilon) + weight_decay * adapters)
    return (outputs.reshape(MICRO, TOKM, D), input_grads.reshape(MICRO, TOKM, D), gradient, updated, first_moment, second_moment, updated.astype(jnp.bfloat16))
```

```python
import math

import jax
import jax.numpy as jnp
from jax import lax
from jax.sharding import PartitionSpec as P

HEAD = 64
FRAME = 196
RANK = 16
CLIP_FRAMES = 16
STEP = 5

norm_epsilon = 1e-06
beta_first = 0.5
beta_second = 0.5
learn_rate = 0.05
weight_decay = 0.01
adam_epsilon = 1e-08


def dot(left, right):
    return jnp.dot(left, right, preferred_element_type=jnp.float32)


def dot_t(left, right):
    return lax.dot_general(left, right, (((1,), (1,)), ((), ())), preferred_element_type=jnp.float32)


def t_dot(left, right):
    return lax.dot_general(left, right, (((0,), (0,)), ((), ())), preferred_element_type=jnp.float32)


def half(values):
    return values.astype(jnp.bfloat16)


def norm_parts(values):
    center = values - jnp.mean(values, axis=-1, keepdims=True)
    spread = jnp.mean(center * center, axis=-1, keepdims=True)
    inverse = lax.rsqrt(spread + norm_epsilon)
    return center * inverse, inverse


def norm_back(unit, inverse, gain, grad):
    scaled = grad * gain
    first = jnp.mean(scaled, axis=-1, keepdims=True)
    second = jnp.mean(scaled * unit, axis=-1, keepdims=True)
    return inverse * (scaled - first - unit * second)


def shards(
    tokens,
    cotangent,
    clip_adapter,
    gain_one,
    gain_two,
    w_qkv,
    w_out,
    w_up,
    w_down,
    adapters,
    moment_one,
    moment_two,
):
    groups = lax.axis_size("mp")
    member = lax.axis_index("mp")
    group_index = lax.axis_index("dp")
    micro_count, shard_rows, width = tokens.shape
    hidden_width = w_up.shape[1] * groups
    heads = width // HEAD
    rank_all = adapters.shape[0]
    full_width = adapters.shape[1] * lax.axis_size(("dp", "mp"))
    frames = shard_rows * groups // FRAME
    frames_micro = frames * lax.axis_size("dp")
    scale = 1.0 / math.sqrt(HEAD)
    span = FRAME // shard_rows
    mine = micro_count // span
    part = member % span
    pairs = [[first * span + k for k in range(span)] for first in range(groups // span)]

    def swap(rows):
        return lax.all_to_all(
            rows, "mp", split_axis=0, concat_axis=1, axis_index_groups=pairs, tiled=True
        ).reshape(mine * FRAME, width)

    def swap_back(rows):
        return lax.all_to_all(
            rows.reshape(mine, FRAME, width),
            "mp",
            split_axis=1,
            concat_axis=0,
            axis_index_groups=pairs,
            tiled=True,
        )

    inputs = swap(tokens).astype(jnp.float32)
    dy = swap(cotangent)

    def whole(weight, first, second):
        return lax.all_gather(
            lax.all_gather(weight, first[0], axis=first[1], tiled=True),
            second[0],
            axis=second[1],
            tiled=True,
        )

    qkv_all = whole(w_qkv, ("dp", 0), ("mp", 2)).reshape(width, 3 * width)
    out_all = whole(w_out, ("dp", 1), ("mp", 0))
    up_all = whole(w_up, ("dp", 0), ("mp", 1))
    down_all = whole(w_down, ("dp", 1), ("mp", 0))
    table = lax.all_gather(half(adapters), ("dp", "mp"), axis=1, tiled=True)
    table = table.reshape(rank_all // RANK, RANK, full_width)
    clips = jnp.stack(
        [
            ((part * mine + i) * frames_micro + group_index * frames + member // span)
            // CLIP_FRAMES
            for i in range(mine)
        ]
    )
    chosen = clip_adapter[clips]
    own = table[chosen].reshape(mine * RANK, full_width)
    ends = [0, width, 4 * width, 5 * width, 6 * width, 7 * width]
    ends += [7 * width + hidden_width, 7 * width + 2 * hidden_width, full_width]
    a_qkv, b_qkv, a_out, b_out, a_up, b_up, a_down, b_down = [
        own[:, ends[i] : ends[i + 1]] for i in range(8)
    ]
    rows = mine * FRAME
    row_frame = lax.broadcasted_iota(jnp.int32, (rows, mine * RANK), 0) // FRAME
    column_frame = lax.broadcasted_iota(jnp.int32, (rows, mine * RANK), 1) // RANK
    mask = row_frame == column_frame

    def low(values):
        return half(jnp.where(mask, values, 0.0))

    shape_heads = (mine, FRAME, heads, HEAD)
    unit_one, inverse_one = norm_parts(inputs)
    normed_one = half(unit_one * gain_one)
    low_qkv = low(dot_t(normed_one, a_qkv))
    projected = half(dot(normed_one, qkv_all) + dot(low_qkv, b_qkv))
    queries = projected[:, 0:width].reshape(shape_heads)
    keys = projected[:, width : 2 * width].reshape(shape_heads)
    values = projected[:, 2 * width :].reshape(shape_heads)
    scores = jnp.einsum("fqhd,fkhd->fhqk", queries, keys, preferred_element_type=jnp.float32)
    scores = scores * scale
    exponent = jnp.exp(scores - jnp.max(scores, axis=-1, keepdims=True))
    soft = exponent / jnp.sum(exponent, axis=-1, keepdims=True)
    soft_half = half(soft)
    attended = half(
        jnp.einsum("fhqk,fkhd->fqhd", soft_half, values, preferred_element_type=jnp.float32)
    ).reshape(rows, width)
    low_out = low(dot_t(attended, a_out))
    middle = inputs + dot(attended, out_all) + dot(low_out, b_out)
    unit_two, inverse_two = norm_parts(middle)
    normed_two = half(unit_two * gain_two)
    low_up = low(dot_t(normed_two, a_up))
    hidden = dot(normed_two, up_all) + dot(low_up, b_up)
    phi = 0.5 * (1.0 + lax.erf(hidden * math.sqrt(0.5)))
    active = half(hidden * phi)
    slope = phi + hidden * jnp.exp(-0.5 * hidden * hidden) * (1.0 / math.sqrt(2.0 * math.pi))
    low_down = low(dot_t(active, a_down))
    outputs = half(middle + dot(active, down_all) + dot(low_down, b_down))

    through_down = low(dot_t(dy, b_down))
    d_active = dot_t(dy, down_all) + dot(through_down, a_down)
    d_hidden = half(d_active * slope)
    through_up = low(dot_t(d_hidden, b_up))
    d_normed_two = dot_t(d_hidden, up_all) + dot(through_up, a_up)
    d_middle = dy.astype(jnp.float32) + norm_back(unit_two, inverse_two, gain_two, d_normed_two)
    d_branch = half(d_middle)
    through_out = low(dot_t(d_branch, b_out))
    d_attended = half(dot_t(d_branch, out_all) + dot(through_out, a_out))
    d_heads = d_attended.reshape(shape_heads)
    d_values = jnp.einsum("fhqk,fqhd->fkhd", soft_half, d_heads, preferred_element_type=jnp.float32)
    d_soft = jnp.einsum("fqhd,fkhd->fhqk", d_heads, values, preferred_element_type=jnp.float32)
    inner = jnp.sum(soft * d_soft, axis=-1, keepdims=True)
    d_scores = half(soft * (d_soft - inner))
    d_queries = scale * jnp.einsum(
        "fhqk,fkhd->fqhd", d_scores, keys, preferred_element_type=jnp.float32
    )
    d_keys = scale * jnp.einsum(
        "fhqk,fqhd->fkhd", d_scores, queries, preferred_element_type=jnp.float32
    )
    d_projected = half(
        jnp.concatenate([d.reshape(rows, width) for d in (d_queries, d_keys, d_values)], axis=1)
    )
    through_qkv = low(dot_t(d_projected, b_qkv))
    d_normed_one = dot_t(d_projected, qkv_all) + dot(through_qkv, a_qkv)
    input_grad = half(d_middle + norm_back(unit_one, inverse_one, gain_one, d_normed_one))
    grads = half(jnp.concatenate(
        [
            t_dot(through_qkv, normed_one),
            t_dot(low_qkv, d_projected),
            t_dot(through_out, attended),
            t_dot(low_out, d_branch),
            t_dot(through_up, normed_two),
            t_dot(low_up, d_hidden),
            t_dot(through_down, active),
            t_dot(low_down, dy),
        ],
        axis=1,
    ))
    pick = (
        lax.broadcasted_iota(jnp.int32, (rank_all, mine * RANK), 0)
        == jnp.repeat(chosen, RANK)[None, :] * RANK
        + lax.broadcasted_iota(jnp.int32, (rank_all, mine * RANK), 1) % RANK
    ).astype(jnp.bfloat16)
    owner_grad = lax.psum_scatter(
        dot(pick, grads), ("dp", "mp"), scatter_dimension=1, tiled=True
    )
    first_moment = beta_first * moment_one + (1.0 - beta_first) * owner_grad
    second_moment = beta_second * moment_two + (1.0 - beta_second) * owner_grad * owner_grad
    first_hat = first_moment / (1.0 - beta_first**STEP)
    second_hat = second_moment / (1.0 - beta_second**STEP)
    updated = adapters - learn_rate * (
        first_hat / (jnp.sqrt(second_hat) + adam_epsilon) + weight_decay * adapters
    )
    return (
        swap_back(outputs),
        swap_back(input_grad),
        owner_grad,
        updated,
        first_moment,
        second_moment,
        updated.astype(jnp.bfloat16),
    )


def solution(mesh):
    spread = P(None, ("dp", "mp"))
    rows = P(None, ("dp", "mp"), None)
    return jax.shard_map(
        shards,
        mesh=mesh,
        in_specs=(
            rows,
            rows,
            P(),
            P(),
            P(),
            P("dp", None, "mp"),
            P("mp", "dp"),
            P("dp", "mp"),
            P("mp", "dp"),
            spread,
            spread,
            spread,
        ),
        out_specs=(rows, rows, spread, spread, spread, spread, spread),
        check_vma=False,
    )
```

```python
import math

import jax
import jax.numpy as jnp
from jax import lax
from jax.experimental import pallas as pl
from jax.experimental.pallas import tpu as pltpu
from jax.sharding import PartitionSpec as P

HEAD = 64
FRAME = 196
RANK = 16
CLIP_FRAMES = 16
STEP = 5

norm_epsilon = 1e-06
beta_first = 0.5
beta_second = 0.5
learn_rate = 0.05
weight_decay = 0.01
adam_epsilon = 1e-08


def dot(left, right):
    return jnp.dot(left, right, preferred_element_type=jnp.float32)


def dot_t(left, right):
    return lax.dot_general(left, right, (((1,), (1,)), ((), ())), preferred_element_type=jnp.float32)


def t_dot(left, right):
    return lax.dot_general(left, right, (((0,), (0,)), ((), ())), preferred_element_type=jnp.float32)


def half(values):
    return values.astype(jnp.bfloat16)


def norm_parts(values):
    center = values - jnp.mean(values, axis=-1, keepdims=True)
    spread = jnp.mean(center * center, axis=-1, keepdims=True)
    inverse = lax.rsqrt(spread + norm_epsilon)
    return center * inverse, inverse


def norm_back(unit, inverse, gain, grad):
    scaled = grad * gain
    first = jnp.mean(scaled, axis=-1, keepdims=True)
    second = jnp.mean(scaled * unit, axis=-1, keepdims=True)
    return inverse * (scaled - first - unit * second)


def adam(owner_grad, adapters, moment_one, moment_two):
    first_moment = beta_first * moment_one + (1.0 - beta_first) * owner_grad
    second_moment = beta_second * moment_two + (1.0 - beta_second) * owner_grad * owner_grad
    first_hat = first_moment / (1.0 - beta_first**STEP)
    second_hat = second_moment / (1.0 - beta_second**STEP)
    updated = adapters - learn_rate * (
        first_hat / (jnp.sqrt(second_hat) + adam_epsilon) + weight_decay * adapters
    )
    return (
        owner_grad,
        updated,
        first_moment,
        second_moment,
        updated.astype(jnp.bfloat16),
    )


def shards(
    tokens,
    cotangent,
    clip_adapter,
    gain_one,
    gain_two,
    w_qkv,
    w_out,
    w_up,
    w_down,
    adapters,
    moment_one,
    moment_two,
):
    groups = lax.axis_size("mp")
    member = lax.axis_index("mp")
    group_index = lax.axis_index("dp")
    micro_count, shard_rows, width = tokens.shape
    hidden_width = w_up.shape[1] * groups
    heads = width // HEAD
    rank_all = adapters.shape[0]
    full_width = adapters.shape[1] * lax.axis_size(("dp", "mp"))
    frames = shard_rows * groups // FRAME
    frames_micro = frames * lax.axis_size("dp")
    scale = 1.0 / math.sqrt(HEAD)
    span = FRAME // shard_rows
    mine = micro_count // span
    part = member % span
    pairs = [[first * span + k for k in range(span)] for first in range(groups // span)]

    def swap(rows):
        return lax.all_to_all(
            rows, "mp", split_axis=0, concat_axis=1, axis_index_groups=pairs, tiled=True
        ).reshape(mine * FRAME, width)

    def swap_back(rows):
        return lax.all_to_all(
            rows.reshape(mine, FRAME, width),
            "mp",
            split_axis=1,
            concat_axis=0,
            axis_index_groups=pairs,
            tiled=True,
        )

    inputs = swap(tokens).astype(jnp.float32)
    dy = swap(cotangent)

    def whole(weight, first, second):
        return lax.all_gather(
            lax.all_gather(weight, first[0], axis=first[1], tiled=True),
            second[0],
            axis=second[1],
            tiled=True,
        )

    qkv_all = whole(w_qkv, ("dp", 0), ("mp", 2)).reshape(width, 3 * width)
    out_all = whole(w_out, ("dp", 1), ("mp", 0))
    up_all = whole(w_up, ("dp", 0), ("mp", 1))
    down_all = whole(w_down, ("dp", 1), ("mp", 0))
    table = lax.all_gather(half(adapters), ("dp", "mp"), axis=1, tiled=True)
    table = table.reshape(rank_all // RANK, RANK, full_width)
    clips = jnp.stack(
        [
            ((part * mine + i) * frames_micro + group_index * frames + member // span)
            // CLIP_FRAMES
            for i in range(mine)
        ]
    )
    chosen = clip_adapter[clips]
    own = table[chosen].reshape(mine * RANK, full_width)
    ends = [0, width, 4 * width, 5 * width, 6 * width, 7 * width]
    ends += [7 * width + hidden_width, 7 * width + 2 * hidden_width, full_width]
    a_qkv, b_qkv, a_out, b_out, a_up, b_up, a_down, b_down = [
        own[:, ends[i] : ends[i + 1]] for i in range(8)
    ]
    rows = mine * FRAME
    row_frame = lax.broadcasted_iota(jnp.int32, (rows, mine * RANK), 0) // FRAME
    column_frame = lax.broadcasted_iota(jnp.int32, (rows, mine * RANK), 1) // RANK
    mask = row_frame == column_frame

    def low(values):
        return half(jnp.where(mask, values, 0.0))

    shape_heads = (mine, FRAME, heads, HEAD)
    unit_one, inverse_one = norm_parts(inputs)
    normed_one = half(unit_one * gain_one)
    low_qkv = low(dot_t(normed_one, a_qkv))
    projected = half(dot(normed_one, qkv_all) + dot(low_qkv, b_qkv))
    queries = projected[:, 0:width].reshape(shape_heads)
    keys = projected[:, width : 2 * width].reshape(shape_heads)
    values = projected[:, 2 * width :].reshape(shape_heads)
    scores = jnp.einsum("fqhd,fkhd->fhqk", queries, keys, preferred_element_type=jnp.float32)
    scores = scores * scale
    exponent = jnp.exp(scores - jnp.max(scores, axis=-1, keepdims=True))
    soft = exponent / jnp.sum(exponent, axis=-1, keepdims=True)
    soft_half = half(soft)
    attended = half(
        jnp.einsum("fhqk,fkhd->fqhd", soft_half, values, preferred_element_type=jnp.float32)
    ).reshape(rows, width)
    low_out = low(dot_t(attended, a_out))
    middle = inputs + dot(attended, out_all) + dot(low_out, b_out)
    unit_two, inverse_two = norm_parts(middle)
    normed_two = half(unit_two * gain_two)
    low_up = low(dot_t(normed_two, a_up))
    hidden = dot(normed_two, up_all) + dot(low_up, b_up)
    phi = 0.5 * (1.0 + lax.erf(hidden * math.sqrt(0.5)))
    active = half(hidden * phi)
    slope = phi + hidden * jnp.exp(-0.5 * hidden * hidden) * (1.0 / math.sqrt(2.0 * math.pi))
    low_down = low(dot_t(active, a_down))
    outputs = half(middle + dot(active, down_all) + dot(low_down, b_down))

    through_down = low(dot_t(dy, b_down))
    d_active = dot_t(dy, down_all) + dot(through_down, a_down)
    d_hidden = half(d_active * slope)
    through_up = low(dot_t(d_hidden, b_up))
    d_normed_two = dot_t(d_hidden, up_all) + dot(through_up, a_up)
    d_middle = dy.astype(jnp.float32) + norm_back(unit_two, inverse_two, gain_two, d_normed_two)
    d_branch = half(d_middle)
    through_out = low(dot_t(d_branch, b_out))
    d_attended = half(dot_t(d_branch, out_all) + dot(through_out, a_out))
    d_heads = d_attended.reshape(shape_heads)
    d_values = jnp.einsum("fhqk,fqhd->fkhd", soft_half, d_heads, preferred_element_type=jnp.float32)
    d_soft = jnp.einsum("fqhd,fkhd->fhqk", d_heads, values, preferred_element_type=jnp.float32)
    inner = jnp.sum(soft * d_soft, axis=-1, keepdims=True)
    d_scores = half(soft * (d_soft - inner))
    d_queries = scale * jnp.einsum(
        "fhqk,fkhd->fqhd", d_scores, keys, preferred_element_type=jnp.float32
    )
    d_keys = scale * jnp.einsum(
        "fhqk,fqhd->fkhd", d_scores, queries, preferred_element_type=jnp.float32
    )
    d_projected = half(
        jnp.concatenate([d.reshape(rows, width) for d in (d_queries, d_keys, d_values)], axis=1)
    )
    through_qkv = low(dot_t(d_projected, b_qkv))
    d_normed_one = dot_t(d_projected, qkv_all) + dot(through_qkv, a_qkv)
    input_grad = half(d_middle + norm_back(unit_one, inverse_one, gain_one, d_normed_one))
    grads = half(jnp.concatenate(
        [
            t_dot(through_qkv, normed_one),
            t_dot(low_qkv, d_projected),
            t_dot(through_out, attended),
            t_dot(low_out, d_branch),
            t_dot(through_up, normed_two),
            t_dot(low_up, d_hidden),
            t_dot(through_down, active),
            t_dot(low_down, dy),
        ],
        axis=1,
    ))
    pick = (
        lax.broadcasted_iota(jnp.int32, (rank_all, mine * RANK), 0)
        == jnp.repeat(chosen, RANK)[None, :] * RANK
        + lax.broadcasted_iota(jnp.int32, (rank_all, mine * RANK), 1) % RANK
    ).astype(jnp.bfloat16)
    owner_grad = lax.psum_scatter(
        dot(pick, grads), ("dp", "mp"), scatter_dimension=1, tiled=True
    )
    return (swap_back(outputs), swap_back(input_grad)) + adam(
        owner_grad, adapters, moment_one, moment_two
    )


MESH = pl.DeviceIdType.MESH
X1, Y1, Y2, X2, C0, C1A, C1B, C2A, C2B = range(9)
HALF_PITCH = 104
HALF_SLOT = 112


def fused_kernel(
    tok_ref,
    cot_ref,
    g1_ref,
    g2_ref,
    shard_ref,
    adp_ref,
    act_ref,
    ing_ref,
    gr_ref,
    wa,
    wf,
    ad,
    ts,
    cs,
    tr,
    cr,
    xf,
    dyb,
    n1,
    n2,
    proj,
    soft,
    att,
    mid,
    acc,
    dn,
    tmp,
    buf,
    dbr,
    dpj,
    bq,
    ao,
    bu,
    an,
    gq,
    go,
    g16,
    gc,
    gs,
    rb,
    osend,
    isend,
    smalls,
    zs,
    zr,
    azs,
    azr,
    ss,
    rs,
    ps,
    pr,
    cxs,
    cxr,
    us,
    ur,
):
    dp = lax.axis_index("dp")
    z = lax.axis_index("mp")
    y = dp // 4
    x = lax.rem(dp // 2, 2)
    c = lax.rem(dp, 2)
    h = lax.rem(z, 2)
    zp = z + 1 - 2 * h
    zn = 4
    shard_rows = tok_ref.shape[1]
    rows = xf.shape[0]
    frame_rows = rows // 2
    width = xf.shape[1]
    local = width // zn
    scale = 1.0 / math.sqrt(HEAD)

    def place(yy, xx, cc, zz):
        return ((yy * 2 + xx) * 2 + cc, zz)

    barrier = pltpu.get_barrier_semaphore()
    for k in range(1, 16):
        yx = lax.rem(y * 2 + x + k // 4, 4)
        target = (yx * 2 + c, lax.rem(z + k % 4, 4))
        pl.semaphore_signal(barrier, inc=1, device_id=target, device_id_type=MESH)
    pl.semaphore_signal(barrier, inc=1, device_id=place(y, x, 1 - c, z), device_id_type=MESH)

    def remote(src, dst, send, recv, target):
        return pltpu.make_async_remote_copy(
            src_ref=src,
            dst_ref=dst,
            send_sem=send,
            recv_sem=recv,
            device_id=target,
            device_id_type=MESH,
        )

    wa[z, y, x, c] = shard_ref[0]
    wf[z, 0, y, x, c] = shard_ref[1]
    wf[z, 1, y, x, c] = shard_ref[2]
    for m in range(4):
        ts[m, pl.ds(96, 16)] = jnp.zeros((16, width), jnp.bfloat16)
        cs[m, pl.ds(96, 16)] = jnp.zeros((16, width), jnp.bfloat16)
        ts[m, pl.ds(0, shard_rows)] = tok_ref[m]
        cs[m, pl.ds(0, shard_rows)] = cot_ref[m]
    span = adp_ref.shape[2]
    low_columns = pl.ds(pl.multiple_of(lax.rem(z, 2) * span, 128), span)
    ad[y, x, c, z // 2, :, low_columns] = adp_ref[h]

    def part(s, zk, yy, xx, cc, first, count):
        if s == 0:
            return wa.at[zk, yy, xx, cc, pl.ds(first, count), :]
        if s == 1:
            return wf.at[zk, :, yy, xx, cc, pl.ds(first, count), :]
        return ad.at[yy, xx, cc, :, pl.ds(first, count), :]

    def move(s, k, what):
        full = 32 if s == 2 else 96
        n = full // 2
        zk = lax.rem(z + k, zn)
        every = pl.ds(0, 2)
        args, target = {
            X1: ((y, x, c, 0, n), (y, 1 - x, c)),
            Y1: ((y, x, c, n, n), (1 - y, x, c)),
            Y2: ((y, every, c, 0, n), (1 - y, x, c)),
            X2: ((every, x, c, n, n), (y, 1 - x, c)),
            C0: ((y, x, c, 0, full), (y, x, 1 - c)),
            C1A: ((y, 1 - x, c, 0, n), (y, x, 1 - c)),
            C1B: ((1 - y, x, c, n, n), (y, x, 1 - c)),
            C2A: ((1 - y, every, c, 0, n), (y, x, 1 - c)),
            C2B: ((every, 1 - x, c, n, n), (y, x, 1 - c)),
        }[what]
        ref = part(s, zk, *args)
        index = s * 4 + k
        return remote(ref, ref, ss.at[index, what], rs.at[index, what], place(*target, z))

    def z_move(s, j):
        ref = part(s, z, y, x, c, 0, 96)
        return remote(ref, ref, zs.at[s, j], zr.at[s, j], (dp, lax.rem(z + zn - j, zn)))

    def ad_move(j):
        other = lax.rem(z + zn - j, zn)
        dst = ad.at[y, x, c, z // 2, :, low_columns]
        return remote(adp_ref.at[lax.rem(other, 2)], dst, azs.at[j], azr.at[j], (dp, other))

    def t1(s, k):
        if s < 2:
            if isinstance(k, int):
                if k:
                    z_move(s, k).wait_recv()
            else:

                @pl.when(k > 0)
                def _():
                    z_move(s, k).wait_recv()

        for what in (X1, Y1, C0):
            move(s, k, what).start()

    def t2(s, k):
        move(s, k, X1).wait_recv()
        move(s, k, Y2).start()
        move(s, k, Y1).wait_recv()
        move(s, k, X2).start()
        move(s, k, C1A).start()
        move(s, k, C1B).start()

    def t3(s, k):
        move(s, k, Y2).wait_recv()
        move(s, k, C2A).start()
        move(s, k, X2).wait_recv()
        move(s, k, C2B).start()

    def ready(s, k):
        for what in (C0, C1A, C1B, C2A, C2B):
            move(s, k, what).wait_recv()

    tok_move = remote(
        ts.at[pl.ds(2 - 2 * h, 2)], tr, ps.at[0], pr.at[0], (dp, zp)
    )
    cot_move = remote(
        cs.at[pl.ds(2 - 2 * h, 2)], cr, ps.at[1], pr.at[1], (dp, zp)
    )
    act_move = remote(
        osend, act_ref.at[pl.ds(2 * h, 2)], ps.at[2], pr.at[2], (dp, zp)
    )
    ing_move = remote(
        isend, ing_ref.at[pl.ds(2 * h, 2)], ps.at[3], pr.at[3], (dp, zp)
    )

    pl.semaphore_wait(barrier, 16)
    for j in range(1, 4):
        ad_move(j).start()
    tok_move.start()
    t1(0, 0)
    for j in range(1, 4):
        z_move(0, j).start()
    cot_move.start()
    for j in range(1, 4):
        z_move(1, j).start()
    for j in range(1, 4):
        ad_move(j).wait_recv()
    t1(2, 0)
    t1(0, 1)
    t2(0, 0)
    t2(2, 0)

    def dot(left, right):
        return jnp.dot(left, right, preferred_element_type=jnp.float32)

    def dot_t(left, right):
        return lax.dot_general(
            left, right, (((1,), (1,)), ((), ())), preferred_element_type=jnp.float32
        )

    def t_dot(left, right):
        return lax.dot_general(
            left, right, (((0,), (0,)), ((), ())), preferred_element_type=jnp.float32
        )

    row_frame = lax.broadcasted_iota(jnp.int32, (rows, 32), 0) // frame_rows
    column_frame = lax.broadcasted_iota(jnp.int32, (rows, 32), 1) // RANK
    mask = row_frame == column_frame

    def low(values):
        return jnp.where(mask, values, 0.0).astype(jnp.bfloat16)

    def tiles(body, step=16):
        @pl.loop(0, rows // step)
        def _(t):
            body(pl.ds(pl.multiple_of(t * step, step), step))

    def norm_parts(values):
        center = values - jnp.mean(values, axis=-1, keepdims=True)
        spread = jnp.mean(center * center, axis=-1, keepdims=True)
        inverse = lax.rsqrt(spread + norm_epsilon)
        return center * inverse, inverse

    def norm_back(values, gain, grad):
        unit, inverse = norm_parts(values)
        scaled = grad * gain
        first = jnp.mean(scaled, axis=-1, keepdims=True)
        second = jnp.mean(scaled * unit, axis=-1, keepdims=True)
        return inverse * (scaled - first - unit * second)

    def group(g):
        return ad[g // 8, (g // 4) % 2, (g // 2) % 2, g % 2]

    def group_ref(g):
        return g16.at[g // 8, (g // 4) % 2, (g // 2) % 2, g % 2]

    def attn_block(zk):
        return wa[zk].reshape(width, width)

    def halves(f):
        own = pl.ds(pl.multiple_of(f * frame_rows + h * HALF_PITCH, 8), HALF_PITCH)
        other = pl.ds(pl.multiple_of(f * frame_rows + (1 - h) * HALF_PITCH, 8), HALF_PITCH)
        return own, other

    def join(dst, own_slots, other_slots):
        for f in range(2):
            own, other = halves(f)
            dst[own] = own_slots[2 * h + f][:HALF_PITCH].astype(jnp.float32)
            dst[other] = other_slots[f][:HALF_PITCH].astype(jnp.float32)

    tok_move.wait_recv()
    join(xf, ts, tr)

    def first_norm(at):
        values = xf[at]
        unit, _ = norm_parts(values)
        n1[at] = (unit * g1_ref[...]).astype(jnp.bfloat16)
        mid[at] = values

    tiles(first_norm)
    t3(2, 0)
    ready(2, 0)
    for k in range(4):
        bq[k] = jnp.concatenate(
            [jnp.zeros((32, local), jnp.bfloat16)]
            + [group(1 + i)[:, k * local : (k + 1) * local] for i in range(3)],
            axis=1,
        )
        ao[k] = group(4)[:, k * local : (k + 1) * local]
        bu[k] = group(7 + k)
        an[k] = group(11 + k)
    smalls[0] = low(dot_t(n1[...], group(0)))
    key_pad = (
        lax.rem(lax.broadcasted_iota(jnp.int32, (frame_rows, 1), 0), HALF_PITCH) >= shard_rows
    )
    bias = jnp.where(key_pad, -1e30, 0.0).astype(jnp.float32)

    LOW_QKV, LOW_OUT, LOW_UP, LOW_DOWN, THR_DOWN, THR_UP, THR_OUT, THR_QKV = range(8)

    def attention(i, out_low):
        zk = lax.rem(z + i, zn)
        block = attn_block(zk)
        proj[zk] = (dot(n1[...], block) + dot(smalls[LOW_QKV], bq[zk])).astype(jnp.bfloat16)
        for f in range(2):
            at = pl.ds(f * frame_rows, frame_rows)
            for head in range(3):
                first = local + head * HEAD
                q = proj[zk, at, first : first + HEAD]
                k = proj[zk, at, first + local : first + local + HEAD]
                v = proj[zk, at, first + 2 * local : first + 2 * local + HEAD]
                scores = dot_t(k, q) * scale + bias
                exponent = jnp.exp(scores - jnp.max(scores, axis=0, keepdims=True))
                weights = exponent / jnp.sum(exponent, axis=0, keepdims=True)
                weights = weights.astype(jnp.bfloat16)
                soft[zk, f * 3 + head] = weights
                att[zk, at, head * HEAD : (head + 1) * HEAD] = (
                    t_dot(weights, v).astype(jnp.bfloat16)
                )
        gathered = att[zk]
        mid[...] += dot_t(gathered, block[:, :local])
        return out_low + dot_t(gathered, ao[zk])

    def attention_step(i, out_low):
        @pl.when(i < 2)
        def _():
            t1(0, i + 2)

        @pl.when(i >= 2)
        def _():
            t1(1, i - 2)

        @pl.when(i < 3)
        def _():
            t2(0, i + 1)

        @pl.when(i == 3)
        def _():
            t2(1, 0)

        t3(0, i)
        ready(0, i)
        return attention(i, out_low)

    out_low = lax.fori_loop(0, 4, attention_step, jnp.zeros((rows, 32), jnp.float32))
    smalls[LOW_OUT] = low(out_low)
    mid[...] += dot(smalls[LOW_OUT], group(5))

    def second_norm(at):
        unit, _ = norm_parts(mid[at])
        n2[at] = (unit * g2_ref[...]).astype(jnp.bfloat16)

    tiles(second_norm)
    cot_move.wait_recv()
    join(tmp, cs, cr)
    dyb[...] = tmp[...].astype(jnp.bfloat16)
    smalls[LOW_UP] = low(dot_t(n2[...], group(6)))
    smalls[THR_DOWN] = low(dot_t(dyb[...], group(15)))
    group_ref(15)[...] = jnp.zeros((32, width), jnp.bfloat16)
    acc[...] = mid[...]
    dn[...] = jnp.zeros_like(dn)

    def feed(i, lows):
        down_low, up_back = lows
        zk = lax.rem(z + i, zn)
        up = wf[zk, 0].reshape(width, width)
        down = wf[zk, 1].reshape(width, width)
        tmp[...] = dot(n2[...], up) + dot(smalls[LOW_UP], bu[zk])

        def gate(at):
            hidden = tmp[at]
            phi = 0.5 + 0.5 * lax.erf(hidden * math.sqrt(0.5))
            bell = jnp.exp(-0.5 * hidden * hidden) * (1.0 / math.sqrt(2.0 * math.pi))
            buf[0, at] = (hidden * phi).astype(jnp.bfloat16)
            tmp[at] = phi + hidden * bell

        tiles(gate)
        active = buf[0]
        acc[...] += dot_t(active, down)
        tmp[...] = tmp[...] * (dot(dyb[...], down) + dot(smalls[THR_DOWN], an[zk]))
        buf[1] = tmp[...].astype(jnp.bfloat16)
        d_hidden = buf[1]
        dn[...] += dot_t(d_hidden, up)
        gu = 7 + zk
        ga = 11 + zk
        g16[gu // 8, lax.rem(gu // 4, 2), lax.rem(gu // 2, 2), lax.rem(gu, 2)] = t_dot(
            smalls[LOW_UP], d_hidden
        ).astype(jnp.bfloat16)
        g16[ga // 8, lax.rem(ga // 4, 2), lax.rem(ga // 2, 2), lax.rem(ga, 2)] = t_dot(
            smalls[THR_DOWN], active
        ).astype(jnp.bfloat16)
        return down_low + dot_t(active, an[zk]), up_back + dot_t(d_hidden, bu[zk])

    def feed_step(i, lows):
        @pl.when(i < 2)
        def _():
            t1(1, i + 2)

        @pl.when(i < 3)
        def _():
            t2(1, i + 1)

        t3(1, i)
        ready(1, i)
        return feed(i, lows)

    empty = jnp.zeros((rows, 32), jnp.float32)
    down_low, up_back = lax.fori_loop(0, 4, feed_step, (empty, empty))
    smalls[LOW_DOWN] = low(down_low)
    smalls[THR_UP] = low(up_back)
    group_ref(15)[...] = t_dot(smalls[LOW_DOWN], dyb[...]).astype(jnp.bfloat16)

    def core_move(yx):
        src = g16.at[yx // 2, yx % 2, 1 - c]
        return remote(src, gc.at[yx], cxs.at[yx], cxr.at[yx], place(y, x, 1 - c, z))

    def owner_move(yx, zz):
        back_yx = lax.rem(y * 2 + x + 4 - yx, 4)
        back_z = lax.rem(z + 4 - zz, 4)
        slot = back_yx * 4 + back_z
        src = gs.at[yx, zz // 2, :, pl.ds((zz % 2) * span, span)]
        copy = remote(src, rb.at[slot], us.at[yx, zz], ur.at[slot], (yx * 2 + c, zz))
        return copy, slot

    def spread_out(yx):
        core_move(yx).wait_recv()
        for g in range(2):
            gs[yx, g] = (
                g16[yx // 2, yx % 2, c, g].astype(jnp.float32) + gc[yx, g].astype(jnp.float32)
            ).astype(jnp.bfloat16)
        for zz in range(4):
            copy, slot = owner_move(yx, zz)

            @pl.when(slot != 0)
            def _():
                copy.start()

            @pl.when(slot == 0)
            def _():
                rb[0] = gs[yx, zz // 2, :, pl.ds((zz % 2) * span, span)]

    core_move(3).start()
    core_move(2).start()

    dn[...] += dot(smalls[THR_UP], group(6))
    group_ref(6)[...] = t_dot(smalls[THR_UP], n2[...]).astype(jnp.bfloat16)
    acc[...] += dot(smalls[LOW_DOWN], group(15))

    def second_back(at):
        value = dyb[at].astype(jnp.float32) + norm_back(mid[at], g2_ref[...], dn[at])
        dn[at] = value
        dbr[at] = value.astype(jnp.bfloat16)

    tiles(second_back)
    for f in range(2):
        own, other = halves(f)
        osend[f, pl.ds(0, HALF_PITCH)] = acc[other].astype(jnp.bfloat16)
        act_ref[2 * h + f, pl.ds(0, HALF_PITCH)] = acc[own].astype(jnp.bfloat16)
    act_move.start()
    smalls[THR_OUT] = low(dot_t(dbr[...], group(5)))
    group_ref(5)[...] = t_dot(smalls[LOW_OUT], dbr[...]).astype(jnp.bfloat16)
    dpj[:, 0:local] = jnp.zeros((rows, local), jnp.bfloat16)
    acc[...] = jnp.zeros_like(acc)

    spread_out(3)
    spread_out(2)

    def attention_back(zk, qkv_back):
        block = attn_block(zk)
        d_att = (dot(dbr[...], block[:, :local]) + dot(smalls[THR_OUT], ao[zk])).astype(
            jnp.bfloat16
        )
        buf[0, :, 0:local] = d_att
        go[zk] = t_dot(smalls[THR_OUT], att[zk]).astype(jnp.bfloat16)
        for f in range(2):
            at = pl.ds(f * frame_rows, frame_rows)
            for head in range(3):
                first = local + head * HEAD
                q = proj[zk, at, first : first + HEAD]
                k = proj[zk, at, first + local : first + local + HEAD]
                v = proj[zk, at, first + 2 * local : first + 2 * local + HEAD]
                d_out = buf[0, at, head * HEAD : (head + 1) * HEAD]
                weights = soft[zk, f * 3 + head]
                d_values = dot(weights, d_out)
                d_soft = dot_t(v, d_out)
                wide = weights.astype(jnp.float32)
                inner = jnp.sum(wide * d_soft, axis=0, keepdims=True)
                d_scores = (wide * (d_soft - inner)).astype(jnp.bfloat16)
                d_keys = dot(d_scores, q) * scale
                d_queries = t_dot(d_scores, k) * scale
                dpj[at, first : first + HEAD] = d_queries.astype(jnp.bfloat16)
                dpj[at, first + local : first + local + HEAD] = d_keys.astype(jnp.bfloat16)
                dpj[at, first + 2 * local : first + 2 * local + HEAD] = d_values.astype(
                    jnp.bfloat16
                )
        d_projected = dpj[...]
        gq[zk] = t_dot(smalls[LOW_QKV], d_projected).astype(jnp.bfloat16)
        acc[...] += dot_t(d_projected, block)
        return qkv_back + dot_t(d_projected, bq[zk])

    qkv_back = lax.fori_loop(0, 4, attention_back, empty)
    smalls[THR_QKV] = low(qkv_back)
    group_ref(0)[...] = t_dot(smalls[THR_QKV], n1[...]).astype(jnp.bfloat16)
    for i in range(3):
        first = (1 + i) * local
        group_ref(1 + i)[...] = jnp.concatenate(
            [gq[k][:, first : first + local] for k in range(4)], axis=1
        )
    group_ref(4)[...] = jnp.concatenate([go[k] for k in range(4)], axis=1)
    core_move(1).start()
    core_move(0).start()

    acc[...] += dot(smalls[THR_QKV], group(0))

    def first_back(at):
        acc[at] = dn[at] + norm_back(xf[at], g1_ref[...], acc[at])

    tiles(first_back)
    for f in range(2):
        own, other = halves(f)
        isend[f, pl.ds(0, HALF_PITCH)] = acc[other].astype(jnp.bfloat16)
        ing_ref[2 * h + f, pl.ds(0, HALF_PITCH)] = acc[own].astype(jnp.bfloat16)
    ing_move.start()
    spread_out(1)
    spread_out(0)

    for slot in range(1, 16):
        remote(rb.at[slot], rb.at[slot], us.at[0, 0], ur.at[slot], (dp, zp)).wait_recv()
    for parity in range(2):
        total = jnp.zeros((32, span), jnp.float32)
        for slot in range(16):
            if slot % 2 == parity:
                total = total + rb[slot].astype(jnp.float32)
        gr_ref[lax.rem(h + parity, 2)] = total
    for yx in range(4):
        core_move(yx).wait_send()
        for zz in range(4):
            copy, slot = owner_move(yx, zz)

            @pl.when(slot != 0)
            def _():
                copy.wait_send()

    tok_move.wait_send()
    cot_move.wait_send()
    for j in range(1, 4):
        ad_move(j).wait_send()
        z_move(0, j).wait_send()
        z_move(1, j).wait_send()

    @pl.loop(0, 4)
    def _(k):
        for what in range(9):
            move(0, k, what).wait_send()
            move(1, k, what).wait_send()

    for what in range(9):
        move(2, 0, what).wait_send()
    act_move.wait()
    ing_move.wait()


def fused(
    tokens,
    cotangent,
    clip_adapter,
    gain_one,
    gain_two,
    w_qkv,
    w_out,
    w_up,
    w_down,
    adapters,
    moment_one,
    moment_two,
):
    micro_count, shard_rows, width = tokens.shape
    rank_all, span = adapters.shape
    shard = jnp.stack(
        [
            jnp.concatenate([w_out.T, w_qkv.reshape(w_qkv.shape[0], -1)], axis=1),
            w_up,
            w_down.T,
        ]
    )
    picked = adapters.astype(jnp.bfloat16).reshape(rank_all // RANK, RANK, span)[clip_adapter]
    adp = picked.reshape(2, 2 * RANK, span)
    rows = 4 * HALF_PITCH
    frame_rows = 2 * HALF_PITCH
    local = width // 4
    bf, f32 = jnp.bfloat16, jnp.float32
    vmem = pl.BlockSpec(memory_space=pltpu.VMEM)
    scratch = [
        pltpu.VMEM((4, 2, 2, 2, 96, width), bf),
        pltpu.VMEM((4, 2, 2, 2, 2, 96, width), bf),
        pltpu.VMEM((2, 2, 2, 2, 32, width), bf),
        pltpu.VMEM((4, HALF_SLOT, width), bf),
        pltpu.VMEM((4, HALF_SLOT, width), bf),
        pltpu.VMEM((2, HALF_SLOT, width), bf),
        pltpu.VMEM((2, HALF_SLOT, width), bf),
        pltpu.VMEM((rows, width), f32),
        pltpu.VMEM((rows, width), bf),
        pltpu.VMEM((rows, width), bf),
        pltpu.VMEM((rows, width), bf),
        pltpu.VMEM((4, rows, width), bf),
        pltpu.VMEM((4, 6, frame_rows, frame_rows), bf),
        pltpu.VMEM((4, rows, local), bf),
        pltpu.VMEM((rows, width), f32),
        pltpu.VMEM((rows, width), f32),
        pltpu.VMEM((rows, width), f32),
        pltpu.VMEM((rows, width), f32),
        pltpu.VMEM((2, rows, width), bf),
        pltpu.VMEM((rows, width), bf),
        pltpu.VMEM((rows, width), bf),
        pltpu.VMEM((4, 32, width), bf),
        pltpu.VMEM((4, 32, local), bf),
        pltpu.VMEM((4, 32, width), bf),
        pltpu.VMEM((4, 32, width), bf),
        pltpu.VMEM((4, 32, width), bf),
        pltpu.VMEM((4, 32, local), bf),
        pltpu.VMEM((2, 2, 2, 2, 32, width), bf),
        pltpu.VMEM((4, 2, 32, width), bf),
        pltpu.VMEM((4, 2, 32, width), bf),
        pltpu.VMEM((16, 32, span), bf),
        pltpu.VMEM((2, HALF_SLOT, width), bf),
        pltpu.VMEM((2, HALF_SLOT, width), bf),
        pltpu.VMEM((8, rows, 32), bf),
        pltpu.SemaphoreType.DMA((2, 4)),
        pltpu.SemaphoreType.DMA((2, 4)),
        pltpu.SemaphoreType.DMA((4,)),
        pltpu.SemaphoreType.DMA((4,)),
        pltpu.SemaphoreType.DMA((9, 9)),
        pltpu.SemaphoreType.DMA((9, 9)),
        pltpu.SemaphoreType.DMA((4,)),
        pltpu.SemaphoreType.DMA((4,)),
        pltpu.SemaphoreType.DMA((4,)),
        pltpu.SemaphoreType.DMA((4,)),
        pltpu.SemaphoreType.DMA((4, 4)),
        pltpu.SemaphoreType.DMA((16,)),
    ]
    act, ing, grads = pl.pallas_call(
        fused_kernel,
        out_shape=(
            jax.ShapeDtypeStruct((micro_count, HALF_SLOT, width), bf),
            jax.ShapeDtypeStruct((micro_count, HALF_SLOT, width), bf),
            jax.ShapeDtypeStruct((2, 2 * RANK, span), f32),
        ),
        in_specs=[vmem] * 6,
        out_specs=(vmem, vmem, vmem),
        scratch_shapes=scratch,
        compiler_params=pltpu.CompilerParams(
            collective_id=0, has_side_effects=True, vmem_limit_bytes=60 * 2**20
        ),
    )(tokens, cotangent, gain_one[None], gain_two[None], shard, adp)
    grads = grads.reshape(micro_count, RANK, span)
    hit = clip_adapter[None, :] == lax.broadcasted_iota(
        jnp.int32, (rank_all // RANK, micro_count), 0
    )
    owner_grad = sum(
        jnp.where(hit[:, m, None, None], grads[m][None], 0.0) for m in range(micro_count)
    ).reshape(rank_all, span)
    return (act[:, :shard_rows], ing[:, :shard_rows]) + adam(
        owner_grad, adapters, moment_one, moment_two
    )


def layer(tokens, *others):
    w_up = others[6]
    sizes = lax.axis_size("dp"), lax.axis_size("mp")
    frames_micro = tokens.shape[1] * sizes[0] * sizes[1] // FRAME
    fits = (
        sizes == (8, 4)
        and tokens.shape[0] == 4
        and 2 * tokens.shape[1] == FRAME
        and frames_micro == CLIP_FRAMES
        and w_up.shape == (tokens.shape[2] // 8, tokens.shape[2])
    )
    return (fused if fits else shards)(tokens, *others)


def solution(mesh):
    spread = P(None, ("dp", "mp"))
    rows = P(None, ("dp", "mp"), None)
    return jax.shard_map(
        layer,
        mesh=mesh,
        in_specs=(
            rows,
            rows,
            P(),
            P(),
            P(),
            P("dp", None, "mp"),
            P("mp", "dp"),
            P("dp", "mp"),
            P("mp", "dp"),
            spread,
            spread,
            spread,
        ),
        out_specs=(rows, rows, spread, spread, spread, spread, spread),
        check_vma=False,
    )
```

```python
import math

import jax
import jax.numpy as jnp
from jax import lax
from jax.experimental import pallas as pl
from jax.experimental.pallas import tpu as pltpu
from jax.sharding import PartitionSpec as P

HEAD = 64
FRAME = 196
RANK = 16
CLIP_FRAMES = 16
STEP = 5

norm_epsilon = 1e-06
beta_first = 0.5
beta_second = 0.5
learn_rate = 0.05
weight_decay = 0.01
adam_epsilon = 1e-08


def dot(left, right):
    return jnp.dot(left, right, preferred_element_type=jnp.float32)


def dot_t(left, right):
    return lax.dot_general(left, right, (((1,), (1,)), ((), ())), preferred_element_type=jnp.float32)


def t_dot(left, right):
    return lax.dot_general(left, right, (((0,), (0,)), ((), ())), preferred_element_type=jnp.float32)


def half(values):
    return values.astype(jnp.bfloat16)


def norm_parts(values):
    center = values - jnp.mean(values, axis=-1, keepdims=True)
    spread = jnp.mean(center * center, axis=-1, keepdims=True)
    inverse = lax.rsqrt(spread + norm_epsilon)
    return center * inverse, inverse


def norm_back(unit, inverse, gain, grad):
    scaled = grad * gain
    first = jnp.mean(scaled, axis=-1, keepdims=True)
    second = jnp.mean(scaled * unit, axis=-1, keepdims=True)
    return inverse * (scaled - first - unit * second)


def adam(owner_grad, adapters, moment_one, moment_two):
    first_moment = beta_first * moment_one + (1.0 - beta_first) * owner_grad
    second_moment = beta_second * moment_two + (1.0 - beta_second) * owner_grad * owner_grad
    first_hat = first_moment / (1.0 - beta_first**STEP)
    second_hat = second_moment / (1.0 - beta_second**STEP)
    updated = adapters - learn_rate * (
        first_hat / (jnp.sqrt(second_hat) + adam_epsilon) + weight_decay * adapters
    )
    return (
        owner_grad,
        updated,
        first_moment,
        second_moment,
        updated.astype(jnp.bfloat16),
    )


def shards(
    tokens,
    cotangent,
    clip_adapter,
    gain_one,
    gain_two,
    w_qkv,
    w_out,
    w_up,
    w_down,
    adapters,
    moment_one,
    moment_two,
):
    groups = lax.axis_size("mp")
    member = lax.axis_index("mp")
    group_index = lax.axis_index("dp")
    micro_count, shard_rows, width = tokens.shape
    hidden_width = w_up.shape[1] * groups
    heads = width // HEAD
    rank_all = adapters.shape[0]
    full_width = adapters.shape[1] * lax.axis_size(("dp", "mp"))
    frames = shard_rows * groups // FRAME
    frames_micro = frames * lax.axis_size("dp")
    scale = 1.0 / math.sqrt(HEAD)
    span = FRAME // shard_rows
    mine = micro_count // span
    part = member % span
    pairs = [[first * span + k for k in range(span)] for first in range(groups // span)]

    def swap(rows):
        return lax.all_to_all(
            rows, "mp", split_axis=0, concat_axis=1, axis_index_groups=pairs, tiled=True
        ).reshape(mine * FRAME, width)

    def swap_back(rows):
        return lax.all_to_all(
            rows.reshape(mine, FRAME, width),
            "mp",
            split_axis=1,
            concat_axis=0,
            axis_index_groups=pairs,
            tiled=True,
        )

    inputs = swap(tokens).astype(jnp.float32)
    dy = swap(cotangent)

    def whole(weight, first, second):
        return lax.all_gather(
            lax.all_gather(weight, first[0], axis=first[1], tiled=True),
            second[0],
            axis=second[1],
            tiled=True,
        )

    qkv_all = whole(w_qkv, ("dp", 0), ("mp", 2)).reshape(width, 3 * width)
    out_all = whole(w_out, ("dp", 1), ("mp", 0))
    up_all = whole(w_up, ("dp", 0), ("mp", 1))
    down_all = whole(w_down, ("dp", 1), ("mp", 0))
    table = lax.all_gather(half(adapters), ("dp", "mp"), axis=1, tiled=True)
    table = table.reshape(rank_all // RANK, RANK, full_width)
    clips = jnp.stack(
        [
            ((part * mine + i) * frames_micro + group_index * frames + member // span)
            // CLIP_FRAMES
            for i in range(mine)
        ]
    )
    chosen = clip_adapter[clips]
    own = table[chosen].reshape(mine * RANK, full_width)
    ends = [0, width, 4 * width, 5 * width, 6 * width, 7 * width]
    ends += [7 * width + hidden_width, 7 * width + 2 * hidden_width, full_width]
    a_qkv, b_qkv, a_out, b_out, a_up, b_up, a_down, b_down = [
        own[:, ends[i] : ends[i + 1]] for i in range(8)
    ]
    rows = mine * FRAME
    row_frame = lax.broadcasted_iota(jnp.int32, (rows, mine * RANK), 0) // FRAME
    column_frame = lax.broadcasted_iota(jnp.int32, (rows, mine * RANK), 1) // RANK
    mask = row_frame == column_frame

    def low(values):
        return half(jnp.where(mask, values, 0.0))

    shape_heads = (mine, FRAME, heads, HEAD)
    unit_one, inverse_one = norm_parts(inputs)
    normed_one = half(unit_one * gain_one)
    low_qkv = low(dot_t(normed_one, a_qkv))
    projected = half(dot(normed_one, qkv_all) + dot(low_qkv, b_qkv))
    queries = projected[:, 0:width].reshape(shape_heads)
    keys = projected[:, width : 2 * width].reshape(shape_heads)
    values = projected[:, 2 * width :].reshape(shape_heads)
    scores = jnp.einsum("fqhd,fkhd->fhqk", queries, keys, preferred_element_type=jnp.float32)
    scores = scores * scale
    exponent = jnp.exp(scores - jnp.max(scores, axis=-1, keepdims=True))
    soft = exponent / jnp.sum(exponent, axis=-1, keepdims=True)
    soft_half = half(soft)
    attended = half(
        jnp.einsum("fhqk,fkhd->fqhd", soft_half, values, preferred_element_type=jnp.float32)
    ).reshape(rows, width)
    low_out = low(dot_t(attended, a_out))
    middle = inputs + dot(attended, out_all) + dot(low_out, b_out)
    unit_two, inverse_two = norm_parts(middle)
    normed_two = half(unit_two * gain_two)
    low_up = low(dot_t(normed_two, a_up))
    hidden = dot(normed_two, up_all) + dot(low_up, b_up)
    phi = 0.5 * (1.0 + lax.erf(hidden * math.sqrt(0.5)))
    active = half(hidden * phi)
    slope = phi + hidden * jnp.exp(-0.5 * hidden * hidden) * (1.0 / math.sqrt(2.0 * math.pi))
    low_down = low(dot_t(active, a_down))
    outputs = half(middle + dot(active, down_all) + dot(low_down, b_down))

    through_down = low(dot_t(dy, b_down))
    d_active = dot_t(dy, down_all) + dot(through_down, a_down)
    d_hidden = half(d_active * slope)
    through_up = low(dot_t(d_hidden, b_up))
    d_normed_two = dot_t(d_hidden, up_all) + dot(through_up, a_up)
    d_middle = dy.astype(jnp.float32) + norm_back(unit_two, inverse_two, gain_two, d_normed_two)
    d_branch = half(d_middle)
    through_out = low(dot_t(d_branch, b_out))
    d_attended = half(dot_t(d_branch, out_all) + dot(through_out, a_out))
    d_heads = d_attended.reshape(shape_heads)
    d_values = jnp.einsum("fhqk,fqhd->fkhd", soft_half, d_heads, preferred_element_type=jnp.float32)
    d_soft = jnp.einsum("fqhd,fkhd->fhqk", d_heads, values, preferred_element_type=jnp.float32)
    inner = jnp.sum(soft * d_soft, axis=-1, keepdims=True)
    d_scores = half(soft * (d_soft - inner))
    d_queries = scale * jnp.einsum(
        "fhqk,fkhd->fqhd", d_scores, keys, preferred_element_type=jnp.float32
    )
    d_keys = scale * jnp.einsum(
        "fhqk,fqhd->fkhd", d_scores, queries, preferred_element_type=jnp.float32
    )
    d_projected = half(
        jnp.concatenate([d.reshape(rows, width) for d in (d_queries, d_keys, d_values)], axis=1)
    )
    through_qkv = low(dot_t(d_projected, b_qkv))
    d_normed_one = dot_t(d_projected, qkv_all) + dot(through_qkv, a_qkv)
    input_grad = half(d_middle + norm_back(unit_one, inverse_one, gain_one, d_normed_one))
    grads = half(jnp.concatenate(
        [
            t_dot(through_qkv, normed_one),
            t_dot(low_qkv, d_projected),
            t_dot(through_out, attended),
            t_dot(low_out, d_branch),
            t_dot(through_up, normed_two),
            t_dot(low_up, d_hidden),
            t_dot(through_down, active),
            t_dot(low_down, dy),
        ],
        axis=1,
    ))
    pick = (
        lax.broadcasted_iota(jnp.int32, (rank_all, mine * RANK), 0)
        == jnp.repeat(chosen, RANK)[None, :] * RANK
        + lax.broadcasted_iota(jnp.int32, (rank_all, mine * RANK), 1) % RANK
    ).astype(jnp.bfloat16)
    owner_grad = lax.psum_scatter(
        dot(pick, grads), ("dp", "mp"), scatter_dimension=1, tiled=True
    )
    return (swap_back(outputs), swap_back(input_grad)) + adam(
        owner_grad, adapters, moment_one, moment_two
    )


MESH = pl.DeviceIdType.MESH
X1, Y1, Y2, X2, C0, C1A, C1B, C2A, C2B = range(9)
HALF_PITCH = 104
HALF_SLOT = 112


def fused_kernel(
    tok_ref,
    cot_ref,
    g1_ref,
    g2_ref,
    wq_ref,
    wo_ref,
    wu_ref,
    wd_ref,
    table_ref,
    clip_ref,
    act_ref,
    ing_ref,
    gr_ref,
    w,
    ad,
    ts,
    cs,
    tr,
    cr,
    xf,
    dyb,
    n1,
    n2,
    proj,
    soft,
    att,
    mid,
    acc,
    dn,
    tmp,
    buf,
    dbr,
    dpj,
    bq,
    ao,
    bu,
    an,
    g16,
    gc,
    gs,
    rb,
    osend,
    isend,
    own_act,
    own_ing,
    orecv,
    irecv,
    adp,
    smalls,
    zs,
    zr,
    azs,
    azr,
    ss,
    rs,
    ps,
    pr,
    cxs,
    cxr,
    us,
    ur,
):
    dp = lax.axis_index("dp")
    z = lax.axis_index("mp")
    y = dp // 4
    x = lax.rem(dp // 2, 2)
    c = lax.rem(dp, 2)
    h = lax.rem(z, 2)
    zp = z + 1 - 2 * h
    zn = 4
    shard_rows = tok_ref.shape[0]
    rows = xf.shape[0]
    frame_rows = rows // 2
    width = xf.shape[1]
    local = width // zn
    scale = 1.0 / math.sqrt(HEAD)

    def place(yy, xx, cc, zz):
        return ((yy * 2 + xx) * 2 + cc, zz)

    def order(at_z, k):
        upper = at_z // 2
        near = at_z + upper * (3 - 2 * at_z)
        swapped = jnp.where((near == 1) & (k < 2), 1 - k, k)
        return swapped + upper * (3 - 2 * swapped)

    def rank_of(at_z, block_z):
        upper = at_z // 2
        near = at_z + upper * (3 - 2 * at_z)
        mirrored = block_z + upper * (3 - 2 * block_z)
        return jnp.where((near == 1) & (mirrored < 2), 1 - mirrored, mirrored)

    barrier = pltpu.get_barrier_semaphore()
    for k in range(1, 16):
        yx = lax.rem(y * 2 + x + k // 4, 4)
        target = (yx * 2 + c, lax.rem(z + k % 4, 4))
        pl.semaphore_signal(barrier, inc=1, device_id=target, device_id_type=MESH)
    pl.semaphore_signal(barrier, inc=1, device_id=place(y, x, 1 - c, z), device_id_type=MESH)

    def remote(src, dst, send, recv, target):
        return pltpu.make_async_remote_copy(
            src_ref=src,
            dst_ref=dst,
            send_sem=send,
            recv_sem=recv,
            device_id=target,
            device_id_type=MESH,
        )

    w[z, 0, y, x, c] = jnp.concatenate([wo_ref[...].T] + [wq_ref[i] for i in range(3)], axis=1)
    span = table_ref.shape[1]
    low_columns = pl.ds(pl.multiple_of(lax.rem(z, 2) * span, 128), span)
    for m in range(4):
        clip = jnp.full((RANK, span), clip_ref[m])
        chosen = jnp.zeros((RANK, span), jnp.float32)
        for a in range(table_ref.shape[0] // RANK):
            chosen = jnp.where(clip == a, table_ref[a * RANK : (a + 1) * RANK], chosen)
        adp[m // 2, pl.ds((m % 2) * RANK, RANK)] = chosen.astype(jnp.bfloat16)
    ad[y, x, c, z // 2, :, low_columns] = adp[h]

    def stage(dst, src):
        for m in range(4):
            dst[m, pl.ds(96, 16)] = jnp.zeros((16, width), jnp.bfloat16)
            dst[m, pl.ds(0, shard_rows)] = src[:, m, :]

    def part(kind, zk, yy, xx, cc, first, count):
        return w.at[zk, kind, yy, xx, cc, pl.ds(first, count), :]

    def phase(q):
        if isinstance(q, int):
            return (0, q) if q < 4 else (1 + q % 2, (q - 4) // 2)
        return 1 + lax.rem(q, 2), (q - 4) // 2

    def move(q, what):
        full = 32 if q is None else 96
        n = full // 2
        every = pl.ds(0, 2)
        args, target = {
            X1: ((y, x, c, 0, n), (y, 1 - x, c)),
            Y1: ((y, x, c, n, n), (1 - y, x, c)),
            Y2: ((y, every, c, 0, n), (1 - y, x, c)),
            X2: ((every, x, c, n, n), (y, 1 - x, c)),
            C0: ((y, x, c, 0, full), (y, x, 1 - c)),
            C1A: ((y, 1 - x, c, 0, n), (y, x, 1 - c)),
            C1B: ((1 - y, x, c, n, n), (y, x, 1 - c)),
            C2A: ((1 - y, every, c, 0, n), (y, x, 1 - c)),
            C2B: ((every, 1 - x, c, n, n), (y, x, 1 - c)),
        }[what]
        if q is None:
            yy, xx, cc, first, count = args
            ref = ad.at[yy, xx, cc, :, pl.ds(first, count), :]
            index = 12
        else:
            kind, k = phase(q)
            ref = part(kind, order(z, k), *args)
            index = q
        return remote(ref, ref, ss.at[index, what], rs.at[index, what], place(*target, z))

    def z_move(q):
        kind, k = phase(q)
        ref = part(kind, z, y, x, c, 0, 96)
        other = order(z, k)
        return remote(ref, ref, zs.at[kind, k], zr.at[kind, rank_of(other, z)], (dp, other))

    def z_wait(q):
        kind, k = phase(q)
        ref = part(kind, z, y, x, c, 0, 96)
        remote(ref, ref, zs.at[kind, k], zr.at[kind, k], (dp, zp)).wait_recv()

    def ad_move(j):
        other = lax.rem(z + zn - j, zn)
        dst = ad.at[y, x, c, z // 2, :, low_columns]
        return remote(adp.at[lax.rem(other, 2)], dst, azs.at[j], azr.at[j], (dp, other))

    def t1(q):
        if isinstance(q, int):
            if q is not None and phase(q)[1]:
                z_wait(q)
        elif q is not None:
            z_wait(q)
        for what in (X1, Y1, C0):
            move(q, what).start()

    def t2(q):
        move(q, X1).wait_recv()
        move(q, Y2).start()
        move(q, Y1).wait_recv()
        move(q, X2).start()
        move(q, C1A).start()
        move(q, C1B).start()

    def t3(q):
        move(q, Y2).wait_recv()
        move(q, C2A).start()
        move(q, X2).wait_recv()
        move(q, C2B).start()

    def ready(q):
        for what in (C0, C1A, C1B, C2A, C2B):
            move(q, what).wait_recv()

    tok_move = remote(
        ts.at[pl.ds(2 - 2 * h, 2)], tr, ps.at[0], pr.at[0], (dp, zp)
    )
    cot_move = remote(
        cs.at[pl.ds(2 - 2 * h, 2)], cr, ps.at[1], pr.at[1], (dp, zp)
    )
    act_move = remote(
        osend, orecv, ps.at[2], pr.at[2], (dp, zp)
    )
    ing_move = remote(
        isend, irecv, ps.at[3], pr.at[3], (dp, zp)
    )

    pl.semaphore_wait(barrier, 16)
    t1(0)
    for j in range(1, 4):
        ad_move(j).start()
    for j in range(1, 4):
        z_move(j).start()
    w[z, 1, y, x, c] = wu_ref[...]
    t1(4)
    stage(ts, tok_ref)
    tok_move.start()
    w[z, 2, y, x, c] = wd_ref[...]
    t2(0)
    t1(1)
    for j in range(1, 4):
        ad_move(j).wait_recv()
    t1(None)
    t2(1)
    t1(2)
    t2(None)
    t3(0)
    z_move(6).start()
    z_move(7).start()
    t2(2)
    t1(3)
    t3(1)
    t3(None)
    stage(cs, cot_ref)
    cot_move.start()
    t2(3)
    t2(4)
    t3(2)
    z_move(8).start()
    z_move(9).start()
    t1(5)
    t3(3)
    z_move(10).start()
    z_move(11).start()

    def dot(left, right):
        return jnp.dot(left, right, preferred_element_type=jnp.float32)

    def dot_t(left, right):
        return lax.dot_general(
            left, right, (((1,), (1,)), ((), ())), preferred_element_type=jnp.float32
        )

    def t_dot(left, right):
        return lax.dot_general(
            left, right, (((0,), (0,)), ((), ())), preferred_element_type=jnp.float32
        )

    row_frame = lax.broadcasted_iota(jnp.int32, (rows, 32), 0) // frame_rows
    column_frame = lax.broadcasted_iota(jnp.int32, (rows, 32), 1) // RANK
    mask = row_frame == column_frame

    def low(values):
        return jnp.where(mask, values, 0.0).astype(jnp.bfloat16)

    def tiles(body, step=416):
        @pl.loop(0, rows // step)
        def _(t):
            body(pl.ds(pl.multiple_of(t * step, step), step))

    def norm_parts(values):
        center = values - jnp.mean(values, axis=-1, keepdims=True)
        spread = jnp.mean(center * center, axis=-1, keepdims=True)
        inverse = lax.rsqrt(spread + norm_epsilon)
        return center * inverse, inverse

    def norm_back(values, gain, grad):
        unit, inverse = norm_parts(values)
        scaled = grad * gain
        first = jnp.mean(scaled, axis=-1, keepdims=True)
        second = jnp.mean(scaled * unit, axis=-1, keepdims=True)
        return inverse * (scaled - first - unit * second)

    def group(g):
        return ad[g // 8, (g // 4) % 2, (g // 2) % 2, g % 2]

    def group_ref(g):
        return g16.at[g // 8, (g // 4) % 2, (g // 2) % 2, g % 2]

    def attn_block(zk):
        return w[zk, 0].reshape(width, width)

    def halves(f):
        own = pl.ds(pl.multiple_of(f * frame_rows + h * HALF_PITCH, 8), HALF_PITCH)
        other = pl.ds(pl.multiple_of(f * frame_rows + (1 - h) * HALF_PITCH, 8), HALF_PITCH)
        return own, other

    def join(dst, own_slots, other_slots):
        for f in range(2):
            own, other = halves(f)
            dst[own] = own_slots[2 * h + f][:HALF_PITCH].astype(jnp.float32)
            dst[other] = other_slots[f][:HALF_PITCH].astype(jnp.float32)

    def give(dst, own, received):
        for f in range(2):
            first, second = own[f, pl.ds(0, shard_rows)], received[f, pl.ds(0, shard_rows)]
            dst[:, f, :] = jnp.where(h == 0, first, second)
            dst[:, 2 + f, :] = jnp.where(h == 0, second, first)

    tok_move.wait_recv()
    join(xf, ts, tr)

    def first_norm(at):
        values = xf[at]
        unit, _ = norm_parts(values)
        n1[at] = (unit * g1_ref[...].reshape(1, width)).astype(jnp.bfloat16)
        mid[at] = values

    tiles(first_norm)
    ready(None)
    for k in range(4):
        ready(k)
    for k in range(4):
        bq[k] = jnp.concatenate(
            [jnp.zeros((32, local), jnp.bfloat16)]
            + [group(1 + i)[:, k * local : (k + 1) * local] for i in range(3)],
            axis=1,
        )
        ao[k] = group(4)[:, k * local : (k + 1) * local]
        bu[k] = group(7 + k)
        an[k] = group(11 + k)
    smalls[0] = low(dot_t(n1[...], group(0)))
    key_pad = (
        lax.rem(lax.broadcasted_iota(jnp.int32, (frame_rows, 1), 0), HALF_PITCH) >= shard_rows
    )
    bias = jnp.where(key_pad, -1e30, 0.0).astype(jnp.float32)

    LOW_QKV, LOW_OUT, LOW_UP, LOW_DOWN, THR_DOWN, THR_UP, THR_OUT, THR_QKV = range(8)

    def attention(i, out_low):
        zk = order(z, i)
        block = attn_block(zk)
        proj[zk] = (dot(n1[...], block) + dot(smalls[LOW_QKV], bq[zk])).astype(jnp.bfloat16)
        for f in range(2):
            at = pl.ds(f * frame_rows, frame_rows)
            for head in range(3):
                first = local + head * HEAD
                q = proj[zk, at, first : first + HEAD]
                k = proj[zk, at, first + local : first + local + HEAD]
                v = proj[zk, at, first + 2 * local : first + 2 * local + HEAD]
                scores = dot_t(k, q) * scale + bias
                exponent = jnp.exp(scores - jnp.max(scores, axis=0, keepdims=True))
                weights = exponent / jnp.sum(exponent, axis=0, keepdims=True)
                weights = weights.astype(jnp.bfloat16)
                soft[zk, f * 3 + head] = weights
                att[zk, at, head * HEAD : (head + 1) * HEAD] = (
                    t_dot(weights, v).astype(jnp.bfloat16)
                )
        gathered = att[zk]
        mid[...] += dot_t(gathered, block[:, :local])
        return out_low + dot_t(gathered, ao[zk])

    def attention_step(i, out_low):
        @pl.when(i == 1)
        def _():
            t1(6)
            t2(5)

        @pl.when(i == 2)
        def _():
            t3(4)

        @pl.when(i == 3)
        def _():
            t1(7)
            t2(6)

        return attention(i, out_low)

    out_low = lax.fori_loop(0, 4, attention_step, jnp.zeros((rows, 32), jnp.float32))
    t3(5)
    ready(4)
    smalls[LOW_OUT] = low(out_low)
    mid[...] += dot(smalls[LOW_OUT], group(5))

    def second_norm(at):
        unit, _ = norm_parts(mid[at])
        n2[at] = (unit * g2_ref[...].reshape(1, width)).astype(jnp.bfloat16)

    tiles(second_norm)
    cot_move.wait_recv()
    join(tmp, cs, cr)
    dyb[...] = tmp[...].astype(jnp.bfloat16)
    smalls[LOW_UP] = low(dot_t(n2[...], group(6)))
    smalls[THR_DOWN] = low(dot_t(dyb[...], group(15)))
    group_ref(15)[...] = jnp.zeros((32, width), jnp.bfloat16)
    t1(8)
    t2(7)
    acc[...] = mid[...]
    dn[...] = jnp.zeros_like(dn)

    def feed(i, lows):
        down_low, up_back = lows
        zk = order(z, i)
        q = 4 + 2 * i

        @pl.when((i > 0) & (i < 3))
        def _():
            t1(q + 3)
            t2(q + 2)

        tmp[...] = dot(n2[...], w[zk, 1].reshape(width, width)) + dot(smalls[LOW_UP], bu[zk])

        def gate(at):
            hidden = tmp[at]
            phi = 0.5 + 0.5 * lax.erf(hidden * math.sqrt(0.5))
            bell = jnp.exp(-0.5 * hidden * hidden) * (1.0 / math.sqrt(2.0 * math.pi))
            buf[0, at] = (hidden * phi).astype(jnp.bfloat16)
            tmp[at] = phi + hidden * bell

        tiles(gate)
        active = buf[0]

        @pl.when(i > 0)
        def _():
            t3(q + 1)

        @pl.when(i == 1)
        def _():
            t1(q + 4)

        @pl.when((i > 0) & (i < 3))
        def _():
            t2(q + 3)

        ready(q + 1)
        down = w[zk, 2].reshape(width, width)
        tmp[...] = tmp[...] * (dot(dyb[...], down) + dot(smalls[THR_DOWN], an[zk]))
        buf[1] = tmp[...].astype(jnp.bfloat16)
        d_hidden = buf[1]
        dn[...] += dot_t(d_hidden, w[zk, 1].reshape(width, width))
        acc[...] += dot_t(active, down)
        gu = 7 + zk
        ga = 11 + zk
        g16[gu // 8, lax.rem(gu // 4, 2), lax.rem(gu // 2, 2), lax.rem(gu, 2)] = t_dot(
            smalls[LOW_UP], d_hidden
        ).astype(jnp.bfloat16)
        g16[ga // 8, lax.rem(ga // 4, 2), lax.rem(ga // 2, 2), lax.rem(ga, 2)] = t_dot(
            smalls[THR_DOWN], active
        ).astype(jnp.bfloat16)
        down_low = down_low + dot_t(active, an[zk])
        up_back = up_back + dot_t(d_hidden, bu[zk])

        @pl.when(i < 3)
        def _():
            t3(q + 2)
            ready(q + 2)

        return down_low, up_back

    empty = jnp.zeros((rows, 32), jnp.float32)
    down_low, up_back = lax.fori_loop(0, 4, feed, (empty, empty))
    smalls[LOW_DOWN] = low(down_low)
    smalls[THR_UP] = low(up_back)
    group_ref(15)[...] = t_dot(smalls[LOW_DOWN], dyb[...]).astype(jnp.bfloat16)

    def core_move(yx):
        src = g16.at[yx // 2, yx % 2, 1 - c]
        return remote(src, gc.at[yx], cxs.at[yx], cxr.at[yx], place(y, x, 1 - c, z))

    def owner_move(yx, zz):
        back_yx = lax.rem(y * 2 + x + 4 - yx, 4)
        back_z = lax.rem(z + 4 - zz, 4)
        slot = back_yx * 4 + back_z
        src = gs.at[yx, zz // 2, :, pl.ds((zz % 2) * span, span)]
        copy = remote(src, rb.at[slot], us.at[yx, zz], ur.at[slot], (yx * 2 + c, zz))
        return copy, slot

    def spread_out(yx):
        core_move(yx).wait_recv()
        for g in range(2):
            gs[yx, g] = (
                g16[yx // 2, yx % 2, c, g].astype(jnp.float32) + gc[yx, g].astype(jnp.float32)
            ).astype(jnp.bfloat16)
        for zz in range(4):
            copy, slot = owner_move(yx, zz)

            @pl.when(slot != 0)
            def _():
                copy.start()

            @pl.when(slot == 0)
            def _():
                rb[0] = gs[yx, zz // 2, :, pl.ds((zz % 2) * span, span)]

    core_move(3).start()
    core_move(2).start()

    dn[...] += dot(smalls[THR_UP], group(6))
    group_ref(6)[...] = t_dot(smalls[THR_UP], n2[...]).astype(jnp.bfloat16)
    acc[...] += dot(smalls[LOW_DOWN], group(15))

    def second_back(at):
        value = dyb[at].astype(jnp.float32) + norm_back(mid[at], g2_ref[...].reshape(1, width), dn[at])
        dn[at] = value
        dbr[at] = value.astype(jnp.bfloat16)

    tiles(second_back)
    for f in range(2):
        own, other = halves(f)
        osend[f, pl.ds(0, HALF_PITCH)] = acc[other].astype(jnp.bfloat16)
        own_act[f] = acc[own].astype(jnp.bfloat16)
    act_move.start()
    smalls[THR_OUT] = low(dot_t(dbr[...], group(5)))
    group_ref(5)[...] = t_dot(smalls[LOW_OUT], dbr[...]).astype(jnp.bfloat16)
    for k in range(4):
        dpj[k, :, 0:local] = jnp.zeros((rows, local), jnp.bfloat16)
    acc[...] = jnp.zeros_like(acc)

    spread_out(3)
    spread_out(2)
    group_ref(4)[...] = jnp.concatenate(
        [t_dot(smalls[THR_OUT], att[k]).astype(jnp.bfloat16) for k in range(4)], axis=1
    )
    core_move(1).start()

    def attention_back(zk, qkv_back):
        block = attn_block(zk)
        d_att = (dot(dbr[...], block[:, :local]) + dot(smalls[THR_OUT], ao[zk])).astype(
            jnp.bfloat16
        )
        buf[0, :, 0:local] = d_att

        @pl.when(zk == 1)
        def _():
            spread_out(1)

        for f in range(2):
            at = pl.ds(f * frame_rows, frame_rows)
            for head in range(3):
                first = local + head * HEAD
                q = proj[zk, at, first : first + HEAD]
                k = proj[zk, at, first + local : first + local + HEAD]
                v = proj[zk, at, first + 2 * local : first + 2 * local + HEAD]
                d_out = buf[0, at, head * HEAD : (head + 1) * HEAD]
                weights = soft[zk, f * 3 + head]
                d_values = dot(weights, d_out)
                d_soft = dot_t(v, d_out)
                wide = weights.astype(jnp.float32)
                inner = jnp.sum(wide * d_soft, axis=0, keepdims=True)
                d_scores = (wide * (d_soft - inner)).astype(jnp.bfloat16)
                d_keys = dot(d_scores, q) * scale
                d_queries = t_dot(k, d_scores).T * scale
                dpj[zk, at, first : first + HEAD] = d_queries.astype(jnp.bfloat16)
                dpj[zk, at, first + local : first + local + HEAD] = d_keys.astype(jnp.bfloat16)
                dpj[zk, at, first + 2 * local : first + 2 * local + HEAD] = d_values.astype(
                    jnp.bfloat16
                )
        d_projected = dpj[zk]
        acc[...] += dot_t(d_projected, block)
        return qkv_back + dot_t(d_projected, bq[zk])

    qkv_back = lax.fori_loop(0, 4, attention_back, empty)
    smalls[THR_QKV] = low(qkv_back)
    acc[...] += dot(smalls[THR_QKV], group(0))

    def first_back(at):
        acc[at] = dn[at] + norm_back(xf[at], g1_ref[...].reshape(1, width), acc[at])

    tiles(first_back)
    for f in range(2):
        own, other = halves(f)
        isend[f, pl.ds(0, HALF_PITCH)] = acc[other].astype(jnp.bfloat16)
        own_ing[f] = acc[own].astype(jnp.bfloat16)
    ing_move.start()
    group_ref(0)[...] = t_dot(smalls[THR_QKV], n1[...]).astype(jnp.bfloat16)
    parts = [t_dot(smalls[LOW_QKV], dpj[k]).astype(jnp.bfloat16) for k in range(4)]
    for i in range(3):
        first = (1 + i) * local
        group_ref(1 + i)[...] = jnp.concatenate(
            [parts[k][:, first : first + local] for k in range(4)], axis=1
        )
    core_move(0).start()
    spread_out(0)

    act_move.wait_recv()
    give(act_ref, own_act, orecv)

    for slot in range(1, 16):
        remote(rb.at[slot], rb.at[slot], us.at[0, 0], ur.at[slot], (dp, zp)).wait_recv()
    for parity in range(2):
        total = jnp.zeros((32, span), jnp.float32)
        for slot in range(16):
            if slot % 2 == parity:
                total = total + rb[slot].astype(jnp.float32)
        first = lax.rem(h + parity, 2)
        for a in range(table_ref.shape[0] // RANK):
            chosen = [
                jnp.where(
                    jnp.full((RANK, span), clip_ref[2 * first + i]) == a,
                    total[i * RANK : (i + 1) * RANK],
                    0.0,
                )
                for i in range(2)
            ]
            gr_ref[first, pl.ds(a * RANK, RANK)] = chosen[0] + chosen[1]
    for yx in range(4):
        core_move(yx).wait_send()
        for zz in range(4):
            copy, slot = owner_move(yx, zz)

            @pl.when(slot != 0)
            def _():
                copy.wait_send()

    tok_move.wait_send()
    cot_move.wait_send()
    for j in range(1, 4):
        ad_move(j).wait_send()

    for q in (1, 2, 3, 6, 7, 8, 9, 10, 11):
        z_move(q).wait_send()
    for q in range(4):
        for what in range(9):
            move(q, what).wait_send()

    @pl.loop(4, 12)
    def _(q):
        for what in range(9):
            move(q, what).wait_send()

    for what in range(9):
        move(None, what).wait_send()
    act_move.wait_send()
    ing_move.wait()
    give(ing_ref, own_ing, irecv)


def fused(
    tokens,
    cotangent,
    clip_adapter,
    gain_one,
    gain_two,
    w_qkv,
    w_out,
    w_up,
    w_down,
    adapters,
    moment_one,
    moment_two,
):
    micro_count, shard_rows, width = tokens.shape
    rank_all, span = adapters.shape
    rows = 4 * HALF_PITCH
    frame_rows = 2 * HALF_PITCH
    local = width // 4
    bf, f32 = jnp.bfloat16, jnp.float32
    vmem = pl.BlockSpec(memory_space=pltpu.VMEM)
    scratch = [
        pltpu.VMEM((4, 3, 2, 2, 2, 96, width), bf),
        pltpu.VMEM((2, 2, 2, 2, 32, width), bf),
        pltpu.VMEM((4, HALF_SLOT, width), bf),
        pltpu.VMEM((4, HALF_SLOT, width), bf),
        pltpu.VMEM((2, HALF_SLOT, width), bf),
        pltpu.VMEM((2, HALF_SLOT, width), bf),
        pltpu.VMEM((rows, width), f32),
        pltpu.VMEM((rows, width), bf),
        pltpu.VMEM((rows, width), bf),
        pltpu.VMEM((rows, width), bf),
        pltpu.VMEM((4, rows, width), bf),
        pltpu.VMEM((4, 6, frame_rows, frame_rows), bf),
        pltpu.VMEM((4, rows, local), bf),
        pltpu.VMEM((rows, width), f32),
        pltpu.VMEM((rows, width), f32),
        pltpu.VMEM((rows, width), f32),
        pltpu.VMEM((rows, width), f32),
        pltpu.VMEM((2, rows, width), bf),
        pltpu.VMEM((rows, width), bf),
        pltpu.VMEM((4, rows, width), bf),
        pltpu.VMEM((4, 32, width), bf),
        pltpu.VMEM((4, 32, local), bf),
        pltpu.VMEM((4, 32, width), bf),
        pltpu.VMEM((4, 32, width), bf),
        pltpu.VMEM((2, 2, 2, 2, 32, width), bf),
        pltpu.VMEM((4, 2, 32, width), bf),
        pltpu.VMEM((4, 2, 32, width), bf),
        pltpu.VMEM((16, 32, span), bf),
        pltpu.VMEM((2, HALF_SLOT, width), bf),
        pltpu.VMEM((2, HALF_SLOT, width), bf),
        pltpu.VMEM((2, HALF_PITCH, width), bf),
        pltpu.VMEM((2, HALF_PITCH, width), bf),
        pltpu.VMEM((2, HALF_SLOT, width), bf),
        pltpu.VMEM((2, HALF_SLOT, width), bf),
        pltpu.VMEM((2, 32, span), bf),
        pltpu.VMEM((8, rows, 32), bf),
        pltpu.SemaphoreType.DMA((3, 4)),
        pltpu.SemaphoreType.DMA((3, 4)),
        pltpu.SemaphoreType.DMA((4,)),
        pltpu.SemaphoreType.DMA((4,)),
        pltpu.SemaphoreType.DMA((13, 9)),
        pltpu.SemaphoreType.DMA((13, 9)),
        pltpu.SemaphoreType.DMA((4,)),
        pltpu.SemaphoreType.DMA((4,)),
        pltpu.SemaphoreType.DMA((4,)),
        pltpu.SemaphoreType.DMA((4,)),
        pltpu.SemaphoreType.DMA((4, 4)),
        pltpu.SemaphoreType.DMA((16,)),
    ]
    act, ing, grads = pl.pallas_call(
        fused_kernel,
        out_shape=(
            jax.ShapeDtypeStruct((shard_rows, micro_count, width), bf),
            jax.ShapeDtypeStruct((shard_rows, micro_count, width), bf),
            jax.ShapeDtypeStruct((2, rank_all, span), f32),
        ),
        in_specs=[vmem] * 9 + [pl.BlockSpec(memory_space=pltpu.SMEM)],
        out_specs=(vmem, vmem, vmem),
        scratch_shapes=scratch,
        compiler_params=pltpu.CompilerParams(
            collective_id=0, has_side_effects=True, vmem_limit_bytes=60 * 2**20
        ),
    )(
        tokens.transpose(1, 0, 2),
        cotangent.transpose(1, 0, 2),
        gain_one,
        gain_two,
        w_qkv.transpose(1, 0, 2),
        w_out,
        w_up,
        w_down.T,
        adapters,
        clip_adapter,
    )
    return (act.transpose(1, 0, 2), ing.transpose(1, 0, 2)) + adam(
        grads[0] + grads[1], adapters, moment_one, moment_two
    )


def layer(tokens, *others):
    w_up = others[6]
    sizes = lax.axis_size("dp"), lax.axis_size("mp")
    frames_micro = tokens.shape[1] * sizes[0] * sizes[1] // FRAME
    fits = (
        sizes == (8, 4)
        and tokens.shape[0] == 4
        and 2 * tokens.shape[1] == FRAME
        and frames_micro == CLIP_FRAMES
        and w_up.shape == (tokens.shape[2] // 8, tokens.shape[2])
    )
    return (fused if fits else shards)(tokens, *others)


def solution(mesh):
    spread = P(None, ("dp", "mp"))
    rows = P(None, ("dp", "mp"), None)
    return jax.shard_map(
        layer,
        mesh=mesh,
        in_specs=(
            rows,
            rows,
            P(),
            P(),
            P(),
            P("dp", None, "mp"),
            P("mp", "dp"),
            P("dp", "mp"),
            P("mp", "dp"),
            spread,
            spread,
            spread,
        ),
        out_specs=(rows, rows, spread, spread, spread, spread, spread),
        check_vma=False,
    )
```

```python
import functools
import math

import jax
import jax.numpy as jnp
from jax import lax
from jax.experimental import pallas as pl
from jax.experimental.pallas import tpu as pltpu
from jax.sharding import PartitionSpec as P

HEAD = 64
FRAME = 196
RANK = 16
CLIP_FRAMES = 16
STEP = 5

norm_epsilon = 1e-06
beta_first = 0.5
beta_second = 0.5
learn_rate = 0.05
weight_decay = 0.01
adam_epsilon = 1e-08


def dot(left, right):
    return jnp.dot(left, right, preferred_element_type=jnp.float32)


def dot_t(left, right):
    return lax.dot_general(left, right, (((1,), (1,)), ((), ())), preferred_element_type=jnp.float32)


def t_dot(left, right):
    return lax.dot_general(left, right, (((0,), (0,)), ((), ())), preferred_element_type=jnp.float32)


def half(values):
    return values.astype(jnp.bfloat16)


def norm_parts(values):
    center = values - jnp.mean(values, axis=-1, keepdims=True)
    spread = jnp.mean(center * center, axis=-1, keepdims=True)
    inverse = lax.rsqrt(spread + norm_epsilon)
    return center * inverse, inverse


def norm_back(unit, inverse, gain, grad):
    scaled = grad * gain
    first = jnp.mean(scaled, axis=-1, keepdims=True)
    second = jnp.mean(scaled * unit, axis=-1, keepdims=True)
    return inverse * (scaled - first - unit * second)


def adam(owner_grad, adapters, moment_one, moment_two):
    first_moment = beta_first * moment_one + (1.0 - beta_first) * owner_grad
    second_moment = beta_second * moment_two + (1.0 - beta_second) * owner_grad * owner_grad
    first_hat = first_moment / (1.0 - beta_first**STEP)
    second_hat = second_moment / (1.0 - beta_second**STEP)
    updated = adapters - learn_rate * (
        first_hat / (jnp.sqrt(second_hat) + adam_epsilon) + weight_decay * adapters
    )
    return (
        owner_grad,
        updated,
        first_moment,
        second_moment,
        updated.astype(jnp.bfloat16),
    )


def shards(
    tokens,
    cotangent,
    clip_adapter,
    gain_one,
    gain_two,
    w_qkv,
    w_out,
    w_up,
    w_down,
    adapters,
    moment_one,
    moment_two,
):
    groups = lax.axis_size("mp")
    member = lax.axis_index("mp")
    group_index = lax.axis_index("dp")
    micro_count, shard_rows, width = tokens.shape
    hidden_width = w_up.shape[1] * groups
    heads = width // HEAD
    rank_all = adapters.shape[0]
    full_width = adapters.shape[1] * lax.axis_size(("dp", "mp"))
    frames = shard_rows * groups // FRAME
    frames_micro = frames * lax.axis_size("dp")
    scale = 1.0 / math.sqrt(HEAD)
    span = FRAME // shard_rows
    mine = micro_count // span
    part = member % span
    pairs = [[first * span + k for k in range(span)] for first in range(groups // span)]

    def swap(rows):
        return lax.all_to_all(
            rows, "mp", split_axis=0, concat_axis=1, axis_index_groups=pairs, tiled=True
        ).reshape(mine * FRAME, width)

    def swap_back(rows):
        return lax.all_to_all(
            rows.reshape(mine, FRAME, width),
            "mp",
            split_axis=1,
            concat_axis=0,
            axis_index_groups=pairs,
            tiled=True,
        )

    inputs = swap(tokens).astype(jnp.float32)
    dy = swap(cotangent)

    def whole(weight, first, second):
        return lax.all_gather(
            lax.all_gather(weight, first[0], axis=first[1], tiled=True),
            second[0],
            axis=second[1],
            tiled=True,
        )

    qkv_all = whole(w_qkv, ("dp", 0), ("mp", 2)).reshape(width, 3 * width)
    out_all = whole(w_out, ("dp", 1), ("mp", 0))
    up_all = whole(w_up, ("dp", 0), ("mp", 1))
    down_all = whole(w_down, ("dp", 1), ("mp", 0))
    table = lax.all_gather(half(adapters), ("dp", "mp"), axis=1, tiled=True)
    table = table.reshape(rank_all // RANK, RANK, full_width)
    clips = jnp.stack(
        [
            ((part * mine + i) * frames_micro + group_index * frames + member // span)
            // CLIP_FRAMES
            for i in range(mine)
        ]
    )
    chosen = clip_adapter[clips]
    own = table[chosen].reshape(mine * RANK, full_width)
    ends = [0, width, 4 * width, 5 * width, 6 * width, 7 * width]
    ends += [7 * width + hidden_width, 7 * width + 2 * hidden_width, full_width]
    a_qkv, b_qkv, a_out, b_out, a_up, b_up, a_down, b_down = [
        own[:, ends[i] : ends[i + 1]] for i in range(8)
    ]
    rows = mine * FRAME
    row_frame = lax.broadcasted_iota(jnp.int32, (rows, mine * RANK), 0) // FRAME
    column_frame = lax.broadcasted_iota(jnp.int32, (rows, mine * RANK), 1) // RANK
    mask = row_frame == column_frame

    def low(values):
        return half(jnp.where(mask, values, 0.0))

    shape_heads = (mine, FRAME, heads, HEAD)
    unit_one, inverse_one = norm_parts(inputs)
    normed_one = half(unit_one * gain_one)
    low_qkv = low(dot_t(normed_one, a_qkv))
    projected = half(dot(normed_one, qkv_all) + dot(low_qkv, b_qkv))
    queries = projected[:, 0:width].reshape(shape_heads)
    keys = projected[:, width : 2 * width].reshape(shape_heads)
    values = projected[:, 2 * width :].reshape(shape_heads)
    scores = jnp.einsum("fqhd,fkhd->fhqk", queries, keys, preferred_element_type=jnp.float32)
    scores = scores * scale
    exponent = jnp.exp(scores - jnp.max(scores, axis=-1, keepdims=True))
    soft = exponent / jnp.sum(exponent, axis=-1, keepdims=True)
    soft_half = half(soft)
    attended = half(
        jnp.einsum("fhqk,fkhd->fqhd", soft_half, values, preferred_element_type=jnp.float32)
    ).reshape(rows, width)
    low_out = low(dot_t(attended, a_out))
    middle = inputs + dot(attended, out_all) + dot(low_out, b_out)
    unit_two, inverse_two = norm_parts(middle)
    normed_two = half(unit_two * gain_two)
    low_up = low(dot_t(normed_two, a_up))
    hidden = dot(normed_two, up_all) + dot(low_up, b_up)
    phi = 0.5 * (1.0 + lax.erf(hidden * math.sqrt(0.5)))
    active = half(hidden * phi)
    slope = phi + hidden * jnp.exp(-0.5 * hidden * hidden) * (1.0 / math.sqrt(2.0 * math.pi))
    low_down = low(dot_t(active, a_down))
    outputs = half(middle + dot(active, down_all) + dot(low_down, b_down))

    through_down = low(dot_t(dy, b_down))
    d_active = dot_t(dy, down_all) + dot(through_down, a_down)
    d_hidden = half(d_active * slope)
    through_up = low(dot_t(d_hidden, b_up))
    d_normed_two = dot_t(d_hidden, up_all) + dot(through_up, a_up)
    d_middle = dy.astype(jnp.float32) + norm_back(unit_two, inverse_two, gain_two, d_normed_two)
    d_branch = half(d_middle)
    through_out = low(dot_t(d_branch, b_out))
    d_attended = half(dot_t(d_branch, out_all) + dot(through_out, a_out))
    d_heads = d_attended.reshape(shape_heads)
    d_values = jnp.einsum("fhqk,fqhd->fkhd", soft_half, d_heads, preferred_element_type=jnp.float32)
    d_soft = jnp.einsum("fqhd,fkhd->fhqk", d_heads, values, preferred_element_type=jnp.float32)
    inner = jnp.sum(soft * d_soft, axis=-1, keepdims=True)
    d_scores = half(soft * (d_soft - inner))
    d_queries = scale * jnp.einsum(
        "fhqk,fkhd->fqhd", d_scores, keys, preferred_element_type=jnp.float32
    )
    d_keys = scale * jnp.einsum(
        "fhqk,fqhd->fkhd", d_scores, queries, preferred_element_type=jnp.float32
    )
    d_projected = half(
        jnp.concatenate([d.reshape(rows, width) for d in (d_queries, d_keys, d_values)], axis=1)
    )
    through_qkv = low(dot_t(d_projected, b_qkv))
    d_normed_one = dot_t(d_projected, qkv_all) + dot(through_qkv, a_qkv)
    input_grad = half(d_middle + norm_back(unit_one, inverse_one, gain_one, d_normed_one))
    grads = half(jnp.concatenate(
        [
            t_dot(through_qkv, normed_one),
            t_dot(low_qkv, d_projected),
            t_dot(through_out, attended),
            t_dot(low_out, d_branch),
            t_dot(through_up, normed_two),
            t_dot(low_up, d_hidden),
            t_dot(through_down, active),
            t_dot(low_down, dy),
        ],
        axis=1,
    ))
    pick = (
        lax.broadcasted_iota(jnp.int32, (rank_all, mine * RANK), 0)
        == jnp.repeat(chosen, RANK)[None, :] * RANK
        + lax.broadcasted_iota(jnp.int32, (rank_all, mine * RANK), 1) % RANK
    ).astype(jnp.bfloat16)
    owner_grad = lax.psum_scatter(
        dot(pick, grads), ("dp", "mp"), scatter_dimension=1, tiled=True
    )
    return (swap_back(outputs), swap_back(input_grad)) + adam(
        owner_grad, adapters, moment_one, moment_two
    )


MESH = pl.DeviceIdType.MESH
X1, Y1, Y2, X2, C0, C1A, C1B, C2A, C2B = range(9)
HALF_PITCH = 104
HALF_SLOT = 112


def fused_kernel(
    tok_ref,
    cot_ref,
    g1_ref,
    g2_ref,
    wq_ref,
    wo_ref,
    wu_ref,
    wd_ref,
    table_ref,
    clip_ref,
    act_ref,
    ing_ref,
    gr_ref,
    w,
    ad,
    ts,
    cs,
    tr,
    cr,
    xf,
    dyb,
    n1,
    n2,
    proj,
    soft,
    att,
    mid,
    acc,
    dn,
    tmp,
    buf,
    dbr,
    dpj,
    bq,
    ao,
    bu,
    an,
    g16,
    gc,
    gs,
    rb,
    osend,
    isend,
    own_act,
    own_ing,
    orecv,
    irecv,
    adp,
    smalls,
    zs,
    zr,
    azs,
    azr,
    ss,
    rs,
    ps,
    pr,
    cxs,
    cxr,
    us,
    ur,
):
    dp = lax.axis_index("dp")
    z = lax.axis_index("mp")
    y = dp // 4
    x = lax.rem(dp // 2, 2)
    c = lax.rem(dp, 2)
    h = lax.rem(z, 2)
    zp = z + 1 - 2 * h
    zn = 4
    shard_rows = tok_ref.shape[0]
    rows = xf.shape[0]
    frame_rows = rows // 2
    width = xf.shape[1]
    local = width // zn
    scale = 1.0 / math.sqrt(HEAD)

    def place(yy, xx, cc, zz):
        return ((yy * 2 + xx) * 2 + cc, zz)

    def order(at_z, k):
        upper = at_z // 2
        near = at_z + upper * (3 - 2 * at_z)
        swapped = jnp.where((near == 1) & (k < 2), 1 - k, k)
        return swapped + upper * (3 - 2 * swapped)

    def rank_of(at_z, block_z):
        upper = at_z // 2
        near = at_z + upper * (3 - 2 * at_z)
        mirrored = block_z + upper * (3 - 2 * block_z)
        return jnp.where((near == 1) & (mirrored < 2), 1 - mirrored, mirrored)

    barrier = pltpu.get_barrier_semaphore()
    for k in range(1, 16):
        yx = lax.rem(y * 2 + x + k // 4, 4)
        target = (yx * 2 + c, lax.rem(z + k % 4, 4))
        pl.semaphore_signal(barrier, inc=1, device_id=target, device_id_type=MESH)
    pl.semaphore_signal(barrier, inc=1, device_id=place(y, x, 1 - c, z), device_id_type=MESH)

    def remote(src, dst, send, recv, target):
        return pltpu.make_async_remote_copy(
            src_ref=src,
            dst_ref=dst,
            send_sem=send,
            recv_sem=recv,
            device_id=target,
            device_id_type=MESH,
        )

    w[z, 0, y, x, c] = jnp.concatenate([wo_ref[...].T] + [wq_ref[i] for i in range(3)], axis=1)
    span = table_ref.shape[1]
    low_columns = pl.ds(pl.multiple_of(lax.rem(z, 2) * span, 128), span)
    for m in range(4):
        clip = jnp.full((RANK, span), clip_ref[m])
        chosen = jnp.zeros((RANK, span), jnp.float32)
        for a in range(table_ref.shape[0] // RANK):
            chosen = jnp.where(clip == a, table_ref[a * RANK : (a + 1) * RANK], chosen)
        adp[m // 2, pl.ds((m % 2) * RANK, RANK)] = chosen.astype(jnp.bfloat16)
    ad[y, x, c, z // 2, :, low_columns] = adp[h]

    def stage(dst, src):
        for m in range(4):
            dst[m, pl.ds(96, 16)] = jnp.zeros((16, width), jnp.bfloat16)
            dst[m, pl.ds(0, shard_rows)] = src[:, m, :]

    def part(kind, zk, yy, xx, cc, first, count):
        return w.at[zk, kind, yy, xx, cc, pl.ds(first, count), :]

    def phase(q):
        if isinstance(q, int):
            return (0, q) if q < 4 else (1 + q % 2, (q - 4) // 2)
        return 1 + lax.rem(q, 2), (q - 4) // 2

    def move(q, what):
        full = 32 if q is None else 96
        n = full // 2
        every = pl.ds(0, 2)
        args, target = {
            X1: ((y, x, c, 0, n), (y, 1 - x, c)),
            Y1: ((y, x, c, n, n), (1 - y, x, c)),
            Y2: ((y, every, c, 0, n), (1 - y, x, c)),
            X2: ((every, x, c, n, n), (y, 1 - x, c)),
            C0: ((y, x, c, 0, full), (y, x, 1 - c)),
            C1A: ((y, 1 - x, c, 0, n), (y, x, 1 - c)),
            C1B: ((1 - y, x, c, n, n), (y, x, 1 - c)),
            C2A: ((1 - y, every, c, 0, n), (y, x, 1 - c)),
            C2B: ((every, 1 - x, c, n, n), (y, x, 1 - c)),
        }[what]
        if q is None:
            yy, xx, cc, first, count = args
            ref = ad.at[yy, xx, cc, :, pl.ds(first, count), :]
            index = 12
        else:
            kind, k = phase(q)
            ref = part(kind, order(z, k), *args)
            index = q
        return remote(ref, ref, ss.at[index, what], rs.at[index, what], place(*target, z))

    def z_move(q):
        kind, k = phase(q)
        ref = part(kind, z, y, x, c, 0, 96)
        other = order(z, k)
        return remote(ref, ref, zs.at[kind, k], zr.at[kind, rank_of(other, z)], (dp, other))

    def z_wait(q):
        kind, k = phase(q)
        ref = part(kind, z, y, x, c, 0, 96)
        remote(ref, ref, zs.at[kind, k], zr.at[kind, k], (dp, zp)).wait_recv()

    def ad_move(j):
        other = lax.rem(z + zn - j, zn)
        dst = ad.at[y, x, c, z // 2, :, low_columns]
        return remote(adp.at[lax.rem(other, 2)], dst, azs.at[j], azr.at[j], (dp, other))

    def t1(q):
        if isinstance(q, int):
            if q is not None and phase(q)[1]:
                z_wait(q)
        elif q is not None:
            z_wait(q)
        for what in (X1, Y1, C0):
            move(q, what).start()

    def t2(q):
        move(q, X1).wait_recv()
        move(q, Y2).start()
        move(q, Y1).wait_recv()
        move(q, X2).start()
        move(q, C1A).start()
        move(q, C1B).start()

    def t3(q):
        move(q, Y2).wait_recv()
        move(q, C2A).start()
        move(q, X2).wait_recv()
        move(q, C2B).start()

    def ready(q):
        for what in (C0, C1A, C1B, C2A, C2B):
            move(q, what).wait_recv()

    tok_move = remote(
        ts.at[pl.ds(2 - 2 * h, 2)], tr, ps.at[0], pr.at[0], (dp, zp)
    )
    cot_move = remote(
        cs.at[pl.ds(2 - 2 * h, 2)], cr, ps.at[1], pr.at[1], (dp, zp)
    )
    act_move = remote(
        osend, orecv, ps.at[2], pr.at[2], (dp, zp)
    )
    ing_moves = [
        remote(isend.at[f], irecv.at[f], ps.at[3 + f], pr.at[3 + f], (dp, zp)) for f in range(2)
    ]

    pl.semaphore_wait(barrier, 16)
    t1(0)
    for j in range(1, 4):
        ad_move(j).start()
    for j in range(1, 4):
        z_move(j).start()
    w[z, 1, y, x, c] = wu_ref[...]
    t1(4)
    stage(ts, tok_ref)
    tok_move.start()
    w[z, 2, y, x, c] = wd_ref[...]
    t2(0)
    t1(1)
    for j in range(1, 4):
        ad_move(j).wait_recv()
    t1(None)
    t2(1)
    t1(2)
    t2(None)
    t3(0)
    z_move(6).start()
    z_move(7).start()
    t2(2)
    t1(3)
    t3(1)
    t3(None)
    stage(cs, cot_ref)
    cot_move.start()
    t2(3)
    t2(4)
    t3(2)
    z_move(8).start()
    z_move(9).start()
    t1(5)
    t3(3)
    z_move(10).start()
    z_move(11).start()

    def dot(left, right):
        return jnp.dot(left, right, preferred_element_type=jnp.float32)

    def dot_t(left, right):
        return lax.dot_general(
            left, right, (((1,), (1,)), ((), ())), preferred_element_type=jnp.float32
        )

    def t_dot(left, right):
        return lax.dot_general(
            left, right, (((0,), (0,)), ((), ())), preferred_element_type=jnp.float32
        )

    row_frame = lax.broadcasted_iota(jnp.int32, (rows, 32), 0) // frame_rows
    column_frame = lax.broadcasted_iota(jnp.int32, (rows, 32), 1) // RANK
    mask = row_frame == column_frame

    def low(values):
        return jnp.where(mask, values, 0.0).astype(jnp.bfloat16)

    def tiles(body, step=416):
        @pl.loop(0, rows // step)
        def _(t):
            body(pl.ds(pl.multiple_of(t * step, step), step))

    def norm_parts(values):
        center = values - jnp.mean(values, axis=-1, keepdims=True)
        spread = jnp.mean(center * center, axis=-1, keepdims=True)
        inverse = lax.rsqrt(spread + norm_epsilon)
        return center * inverse, inverse

    def norm_back(values, gain, grad):
        unit, inverse = norm_parts(values)
        scaled = grad * gain
        first = jnp.mean(scaled, axis=-1, keepdims=True)
        second = jnp.mean(scaled * unit, axis=-1, keepdims=True)
        return inverse * (scaled - first - unit * second)

    def group(g):
        return ad[g // 8, (g // 4) % 2, (g // 2) % 2, g % 2]

    def group_ref(g):
        return g16.at[g // 8, (g // 4) % 2, (g // 2) % 2, g % 2]

    def attn_block(zk):
        return w[zk, 0].reshape(width, width)

    def halves(f):
        own = pl.ds(pl.multiple_of(f * frame_rows + h * HALF_PITCH, 8), HALF_PITCH)
        other = pl.ds(pl.multiple_of(f * frame_rows + (1 - h) * HALF_PITCH, 8), HALF_PITCH)
        return own, other

    def join(dst, own_slots, other_slots):
        for f in range(2):
            own, other = halves(f)
            dst[own] = own_slots[2 * h + f][:HALF_PITCH].astype(jnp.float32)
            dst[other] = other_slots[f][:HALF_PITCH].astype(jnp.float32)

    def give(dst, own, received):
        for f in range(2):
            first, second = own[f, pl.ds(0, shard_rows)], received[f, pl.ds(0, shard_rows)]
            dst[:, f, :] = jnp.where(h == 0, first, second)
            dst[:, 2 + f, :] = jnp.where(h == 0, second, first)

    tok_move.wait_recv()
    join(xf, ts, tr)

    def first_norm(at):
        values = xf[at]
        unit, _ = norm_parts(values)
        n1[at] = (unit * g1_ref[...].reshape(1, width)).astype(jnp.bfloat16)
        mid[at] = values

    tiles(first_norm)
    ready(None)
    for k in range(4):
        ready(k)
    for k in range(4):
        bq[k] = jnp.concatenate(
            [jnp.zeros((32, local), jnp.bfloat16)]
            + [group(1 + i)[:, k * local : (k + 1) * local] for i in range(3)],
            axis=1,
        )
        ao[k] = group(4)[:, k * local : (k + 1) * local]
        bu[k] = group(7 + k)
        an[k] = group(11 + k)
    smalls[0] = low(dot_t(n1[...], group(0)))
    key_pad = (
        lax.rem(lax.broadcasted_iota(jnp.int32, (frame_rows, 1), 0), HALF_PITCH) >= shard_rows
    )
    bias = jnp.where(key_pad, -1e30, 0.0).astype(jnp.float32)

    LOW_QKV, LOW_OUT, LOW_UP, LOW_DOWN, THR_DOWN, THR_UP, THR_OUT, THR_QKV = range(8)

    def attention(i, out_low):
        zk = order(z, i)
        block = attn_block(zk)
        proj[zk] = (dot(n1[...], block) + dot(smalls[LOW_QKV], bq[zk])).astype(jnp.bfloat16)
        for f in range(2):
            at = pl.ds(f * frame_rows, frame_rows)
            for head in range(3):
                first = local + head * HEAD
                q = proj[zk, at, first : first + HEAD]
                k = proj[zk, at, first + local : first + local + HEAD]
                v = proj[zk, at, first + 2 * local : first + 2 * local + HEAD]
                scores = dot_t(k, q) * scale + bias
                exponent = jnp.exp(scores - jnp.max(scores, axis=0, keepdims=True))
                weights = exponent / jnp.sum(exponent, axis=0, keepdims=True)
                weights = weights.astype(jnp.bfloat16)
                soft[zk, f * 3 + head] = weights
                att[zk, at, head * HEAD : (head + 1) * HEAD] = (
                    t_dot(weights, v).astype(jnp.bfloat16)
                )
        gathered = att[zk]
        mid[...] += dot_t(gathered, block[:, :local])
        return out_low + dot_t(gathered, ao[zk])

    def attention_step(i, out_low):
        @pl.when(i == 1)
        def _():
            t1(6)
            t2(5)

        @pl.when(i == 2)
        def _():
            t3(4)

        @pl.when(i == 3)
        def _():
            t1(7)
            t2(6)

        return attention(i, out_low)

    out_low = lax.fori_loop(0, 4, attention_step, jnp.zeros((rows, 32), jnp.float32))
    t3(5)
    ready(4)
    smalls[LOW_OUT] = low(out_low)
    mid[...] += dot(smalls[LOW_OUT], group(5))

    def second_norm(at):
        unit, _ = norm_parts(mid[at])
        n2[at] = (unit * g2_ref[...].reshape(1, width)).astype(jnp.bfloat16)

    tiles(second_norm)
    cot_move.wait_recv()
    join(tmp, cs, cr)
    dyb[...] = tmp[...].astype(jnp.bfloat16)
    smalls[LOW_UP] = low(dot_t(n2[...], group(6)))
    smalls[THR_DOWN] = low(dot_t(dyb[...], group(15)))
    group_ref(15)[...] = jnp.zeros((32, width), jnp.bfloat16)
    t1(8)
    t2(7)
    acc[...] = mid[...]
    dn[...] = jnp.zeros_like(dn)

    def feed(i, lows):
        down_low, up_back = lows
        zk = order(z, i)
        q = 4 + 2 * i

        @pl.when((i > 0) & (i < 3))
        def _():
            t1(q + 3)
            t2(q + 2)

        tmp[...] = dot(n2[...], w[zk, 1].reshape(width, width)) + dot(smalls[LOW_UP], bu[zk])

        def gate(at):
            hidden = tmp[at]
            phi = 0.5 + 0.5 * lax.erf(hidden * math.sqrt(0.5))
            bell = jnp.exp(-0.5 * hidden * hidden) * (1.0 / math.sqrt(2.0 * math.pi))
            buf[0, at] = (hidden * phi).astype(jnp.bfloat16)
            tmp[at] = phi + hidden * bell

        tiles(gate)
        active = buf[0]
        down_low = down_low + dot_t(active, an[zk])
        ga = 11 + zk
        g16[ga // 8, lax.rem(ga // 4, 2), lax.rem(ga // 2, 2), lax.rem(ga, 2)] = t_dot(
            smalls[THR_DOWN], active
        ).astype(jnp.bfloat16)

        @pl.when(i > 0)
        def _():
            t3(q + 1)

        @pl.when(i == 1)
        def _():
            t1(q + 4)

        @pl.when((i > 0) & (i < 3))
        def _():
            t2(q + 3)

        ready(q + 1)
        down = w[zk, 2].reshape(width, width)
        tmp[...] = tmp[...] * (dot(dyb[...], down) + dot(smalls[THR_DOWN], an[zk]))
        buf[1] = tmp[...].astype(jnp.bfloat16)
        d_hidden = buf[1]
        dn[...] += dot_t(d_hidden, w[zk, 1].reshape(width, width))
        acc[...] += dot_t(active, down)
        gu = 7 + zk
        g16[gu // 8, lax.rem(gu // 4, 2), lax.rem(gu // 2, 2), lax.rem(gu, 2)] = t_dot(
            smalls[LOW_UP], d_hidden
        ).astype(jnp.bfloat16)
        up_back = up_back + dot_t(d_hidden, bu[zk])

        @pl.when(i < 3)
        def _():
            t3(q + 2)
            ready(q + 2)

        return down_low, up_back

    empty = jnp.zeros((rows, 32), jnp.float32)
    down_low, up_back = lax.fori_loop(0, 4, feed, (empty, empty))
    smalls[LOW_DOWN] = low(down_low)
    smalls[THR_UP] = low(up_back)
    group_ref(15)[...] = t_dot(smalls[LOW_DOWN], dyb[...]).astype(jnp.bfloat16)

    def core_move(yx):
        src = g16.at[yx // 2, yx % 2, 1 - c]
        return remote(src, gc.at[yx], cxs.at[yx], cxr.at[yx], place(y, x, 1 - c, z))

    def owner_move(yx, zz):
        back_yx = lax.rem(y * 2 + x + 4 - yx, 4)
        back_z = lax.rem(z + 4 - zz, 4)
        slot = back_yx * 4 + back_z
        src = gs.at[yx, zz // 2, :, pl.ds((zz % 2) * span, span)]
        copy = remote(src, rb.at[slot], us.at[yx, zz], ur.at[slot], (yx * 2 + c, zz))
        return copy, slot

    def spread_out(yx):
        core_move(yx).wait_recv()
        for g in range(2):
            gs[yx, g] = (
                g16[yx // 2, yx % 2, c, g].astype(jnp.float32) + gc[yx, g].astype(jnp.float32)
            ).astype(jnp.bfloat16)
        for zz in range(4):
            copy, slot = owner_move(yx, zz)

            @pl.when(slot != 0)
            def _():
                copy.start()

            @pl.when(slot == 0)
            def _():
                rb[0] = gs[yx, zz // 2, :, pl.ds((zz % 2) * span, span)]

    core_move(3).start()
    core_move(2).start()

    group_ref(6)[...] = t_dot(smalls[THR_UP], n2[...]).astype(jnp.bfloat16)
    acc[...] += dot(smalls[LOW_DOWN], group(15))

    def second_back(at):
        grad = dn[at] + dot(smalls[THR_UP, at], group(6))
        value = dyb[at].astype(jnp.float32) + norm_back(
            mid[at], g2_ref[...].reshape(1, width), grad
        )
        dn[at] = value
        dbr[at] = value.astype(jnp.bfloat16)

    tiles(second_back)
    for f in range(2):
        own, other = halves(f)
        osend[f, pl.ds(0, HALF_PITCH)] = acc[other].astype(jnp.bfloat16)
        own_act[f] = acc[own].astype(jnp.bfloat16)
    act_move.start()
    smalls[THR_OUT] = low(dot_t(dbr[...], group(5)))
    group_ref(5)[...] = t_dot(smalls[LOW_OUT], dbr[...]).astype(jnp.bfloat16)
    for k in range(4):
        dpj[k, :, 0:local] = jnp.zeros((rows, local), jnp.bfloat16)
    acc[...] = jnp.zeros_like(acc)

    spread_out(3)
    spread_out(2)
    group_ref(4)[...] = jnp.concatenate(
        [t_dot(smalls[THR_OUT], att[k]).astype(jnp.bfloat16) for k in range(4)], axis=1
    )
    core_move(1).start()

    def attention_back(zk, qkv_back):
        block = attn_block(zk)
        d_att = (dot(dbr[...], block[:, :local]) + dot(smalls[THR_OUT], ao[zk])).astype(
            jnp.bfloat16
        )
        buf[0, :, 0:local] = d_att

        @pl.when(zk == 1)
        def _():
            spread_out(1)

        for f in range(2):
            at = pl.ds(f * frame_rows, frame_rows)
            for head in range(3):
                first = local + head * HEAD
                q = proj[zk, at, first : first + HEAD]
                k = proj[zk, at, first + local : first + local + HEAD]
                v = proj[zk, at, first + 2 * local : first + 2 * local + HEAD]
                d_out = buf[0, at, head * HEAD : (head + 1) * HEAD]
                weights = soft[zk, f * 3 + head]
                d_values = dot(weights, d_out)
                d_soft = dot_t(v, d_out)
                wide = weights.astype(jnp.float32)
                inner = jnp.sum(wide * d_soft, axis=0, keepdims=True)
                d_scores = (wide * (d_soft - inner)).astype(jnp.bfloat16)
                d_keys = dot(d_scores, q) * scale
                d_queries = t_dot(k, d_scores).T * scale
                dpj[zk, at, first : first + HEAD] = d_queries.astype(jnp.bfloat16)
                dpj[zk, at, first + local : first + local + HEAD] = d_keys.astype(jnp.bfloat16)
                dpj[zk, at, first + 2 * local : first + 2 * local + HEAD] = d_values.astype(
                    jnp.bfloat16
                )
        d_projected = dpj[zk]
        acc[...] += dot_t(d_projected, block)
        return qkv_back + dot_t(d_projected, bq[zk])

    qkv_back = lax.fori_loop(0, 4, attention_back, empty)
    smalls[THR_QKV] = low(qkv_back)

    def first_back(at):
        grad = acc[at] + dot(smalls[THR_QKV, at], group(0))
        acc[at] = dn[at] + norm_back(xf[at], g1_ref[...].reshape(1, width), grad)

    tiles(first_back)
    for f in range(2):
        own, other = halves(f)
        isend[f, pl.ds(0, HALF_PITCH)] = acc[other].astype(jnp.bfloat16)
        own_ing[f] = acc[own].astype(jnp.bfloat16)
    for f in range(2):
        ing_moves[f].start()
    group_ref(0)[...] = t_dot(smalls[THR_QKV], n1[...]).astype(jnp.bfloat16)
    parts = [t_dot(smalls[LOW_QKV], dpj[k]).astype(jnp.bfloat16) for k in range(4)]
    for i in range(3):
        first = (1 + i) * local
        group_ref(1 + i)[...] = jnp.concatenate(
            [parts[k][:, first : first + local] for k in range(4)], axis=1
        )
    core_move(0).start()
    spread_out(0)

    act_move.wait_recv()
    give(act_ref, own_act, orecv)

    for slot in range(1, 16):
        remote(rb.at[slot], rb.at[slot], us.at[0, 0], ur.at[slot], (dp, zp)).wait_recv()
    for parity in range(2):
        total = jnp.zeros((32, span), jnp.float32)
        for slot in range(16):
            if slot % 2 == parity:
                total = total + rb[slot].astype(jnp.float32)
        first = lax.rem(h + parity, 2)
        for a in range(table_ref.shape[0] // RANK):
            chosen = [
                jnp.where(
                    jnp.full((RANK, span), clip_ref[2 * first + i]) == a,
                    total[i * RANK : (i + 1) * RANK],
                    0.0,
                )
                for i in range(2)
            ]
            gr_ref[first, pl.ds(a * RANK, RANK)] = chosen[0] + chosen[1]
    for yx in range(4):
        core_move(yx).wait_send()
        for zz in range(4):
            copy, slot = owner_move(yx, zz)

            @pl.when(slot != 0)
            def _():
                copy.wait_send()

    tok_move.wait_send()
    cot_move.wait_send()
    for j in range(1, 4):
        ad_move(j).wait_send()

    for q in (1, 2, 3, 6, 7, 8, 9, 10, 11):
        z_move(q).wait_send()
    for q in range(4):
        for what in range(9):
            move(q, what).wait_send()

    @pl.loop(4, 12)
    def _(q):
        for what in range(9):
            move(q, what).wait_send()

    for what in range(9):
        move(None, what).wait_send()
    act_move.wait_send()
    for f in range(2):
        ing_moves[f].wait()
    give(ing_ref, own_ing, irecv)


def finish_kernel(
    act_ref, ing_ref, gr_ref, table_ref, one_ref, two_ref, act_out, ing_out, *outs
):
    act_out[...] = act_ref[...]
    ing_out[...] = ing_ref[...]
    results = adam(gr_ref[0] + gr_ref[1], table_ref[...], one_ref[...], two_ref[...])
    for out, result in zip(outs, results):
        out[...] = result


def fused(
    tokens,
    cotangent,
    clip_adapter,
    gain_one,
    gain_two,
    w_qkv,
    w_out,
    w_up,
    w_down,
    adapters,
    moment_one,
    moment_two,
):
    micro_count, shard_rows, width = tokens.shape
    rank_all, span = adapters.shape
    rows = 4 * HALF_PITCH
    frame_rows = 2 * HALF_PITCH
    local = width // 4
    bf, f32 = jnp.bfloat16, jnp.float32
    vmem = pl.BlockSpec(memory_space=pltpu.VMEM)
    smem = pl.BlockSpec(memory_space=pltpu.SMEM)
    scratch = [
        pltpu.VMEM((4, 3, 2, 2, 2, 96, width), bf),
        pltpu.VMEM((2, 2, 2, 2, 32, width), bf),
        pltpu.VMEM((4, HALF_SLOT, width), bf),
        pltpu.VMEM((4, HALF_SLOT, width), bf),
        pltpu.VMEM((2, HALF_SLOT, width), bf),
        pltpu.VMEM((2, HALF_SLOT, width), bf),
        pltpu.VMEM((rows, width), f32),
        pltpu.VMEM((rows, width), bf),
        pltpu.VMEM((rows, width), bf),
        pltpu.VMEM((rows, width), bf),
        pltpu.VMEM((4, rows, width), bf),
        pltpu.VMEM((4, 6, frame_rows, frame_rows), bf),
        pltpu.VMEM((4, rows, local), bf),
        pltpu.VMEM((rows, width), f32),
        pltpu.VMEM((rows, width), f32),
        pltpu.VMEM((rows, width), f32),
        pltpu.VMEM((rows, width), f32),
        pltpu.VMEM((2, rows, width), bf),
        pltpu.VMEM((rows, width), bf),
        pltpu.VMEM((4, rows, width), bf),
        pltpu.VMEM((4, 32, width), bf),
        pltpu.VMEM((4, 32, local), bf),
        pltpu.VMEM((4, 32, width), bf),
        pltpu.VMEM((4, 32, width), bf),
        pltpu.VMEM((2, 2, 2, 2, 32, width), bf),
        pltpu.VMEM((4, 2, 32, width), bf),
        pltpu.VMEM((4, 2, 32, width), bf),
        pltpu.VMEM((16, 32, span), bf),
        pltpu.VMEM((2, HALF_SLOT, width), bf),
        pltpu.VMEM((2, HALF_SLOT, width), bf),
        pltpu.VMEM((2, HALF_PITCH, width), bf),
        pltpu.VMEM((2, HALF_PITCH, width), bf),
        pltpu.VMEM((2, HALF_SLOT, width), bf),
        pltpu.VMEM((2, HALF_SLOT, width), bf),
        pltpu.VMEM((2, 32, span), bf),
        pltpu.VMEM((8, rows, 32), bf),
        pltpu.SemaphoreType.DMA((3, 4)),
        pltpu.SemaphoreType.DMA((3, 4)),
        pltpu.SemaphoreType.DMA((4,)),
        pltpu.SemaphoreType.DMA((4,)),
        pltpu.SemaphoreType.DMA((13, 9)),
        pltpu.SemaphoreType.DMA((13, 9)),
        pltpu.SemaphoreType.DMA((5,)),
        pltpu.SemaphoreType.DMA((5,)),
        pltpu.SemaphoreType.DMA((4,)),
        pltpu.SemaphoreType.DMA((4,)),
        pltpu.SemaphoreType.DMA((4, 4)),
        pltpu.SemaphoreType.DMA((16,)),
    ]
    act, ing, grads = pl.pallas_call(
        fused_kernel,
        out_shape=(
            jax.ShapeDtypeStruct((shard_rows, micro_count, width), bf),
            jax.ShapeDtypeStruct((shard_rows, micro_count, width), bf),
            jax.ShapeDtypeStruct((2, rank_all, span), f32),
        ),
        in_specs=[vmem] * 9 + [smem],
        out_specs=(vmem, vmem, vmem),
        scratch_shapes=scratch,
        compiler_params=pltpu.CompilerParams(
            collective_id=0, has_side_effects=True, vmem_limit_bytes=60 * 2**20
        ),
    )(
        tokens.transpose(1, 0, 2),
        cotangent.transpose(1, 0, 2),
        gain_one,
        gain_two,
        w_qkv.transpose(1, 0, 2),
        w_out,
        w_up,
        w_down.T,
        adapters,
        clip_adapter,
    )
    plain = jax.ShapeDtypeStruct((rank_all, span), f32)
    rows_spec = pl.BlockSpec((shard_rows // 2, micro_count, width), lambda i: (i, 0, 0))
    plain_spec = pl.BlockSpec((rank_all // 2, span), lambda i: (i, 0))
    act, ing, *others = pl.pallas_call(
        finish_kernel,
        out_shape=(act, ing) + (plain,) * 4 + (jax.ShapeDtypeStruct((rank_all, span), bf),),
        grid=(2,),
        in_specs=[rows_spec] * 2
        + [pl.BlockSpec((2, rank_all // 2, span), lambda i: (0, i, 0))]
        + [plain_spec] * 3,
        out_specs=(rows_spec,) * 2 + (plain_spec,) * 5,
    )(act, ing, grads, adapters, moment_one, moment_two)
    return (act.transpose(1, 0, 2), ing.transpose(1, 0, 2), *others)


def layer(tokens, *others):
    w_up = others[6]
    sizes = lax.axis_size("dp"), lax.axis_size("mp")
    frames_micro = tokens.shape[1] * sizes[0] * sizes[1] // FRAME
    fits = (
        sizes == (8, 4)
        and tokens.shape[0] == 4
        and 2 * tokens.shape[1] == FRAME
        and frames_micro == CLIP_FRAMES
        and w_up.shape == (tokens.shape[2] // 8, tokens.shape[2])
    )
    return (fused if fits else shards)(tokens, *others)


def solution(mesh):
    spread = P(None, ("dp", "mp"))
    rows = P(None, ("dp", "mp"), None)
    return jax.shard_map(
        layer,
        mesh=mesh,
        in_specs=(
            rows,
            rows,
            P(),
            P(),
            P(),
            P("dp", None, "mp"),
            P("mp", "dp"),
            P("dp", "mp"),
            P("mp", "dp"),
            spread,
            spread,
            spread,
        ),
        out_specs=(rows, rows, spread, spread, spread, spread, spread),
        check_vma=False,
    )
```

```python
import functools
import math

import jax
import jax.numpy as jnp
from jax import lax
from jax.experimental import pallas as pl
from jax.experimental.pallas import tpu as pltpu
from jax.sharding import PartitionSpec as P

HEAD = 64
FRAME = 196
RANK = 16
CLIP_FRAMES = 16
STEP = 5

norm_epsilon = 1e-06
beta_first = 0.5
beta_second = 0.5
learn_rate = 0.05
weight_decay = 0.01
adam_epsilon = 1e-08


def dot(left, right):
    return jnp.dot(left, right, preferred_element_type=jnp.float32)


def dot_t(left, right):
    return lax.dot_general(left, right, (((1,), (1,)), ((), ())), preferred_element_type=jnp.float32)


def t_dot(left, right):
    return lax.dot_general(left, right, (((0,), (0,)), ((), ())), preferred_element_type=jnp.float32)


def half(values):
    return values.astype(jnp.bfloat16)


def norm_parts(values):
    center = values - jnp.mean(values, axis=-1, keepdims=True)
    spread = jnp.mean(center * center, axis=-1, keepdims=True)
    inverse = lax.rsqrt(spread + norm_epsilon)
    return center * inverse, inverse


def norm_back(unit, inverse, gain, grad):
    scaled = grad * gain
    first = jnp.mean(scaled, axis=-1, keepdims=True)
    second = jnp.mean(scaled * unit, axis=-1, keepdims=True)
    return inverse * (scaled - first - unit * second)


def adam(owner_grad, adapters, moment_one, moment_two):
    first_moment = beta_first * moment_one + (1.0 - beta_first) * owner_grad
    second_moment = beta_second * moment_two + (1.0 - beta_second) * owner_grad * owner_grad
    first_hat = first_moment / (1.0 - beta_first**STEP)
    second_hat = second_moment / (1.0 - beta_second**STEP)
    updated = adapters - learn_rate * (
        first_hat / (jnp.sqrt(second_hat) + adam_epsilon) + weight_decay * adapters
    )
    return (
        owner_grad,
        updated,
        first_moment,
        second_moment,
        updated.astype(jnp.bfloat16),
    )


def shards(
    tokens,
    cotangent,
    clip_adapter,
    gain_one,
    gain_two,
    w_qkv,
    w_out,
    w_up,
    w_down,
    adapters,
    moment_one,
    moment_two,
):
    groups = lax.axis_size("mp")
    member = lax.axis_index("mp")
    group_index = lax.axis_index("dp")
    micro_count, shard_rows, width = tokens.shape
    hidden_width = w_up.shape[1] * groups
    heads = width // HEAD
    rank_all = adapters.shape[0]
    full_width = adapters.shape[1] * lax.axis_size(("dp", "mp"))
    frames = shard_rows * groups // FRAME
    frames_micro = frames * lax.axis_size("dp")
    scale = 1.0 / math.sqrt(HEAD)
    span = FRAME // shard_rows
    mine = micro_count // span
    part = member % span
    pairs = [[first * span + k for k in range(span)] for first in range(groups // span)]

    def swap(rows):
        return lax.all_to_all(
            rows, "mp", split_axis=0, concat_axis=1, axis_index_groups=pairs, tiled=True
        ).reshape(mine * FRAME, width)

    def swap_back(rows):
        return lax.all_to_all(
            rows.reshape(mine, FRAME, width),
            "mp",
            split_axis=1,
            concat_axis=0,
            axis_index_groups=pairs,
            tiled=True,
        )

    inputs = swap(tokens).astype(jnp.float32)
    dy = swap(cotangent)

    def whole(weight, first, second):
        return lax.all_gather(
            lax.all_gather(weight, first[0], axis=first[1], tiled=True),
            second[0],
            axis=second[1],
            tiled=True,
        )

    qkv_all = whole(w_qkv, ("dp", 0), ("mp", 2)).reshape(width, 3 * width)
    out_all = whole(w_out, ("dp", 1), ("mp", 0))
    up_all = whole(w_up, ("dp", 0), ("mp", 1))
    down_all = whole(w_down, ("dp", 1), ("mp", 0))
    table = lax.all_gather(half(adapters), ("dp", "mp"), axis=1, tiled=True)
    table = table.reshape(rank_all // RANK, RANK, full_width)
    clips = jnp.stack(
        [
            ((part * mine + i) * frames_micro + group_index * frames + member // span)
            // CLIP_FRAMES
            for i in range(mine)
        ]
    )
    chosen = clip_adapter[clips]
    own = table[chosen].reshape(mine * RANK, full_width)
    ends = [0, width, 4 * width, 5 * width, 6 * width, 7 * width]
    ends += [7 * width + hidden_width, 7 * width + 2 * hidden_width, full_width]
    a_qkv, b_qkv, a_out, b_out, a_up, b_up, a_down, b_down = [
        own[:, ends[i] : ends[i + 1]] for i in range(8)
    ]
    rows = mine * FRAME
    row_frame = lax.broadcasted_iota(jnp.int32, (rows, mine * RANK), 0) // FRAME
    column_frame = lax.broadcasted_iota(jnp.int32, (rows, mine * RANK), 1) // RANK
    mask = row_frame == column_frame

    def low(values):
        return half(jnp.where(mask, values, 0.0))

    shape_heads = (mine, FRAME, heads, HEAD)
    unit_one, inverse_one = norm_parts(inputs)
    normed_one = half(unit_one * gain_one)
    low_qkv = low(dot_t(normed_one, a_qkv))
    projected = half(dot(normed_one, qkv_all) + dot(low_qkv, b_qkv))
    queries = projected[:, 0:width].reshape(shape_heads)
    keys = projected[:, width : 2 * width].reshape(shape_heads)
    values = projected[:, 2 * width :].reshape(shape_heads)
    scores = jnp.einsum("fqhd,fkhd->fhqk", queries, keys, preferred_element_type=jnp.float32)
    scores = scores * scale
    exponent = jnp.exp(scores - jnp.max(scores, axis=-1, keepdims=True))
    soft = exponent / jnp.sum(exponent, axis=-1, keepdims=True)
    soft_half = half(soft)
    attended = half(
        jnp.einsum("fhqk,fkhd->fqhd", soft_half, values, preferred_element_type=jnp.float32)
    ).reshape(rows, width)
    low_out = low(dot_t(attended, a_out))
    middle = inputs + dot(attended, out_all) + dot(low_out, b_out)
    unit_two, inverse_two = norm_parts(middle)
    normed_two = half(unit_two * gain_two)
    low_up = low(dot_t(normed_two, a_up))
    hidden = dot(normed_two, up_all) + dot(low_up, b_up)
    phi = 0.5 * (1.0 + lax.erf(hidden * math.sqrt(0.5)))
    active = half(hidden * phi)
    slope = phi + hidden * jnp.exp(-0.5 * hidden * hidden) * (1.0 / math.sqrt(2.0 * math.pi))
    low_down = low(dot_t(active, a_down))
    outputs = half(middle + dot(active, down_all) + dot(low_down, b_down))

    through_down = low(dot_t(dy, b_down))
    d_active = dot_t(dy, down_all) + dot(through_down, a_down)
    d_hidden = half(d_active * slope)
    through_up = low(dot_t(d_hidden, b_up))
    d_normed_two = dot_t(d_hidden, up_all) + dot(through_up, a_up)
    d_middle = dy.astype(jnp.float32) + norm_back(unit_two, inverse_two, gain_two, d_normed_two)
    d_branch = half(d_middle)
    through_out = low(dot_t(d_branch, b_out))
    d_attended = half(dot_t(d_branch, out_all) + dot(through_out, a_out))
    d_heads = d_attended.reshape(shape_heads)
    d_values = jnp.einsum("fhqk,fqhd->fkhd", soft_half, d_heads, preferred_element_type=jnp.float32)
    d_soft = jnp.einsum("fqhd,fkhd->fhqk", d_heads, values, preferred_element_type=jnp.float32)
    inner = jnp.sum(soft * d_soft, axis=-1, keepdims=True)
    d_scores = half(soft * (d_soft - inner))
    d_queries = scale * jnp.einsum(
        "fhqk,fkhd->fqhd", d_scores, keys, preferred_element_type=jnp.float32
    )
    d_keys = scale * jnp.einsum(
        "fhqk,fqhd->fkhd", d_scores, queries, preferred_element_type=jnp.float32
    )
    d_projected = half(
        jnp.concatenate([d.reshape(rows, width) for d in (d_queries, d_keys, d_values)], axis=1)
    )
    through_qkv = low(dot_t(d_projected, b_qkv))
    d_normed_one = dot_t(d_projected, qkv_all) + dot(through_qkv, a_qkv)
    input_grad = half(d_middle + norm_back(unit_one, inverse_one, gain_one, d_normed_one))
    grads = half(jnp.concatenate(
        [
            t_dot(through_qkv, normed_one),
            t_dot(low_qkv, d_projected),
            t_dot(through_out, attended),
            t_dot(low_out, d_branch),
            t_dot(through_up, normed_two),
            t_dot(low_up, d_hidden),
            t_dot(through_down, active),
            t_dot(low_down, dy),
        ],
        axis=1,
    ))
    pick = (
        lax.broadcasted_iota(jnp.int32, (rank_all, mine * RANK), 0)
        == jnp.repeat(chosen, RANK)[None, :] * RANK
        + lax.broadcasted_iota(jnp.int32, (rank_all, mine * RANK), 1) % RANK
    ).astype(jnp.bfloat16)
    owner_grad = lax.psum_scatter(
        dot(pick, grads), ("dp", "mp"), scatter_dimension=1, tiled=True
    )
    return (swap_back(outputs), swap_back(input_grad)) + adam(
        owner_grad, adapters, moment_one, moment_two
    )


MESH = pl.DeviceIdType.MESH
X1, Y1, Y2, X2, C0, C1A, C1B, C2A, C2B = range(9)
HALF_PITCH = 104
HALF_SLOT = 112


def fused_kernel(
    tok_ref,
    cot_ref,
    g1_ref,
    g2_ref,
    wq_ref,
    wo_ref,
    wu_ref,
    wd_ref,
    table_ref,
    clip_ref,
    act_ref,
    ing_ref,
    gr_ref,
    w,
    ad,
    ts,
    cs,
    tr,
    cr,
    xf,
    dyb,
    n1,
    n2,
    proj,
    soft,
    att,
    mid,
    acc,
    dn,
    tmp,
    buf,
    dbr,
    dpj,
    bq,
    ao,
    bu,
    an,
    g16,
    gc,
    gs,
    rb,
    osend,
    isend,
    own_act,
    own_ing,
    orecv,
    irecv,
    adp,
    smalls,
    zs,
    zr,
    azs,
    azr,
    ss,
    rs,
    ps,
    pr,
    cxs,
    cxr,
    us,
    ur,
):
    dp = lax.axis_index("dp")
    z = lax.axis_index("mp")
    y = dp // 4
    x = lax.rem(dp // 2, 2)
    c = lax.rem(dp, 2)
    h = lax.rem(z, 2)
    zp = z + 1 - 2 * h
    zn = 4
    shard_rows = tok_ref.shape[0]
    rows = xf.shape[0]
    frame_rows = rows // 2
    width = xf.shape[1]
    local = width // zn
    scale = 1.0 / math.sqrt(HEAD)

    def place(yy, xx, cc, zz):
        return ((yy * 2 + xx) * 2 + cc, zz)

    def order(at_z, k):
        upper = at_z // 2
        near = at_z + upper * (3 - 2 * at_z)
        swapped = jnp.where((near == 1) & (k < 2), 1 - k, k)
        return swapped + upper * (3 - 2 * swapped)

    def rank_of(at_z, block_z):
        upper = at_z // 2
        near = at_z + upper * (3 - 2 * at_z)
        mirrored = block_z + upper * (3 - 2 * block_z)
        return jnp.where((near == 1) & (mirrored < 2), 1 - mirrored, mirrored)

    barrier = pltpu.get_barrier_semaphore()
    for k in range(1, 16):
        yx = lax.rem(y * 2 + x + k // 4, 4)
        target = (yx * 2 + c, lax.rem(z + k % 4, 4))
        pl.semaphore_signal(barrier, inc=1, device_id=target, device_id_type=MESH)
    pl.semaphore_signal(barrier, inc=1, device_id=place(y, x, 1 - c, z), device_id_type=MESH)

    def remote(src, dst, send, recv, target):
        return pltpu.make_async_remote_copy(
            src_ref=src,
            dst_ref=dst,
            send_sem=send,
            recv_sem=recv,
            device_id=target,
            device_id_type=MESH,
        )

    w[z, 0, y, x, c] = jnp.concatenate([wo_ref[...].T] + [wq_ref[i] for i in range(3)], axis=1)
    span = table_ref.shape[1]
    low_columns = pl.ds(pl.multiple_of(lax.rem(z, 2) * span, 128), span)
    for m in range(4):
        clip = jnp.full((RANK, span), clip_ref[m])
        chosen = jnp.zeros((RANK, span), jnp.float32)
        for a in range(table_ref.shape[0] // RANK):
            chosen = jnp.where(clip == a, table_ref[a * RANK : (a + 1) * RANK], chosen)
        adp[m // 2, pl.ds((m % 2) * RANK, RANK)] = chosen.astype(jnp.bfloat16)
    ad[y, x, c, z // 2, :, low_columns] = adp[h]

    def stage(dst, src):
        for m in range(4):
            dst[m, pl.ds(96, 16)] = jnp.zeros((16, width), jnp.bfloat16)
            dst[m, pl.ds(0, shard_rows)] = src[:, m, :]

    def part(kind, zk, yy, xx, cc, first, count):
        return w.at[zk, kind, yy, xx, cc, pl.ds(first, count), :]

    def phase(q):
        if isinstance(q, int):
            return (0, q) if q < 4 else (1 + q % 2, (q - 4) // 2)
        return 1 + lax.rem(q, 2), (q - 4) // 2

    def move(q, what):
        full = 32 if q is None else 96
        n = full // 2
        every = pl.ds(0, 2)
        args, target = {
            X1: ((y, x, c, 0, n), (y, 1 - x, c)),
            Y1: ((y, x, c, n, n), (1 - y, x, c)),
            Y2: ((y, every, c, 0, n), (1 - y, x, c)),
            X2: ((every, x, c, n, n), (y, 1 - x, c)),
            C0: ((y, x, c, 0, full), (y, x, 1 - c)),
            C1A: ((y, 1 - x, c, 0, n), (y, x, 1 - c)),
            C1B: ((1 - y, x, c, n, n), (y, x, 1 - c)),
            C2A: ((1 - y, every, c, 0, n), (y, x, 1 - c)),
            C2B: ((every, 1 - x, c, n, n), (y, x, 1 - c)),
        }[what]
        if q is None:
            yy, xx, cc, first, count = args
            ref = ad.at[yy, xx, cc, :, pl.ds(first, count), :]
            index = 12
        else:
            kind, k = phase(q)
            ref = part(kind, order(z, k), *args)
            index = q
        return remote(ref, ref, ss.at[index, what], rs.at[index, what], place(*target, z))

    def z_move(q):
        kind, k = phase(q)
        ref = part(kind, z, y, x, c, 0, 96)
        other = order(z, k)
        return remote(ref, ref, zs.at[kind, k], zr.at[kind, rank_of(other, z)], (dp, other))

    def z_wait(q):
        kind, k = phase(q)
        ref = part(kind, z, y, x, c, 0, 96)
        remote(ref, ref, zs.at[kind, k], zr.at[kind, k], (dp, zp)).wait_recv()

    def ad_move(j):
        other = lax.rem(z + zn - j, zn)
        dst = ad.at[y, x, c, z // 2, :, low_columns]
        return remote(adp.at[lax.rem(other, 2)], dst, azs.at[j], azr.at[j], (dp, other))

    def t1(q):
        if isinstance(q, int):
            if q is not None and phase(q)[1]:
                z_wait(q)
        elif q is not None:
            z_wait(q)
        for what in (X1, Y1, C0):
            move(q, what).start()

    def t2(q):
        move(q, X1).wait_recv()
        move(q, Y2).start()
        move(q, Y1).wait_recv()
        move(q, X2).start()
        move(q, C1A).start()
        move(q, C1B).start()

    def t3(q):
        move(q, Y2).wait_recv()
        move(q, C2A).start()
        move(q, X2).wait_recv()
        move(q, C2B).start()

    def ready(q):
        for what in (C0, C1A, C1B, C2A, C2B):
            move(q, what).wait_recv()

    tok_move = remote(
        ts.at[pl.ds(2 - 2 * h, 2)], tr, ps.at[0], pr.at[0], (dp, zp)
    )
    cot_move = remote(
        cs.at[pl.ds(2 - 2 * h, 2)], cr, ps.at[1], pr.at[1], (dp, zp)
    )
    act_move = remote(
        osend, orecv, ps.at[2], pr.at[2], (dp, zp)
    )
    ing_moves = [
        remote(isend.at[f], irecv.at[f], ps.at[3 + f], pr.at[3 + f], (dp, zp)) for f in range(2)
    ]

    pl.semaphore_wait(barrier, 16)
    t1(0)
    for j in range(1, 4):
        ad_move(j).start()
    z_move(1).start()
    w[z, 1, y, x, c] = wu_ref[...]
    t1(4)
    stage(ts, tok_ref)
    tok_move.start()
    z_move(2).start()
    z_move(3).start()
    w[z, 2, y, x, c] = wd_ref[...]
    t2(0)
    t1(1)
    for j in range(1, 4):
        ad_move(j).wait_recv()
    t1(None)
    t2(1)
    t1(2)
    t2(None)
    t3(0)
    z_move(6).start()
    z_move(7).start()
    t2(2)
    t1(3)
    t3(1)
    t3(None)
    t2(3)
    t2(4)
    t3(2)
    z_move(8).start()
    z_move(9).start()
    stage(cs, cot_ref)
    cot_move.start()
    t1(5)
    t3(3)
    z_move(10).start()
    z_move(11).start()

    def dot(left, right):
        return jnp.dot(left, right, preferred_element_type=jnp.float32)

    def dot_t(left, right):
        return lax.dot_general(
            left, right, (((1,), (1,)), ((), ())), preferred_element_type=jnp.float32
        )

    def t_dot(left, right):
        return lax.dot_general(
            left, right, (((0,), (0,)), ((), ())), preferred_element_type=jnp.float32
        )

    row_frame = lax.broadcasted_iota(jnp.int32, (rows, 32), 0) // frame_rows
    column_frame = lax.broadcasted_iota(jnp.int32, (rows, 32), 1) // RANK
    mask = row_frame == column_frame

    def low(values):
        return jnp.where(mask, values, 0.0).astype(jnp.bfloat16)

    def tiles(body, step=416):
        @pl.loop(0, rows // step)
        def _(t):
            body(pl.ds(pl.multiple_of(t * step, step), step))

    def norm_parts(values):
        center = values - jnp.mean(values, axis=-1, keepdims=True)
        spread = jnp.mean(center * center, axis=-1, keepdims=True)
        inverse = lax.rsqrt(spread + norm_epsilon)
        return center * inverse, inverse

    def norm_back(values, gain, grad):
        unit, inverse = norm_parts(values)
        scaled = grad * gain
        first = jnp.mean(scaled, axis=-1, keepdims=True)
        second = jnp.mean(scaled * unit, axis=-1, keepdims=True)
        return inverse * (scaled - first - unit * second)

    def group(g):
        return ad[g // 8, (g // 4) % 2, (g // 2) % 2, g % 2]

    def group_ref(g):
        return g16.at[g // 8, (g // 4) % 2, (g // 2) % 2, g % 2]

    def attn_block(zk):
        return w[zk, 0].reshape(width, width)

    def halves(f):
        own = pl.ds(pl.multiple_of(f * frame_rows + h * HALF_PITCH, 8), HALF_PITCH)
        other = pl.ds(pl.multiple_of(f * frame_rows + (1 - h) * HALF_PITCH, 8), HALF_PITCH)
        return own, other

    def join(dst, own_slots, other_slots):
        for f in range(2):
            own, other = halves(f)
            dst[own] = own_slots[2 * h + f][:HALF_PITCH].astype(jnp.float32)
            dst[other] = other_slots[f][:HALF_PITCH].astype(jnp.float32)

    def give(dst, own, received):
        for f in range(2):
            first, second = own[f, pl.ds(0, shard_rows)], received[f, pl.ds(0, shard_rows)]
            dst[:, f, :] = jnp.where(h == 0, first, second)
            dst[:, 2 + f, :] = jnp.where(h == 0, second, first)

    tok_move.wait_recv()
    join(xf, ts, tr)

    def first_norm(at):
        values = xf[at]
        unit, _ = norm_parts(values)
        n1[at] = (unit * g1_ref[...].reshape(1, width)).astype(jnp.bfloat16)
        mid[at] = values

    tiles(first_norm)
    ready(None)
    for k in range(4):
        ready(k)
    for k in range(4):
        bq[k] = jnp.concatenate(
            [jnp.zeros((32, local), jnp.bfloat16)]
            + [group(1 + i)[:, k * local : (k + 1) * local] for i in range(3)],
            axis=1,
        )
        ao[k] = group(4)[:, k * local : (k + 1) * local]
        bu[k] = group(7 + k)
        an[k] = group(11 + k)
    smalls[0] = low(dot_t(n1[...], group(0)))
    key_pad = (
        lax.rem(lax.broadcasted_iota(jnp.int32, (frame_rows, 1), 0), HALF_PITCH) >= shard_rows
    )
    bias = jnp.where(key_pad, -1e30, 0.0).astype(jnp.float32)

    LOW_QKV, LOW_OUT, LOW_UP, LOW_DOWN, THR_DOWN, THR_UP, THR_OUT, THR_QKV = range(8)

    def attention(i, out_low):
        zk = order(z, i)
        block = attn_block(zk)
        proj[zk] = (dot(n1[...], block) + dot(smalls[LOW_QKV], bq[zk])).astype(jnp.bfloat16)
        for f in range(2):
            at = pl.ds(f * frame_rows, frame_rows)
            for head in range(3):
                first = local + head * HEAD
                q = proj[zk, at, first : first + HEAD]
                k = proj[zk, at, first + local : first + local + HEAD]
                v = proj[zk, at, first + 2 * local : first + 2 * local + HEAD]
                scores = dot_t(k, q) * scale + bias
                exponent = jnp.exp(scores - jnp.max(scores, axis=0, keepdims=True))
                weights = exponent / jnp.sum(exponent, axis=0, keepdims=True)
                weights = weights.astype(jnp.bfloat16)
                soft[zk, f * 3 + head] = weights
                att[zk, at, head * HEAD : (head + 1) * HEAD] = (
                    t_dot(weights, v).astype(jnp.bfloat16)
                )
        gathered = att[zk]
        mid[...] += dot_t(gathered, block[:, :local])
        return out_low + dot_t(gathered, ao[zk])

    def attention_step(i, out_low):
        @pl.when(i == 1)
        def _():
            t1(6)
            t2(5)

        @pl.when(i == 2)
        def _():
            t3(4)

        @pl.when(i == 3)
        def _():
            t1(7)
            t2(6)

        return attention(i, out_low)

    out_low = lax.fori_loop(0, 4, attention_step, jnp.zeros((rows, 32), jnp.float32))
    t3(5)
    ready(4)
    smalls[LOW_OUT] = low(out_low)
    mid[...] += dot(smalls[LOW_OUT], group(5))

    def second_norm(at):
        unit, _ = norm_parts(mid[at])
        n2[at] = (unit * g2_ref[...].reshape(1, width)).astype(jnp.bfloat16)

    tiles(second_norm)
    cot_move.wait_recv()
    join(tmp, cs, cr)
    dyb[...] = tmp[...].astype(jnp.bfloat16)
    smalls[LOW_UP] = low(dot_t(n2[...], group(6)))
    smalls[THR_DOWN] = low(dot_t(dyb[...], group(15)))
    group_ref(15)[...] = jnp.zeros((32, width), jnp.bfloat16)
    t1(8)
    t2(7)
    acc[...] = mid[...]
    dn[...] = jnp.zeros_like(dn)

    def feed(i, lows):
        down_low, up_back = lows
        zk = order(z, i)
        q = 4 + 2 * i

        @pl.when((i > 0) & (i < 3))
        def _():
            t1(q + 3)
            t2(q + 2)

        tmp[...] = dot(n2[...], w[zk, 1].reshape(width, width)) + dot(smalls[LOW_UP], bu[zk])

        def gate(at):
            hidden = tmp[at]
            phi = 0.5 + 0.5 * lax.erf(hidden * math.sqrt(0.5))
            bell = jnp.exp(-0.5 * hidden * hidden) * (1.0 / math.sqrt(2.0 * math.pi))
            buf[0, at] = (hidden * phi).astype(jnp.bfloat16)
            tmp[at] = phi + hidden * bell

        tiles(gate)
        active = buf[0]
        down_low = down_low + dot_t(active, an[zk])
        ga = 11 + zk
        g16[ga // 8, lax.rem(ga // 4, 2), lax.rem(ga // 2, 2), lax.rem(ga, 2)] = t_dot(
            smalls[THR_DOWN], active
        ).astype(jnp.bfloat16)

        @pl.when(i > 0)
        def _():
            t3(q + 1)

        @pl.when(i == 1)
        def _():
            t1(q + 4)

        @pl.when((i > 0) & (i < 3))
        def _():
            t2(q + 3)

        ready(q + 1)
        down = w[zk, 2].reshape(width, width)
        tmp[...] = tmp[...] * (dot(dyb[...], down) + dot(smalls[THR_DOWN], an[zk]))
        buf[1] = tmp[...].astype(jnp.bfloat16)
        d_hidden = buf[1]
        dn[...] += dot_t(d_hidden, w[zk, 1].reshape(width, width))
        acc[...] += dot_t(active, down)
        gu = 7 + zk
        g16[gu // 8, lax.rem(gu // 4, 2), lax.rem(gu // 2, 2), lax.rem(gu, 2)] = t_dot(
            smalls[LOW_UP], d_hidden
        ).astype(jnp.bfloat16)
        up_back = up_back + dot_t(d_hidden, bu[zk])

        @pl.when(i < 3)
        def _():
            t3(q + 2)
            ready(q + 2)

        return down_low, up_back

    empty = jnp.zeros((rows, 32), jnp.float32)
    down_low, up_back = lax.fori_loop(0, 4, feed, (empty, empty))
    smalls[LOW_DOWN] = low(down_low)
    smalls[THR_UP] = low(up_back)
    group_ref(15)[...] = t_dot(smalls[LOW_DOWN], dyb[...]).astype(jnp.bfloat16)

    def core_move(yx):
        src = g16.at[yx // 2, yx % 2, 1 - c]
        return remote(src, gc.at[yx], cxs.at[yx], cxr.at[yx], place(y, x, 1 - c, z))

    def owner_move(yx, zz):
        back_yx = lax.rem(y * 2 + x + 4 - yx, 4)
        back_z = lax.rem(z + 4 - zz, 4)
        slot = back_yx * 4 + back_z
        src = gs.at[yx, zz // 2, :, pl.ds((zz % 2) * span, span)]
        copy = remote(src, rb.at[slot], us.at[yx, zz], ur.at[slot], (yx * 2 + c, zz))
        return copy, slot

    def spread_out(yx):
        core_move(yx).wait_recv()
        for g in range(2):
            gs[yx, g] = (
                g16[yx // 2, yx % 2, c, g].astype(jnp.float32) + gc[yx, g].astype(jnp.float32)
            ).astype(jnp.bfloat16)
        for zz in range(4):
            copy, slot = owner_move(yx, zz)

            @pl.when(slot != 0)
            def _():
                copy.start()

            @pl.when(slot == 0)
            def _():
                rb[0] = gs[yx, zz // 2, :, pl.ds((zz % 2) * span, span)]

    core_move(3).start()
    core_move(2).start()

    group_ref(6)[...] = t_dot(smalls[THR_UP], n2[...]).astype(jnp.bfloat16)
    acc[...] += dot(smalls[LOW_DOWN], group(15))

    def second_back(at):
        grad = dn[at] + dot(smalls[THR_UP, at], group(6))
        value = dyb[at].astype(jnp.float32) + norm_back(
            mid[at], g2_ref[...].reshape(1, width), grad
        )
        dn[at] = value
        dbr[at] = value.astype(jnp.bfloat16)

    tiles(second_back)
    for f in range(2):
        own, other = halves(f)
        osend[f, pl.ds(0, HALF_PITCH)] = acc[other].astype(jnp.bfloat16)
        own_act[f] = acc[own].astype(jnp.bfloat16)
    act_move.start()
    smalls[THR_OUT] = low(dot_t(dbr[...], group(5)))
    group_ref(5)[...] = t_dot(smalls[LOW_OUT], dbr[...]).astype(jnp.bfloat16)
    for k in range(4):
        dpj[k, :, 0:local] = jnp.zeros((rows, local), jnp.bfloat16)
    acc[...] = jnp.zeros_like(acc)

    spread_out(3)
    spread_out(2)
    group_ref(4)[...] = jnp.concatenate(
        [t_dot(smalls[THR_OUT], att[k]).astype(jnp.bfloat16) for k in range(4)], axis=1
    )
    core_move(1).start()

    def attention_back(zk, qkv_back):
        block = attn_block(zk)
        d_att = (dot(dbr[...], block[:, :local]) + dot(smalls[THR_OUT], ao[zk])).astype(
            jnp.bfloat16
        )
        buf[0, :, 0:local] = d_att

        @pl.when(zk == 1)
        def _():
            spread_out(1)

        for f in range(2):
            at = pl.ds(f * frame_rows, frame_rows)
            for head in range(3):
                first = local + head * HEAD
                q = proj[zk, at, first : first + HEAD]
                k = proj[zk, at, first + local : first + local + HEAD]
                v = proj[zk, at, first + 2 * local : first + 2 * local + HEAD]
                d_out = buf[0, at, head * HEAD : (head + 1) * HEAD]
                weights = soft[zk, f * 3 + head]
                d_values = dot(weights, d_out)
                d_soft = dot_t(v, d_out)
                wide = weights.astype(jnp.float32)
                inner = jnp.sum(wide * d_soft, axis=0, keepdims=True)
                d_scores = (wide * (d_soft - inner)).astype(jnp.bfloat16)
                d_keys = dot(d_scores, q) * scale
                d_queries = t_dot(k, d_scores).T * scale
                dpj[zk, at, first : first + HEAD] = d_queries.astype(jnp.bfloat16)
                dpj[zk, at, first + local : first + local + HEAD] = d_keys.astype(jnp.bfloat16)
                dpj[zk, at, first + 2 * local : first + 2 * local + HEAD] = d_values.astype(
                    jnp.bfloat16
                )
        d_projected = dpj[zk]
        acc[...] += dot_t(d_projected, block)
        return qkv_back + dot_t(d_projected, bq[zk])

    qkv_back = lax.fori_loop(0, 4, attention_back, empty)
    smalls[THR_QKV] = low(qkv_back)

    for f in range(2):
        at = pl.ds(f * frame_rows, frame_rows)
        grad = acc[at] + dot(smalls[THR_QKV, at], group(0))
        acc[at] = dn[at] + norm_back(xf[at], g1_ref[...].reshape(1, width), grad)
        own, other = halves(f)
        isend[f, pl.ds(0, HALF_PITCH)] = acc[other].astype(jnp.bfloat16)
        if f == 0:
            ing_moves[0].start()
        own_ing[f] = acc[own].astype(jnp.bfloat16)
    group_ref(0)[...] = t_dot(smalls[THR_QKV], n1[...]).astype(jnp.bfloat16)
    parts = [t_dot(smalls[LOW_QKV], dpj[k]).astype(jnp.bfloat16) for k in range(4)]
    for i in range(3):
        first = (1 + i) * local
        group_ref(1 + i)[...] = jnp.concatenate(
            [parts[k][:, first : first + local] for k in range(4)], axis=1
        )
    core_move(0).start()
    spread_out(0)
    ing_moves[1].start()

    act_move.wait_recv()
    give(act_ref, own_act, orecv)

    for slot in range(1, 16):
        remote(rb.at[slot], rb.at[slot], us.at[0, 0], ur.at[slot], (dp, zp)).wait_recv()
    for parity in range(2):
        total = jnp.zeros((32, span), jnp.float32)
        for slot in range(16):
            if slot % 2 == parity:
                total = total + rb[slot].astype(jnp.float32)
        first = lax.rem(h + parity, 2)
        for a in range(table_ref.shape[0] // RANK):
            chosen = [
                jnp.where(
                    jnp.full((RANK, span), clip_ref[2 * first + i]) == a,
                    total[i * RANK : (i + 1) * RANK],
                    0.0,
                )
                for i in range(2)
            ]
            gr_ref[first, pl.ds(a * RANK, RANK)] = chosen[0] + chosen[1]
    for yx in range(4):
        core_move(yx).wait_send()
        for zz in range(4):
            copy, slot = owner_move(yx, zz)

            @pl.when(slot != 0)
            def _():
                copy.wait_send()

    tok_move.wait_send()
    cot_move.wait_send()
    for j in range(1, 4):
        ad_move(j).wait_send()

    for q in (1, 2, 3, 6, 7, 8, 9, 10, 11):
        z_move(q).wait_send()
    for q in range(4):
        for what in range(9):
            move(q, what).wait_send()

    @pl.loop(4, 12)
    def _(q):
        for what in range(9):
            move(q, what).wait_send()

    for what in range(9):
        move(None, what).wait_send()
    act_move.wait_send()
    for f in range(2):
        ing_moves[f].wait()
    give(ing_ref, own_ing, irecv)


def finish_kernel(
    act_ref, ing_ref, gr_ref, table_ref, one_ref, two_ref, act_out, ing_out, *outs
):
    act_out[...] = act_ref[...]
    ing_out[...] = ing_ref[...]
    results = adam(gr_ref[0] + gr_ref[1], table_ref[...], one_ref[...], two_ref[...])
    for out, result in zip(outs, results):
        out[...] = result


def fused(
    tokens,
    cotangent,
    clip_adapter,
    gain_one,
    gain_two,
    w_qkv,
    w_out,
    w_up,
    w_down,
    adapters,
    moment_one,
    moment_two,
):
    micro_count, shard_rows, width = tokens.shape
    rank_all, span = adapters.shape
    rows = 4 * HALF_PITCH
    frame_rows = 2 * HALF_PITCH
    local = width // 4
    bf, f32 = jnp.bfloat16, jnp.float32
    vmem = pl.BlockSpec(memory_space=pltpu.VMEM)
    smem = pl.BlockSpec(memory_space=pltpu.SMEM)
    scratch = [
        pltpu.VMEM((4, 3, 2, 2, 2, 96, width), bf),
        pltpu.VMEM((2, 2, 2, 2, 32, width), bf),
        pltpu.VMEM((4, HALF_SLOT, width), bf),
        pltpu.VMEM((4, HALF_SLOT, width), bf),
        pltpu.VMEM((2, HALF_SLOT, width), bf),
        pltpu.VMEM((2, HALF_SLOT, width), bf),
        pltpu.VMEM((rows, width), f32),
        pltpu.VMEM((rows, width), bf),
        pltpu.VMEM((rows, width), bf),
        pltpu.VMEM((rows, width), bf),
        pltpu.VMEM((4, rows, width), bf),
        pltpu.VMEM((4, 6, frame_rows, frame_rows), bf),
        pltpu.VMEM((4, rows, local), bf),
        pltpu.VMEM((rows, width), f32),
        pltpu.VMEM((rows, width), f32),
        pltpu.VMEM((rows, width), f32),
        pltpu.VMEM((rows, width), f32),
        pltpu.VMEM((2, rows, width), bf),
        pltpu.VMEM((rows, width), bf),
        pltpu.VMEM((4, rows, width), bf),
        pltpu.VMEM((4, 32, width), bf),
        pltpu.VMEM((4, 32, local), bf),
        pltpu.VMEM((4, 32, width), bf),
        pltpu.VMEM((4, 32, width), bf),
        pltpu.VMEM((2, 2, 2, 2, 32, width), bf),
        pltpu.VMEM((4, 2, 32, width), bf),
        pltpu.VMEM((4, 2, 32, width), bf),
        pltpu.VMEM((16, 32, span), bf),
        pltpu.VMEM((2, HALF_SLOT, width), bf),
        pltpu.VMEM((2, HALF_SLOT, width), bf),
        pltpu.VMEM((2, HALF_PITCH, width), bf),
        pltpu.VMEM((2, HALF_PITCH, width), bf),
        pltpu.VMEM((2, HALF_SLOT, width), bf),
        pltpu.VMEM((2, HALF_SLOT, width), bf),
        pltpu.VMEM((2, 32, span), bf),
        pltpu.VMEM((8, rows, 32), bf),
        pltpu.SemaphoreType.DMA((3, 4)),
        pltpu.SemaphoreType.DMA((3, 4)),
        pltpu.SemaphoreType.DMA((4,)),
        pltpu.SemaphoreType.DMA((4,)),
        pltpu.SemaphoreType.DMA((13, 9)),
        pltpu.SemaphoreType.DMA((13, 9)),
        pltpu.SemaphoreType.DMA((5,)),
        pltpu.SemaphoreType.DMA((5,)),
        pltpu.SemaphoreType.DMA((4,)),
        pltpu.SemaphoreType.DMA((4,)),
        pltpu.SemaphoreType.DMA((4, 4)),
        pltpu.SemaphoreType.DMA((16,)),
    ]
    act, ing, grads = pl.pallas_call(
        fused_kernel,
        out_shape=(
            jax.ShapeDtypeStruct((shard_rows, micro_count, width), bf),
            jax.ShapeDtypeStruct((shard_rows, micro_count, width), bf),
            jax.ShapeDtypeStruct((2, rank_all, span), f32),
        ),
        in_specs=[vmem] * 9 + [smem],
        out_specs=(vmem, vmem, vmem),
        scratch_shapes=scratch,
        compiler_params=pltpu.CompilerParams(
            collective_id=0, has_side_effects=True, vmem_limit_bytes=60 * 2**20
        ),
    )(
        tokens.transpose(1, 0, 2),
        cotangent.transpose(1, 0, 2),
        gain_one,
        gain_two,
        w_qkv.transpose(1, 0, 2),
        w_out,
        w_up,
        w_down.T,
        adapters,
        clip_adapter,
    )
    plain = jax.ShapeDtypeStruct((rank_all, span), f32)
    rows_spec = pl.BlockSpec((shard_rows // 2, micro_count, width), lambda i: (i, 0, 0))
    plain_spec = pl.BlockSpec((rank_all // 2, span), lambda i: (i, 0))
    act, ing, *others = pl.pallas_call(
        finish_kernel,
        out_shape=(act, ing) + (plain,) * 4 + (jax.ShapeDtypeStruct((rank_all, span), bf),),
        grid=(2,),
        in_specs=[rows_spec] * 2
        + [pl.BlockSpec((2, rank_all // 2, span), lambda i: (0, i, 0))]
        + [plain_spec] * 3,
        out_specs=(rows_spec,) * 2 + (plain_spec,) * 5,
    )(act, ing, grads, adapters, moment_one, moment_two)
    return (act.transpose(1, 0, 2), ing.transpose(1, 0, 2), *others)


def layer(tokens, *others):
    w_up = others[6]
    sizes = lax.axis_size("dp"), lax.axis_size("mp")
    frames_micro = tokens.shape[1] * sizes[0] * sizes[1] // FRAME
    fits = (
        sizes == (8, 4)
        and tokens.shape[0] == 4
        and 2 * tokens.shape[1] == FRAME
        and frames_micro == CLIP_FRAMES
        and w_up.shape == (tokens.shape[2] // 8, tokens.shape[2])
    )
    return (fused if fits else shards)(tokens, *others)


def solution(mesh):
    spread = P(None, ("dp", "mp"))
    rows = P(None, ("dp", "mp"), None)
    return jax.shard_map(
        layer,
        mesh=mesh,
        in_specs=(
            rows,
            rows,
            P(),
            P(),
            P(),
            P("dp", None, "mp"),
            P("mp", "dp"),
            P("dp", "mp"),
            P("mp", "dp"),
            spread,
            spread,
            spread,
        ),
        out_specs=(rows, rows, spread, spread, spread, spread, spread),
        check_vma=False,
    )
```

```python
import functools
import math

import jax
import jax.numpy as jnp
from jax import lax
from jax.experimental import pallas as pl
from jax.experimental.pallas import tpu as pltpu
from jax.sharding import PartitionSpec as P

HEAD = 64
FRAME = 196
RANK = 16
CLIP_FRAMES = 16
STEP = 5

norm_epsilon = 1e-06
beta_first = 0.5
beta_second = 0.5
learn_rate = 0.05
weight_decay = 0.01
adam_epsilon = 1e-08


def dot(left, right):
    return jnp.dot(left, right, preferred_element_type=jnp.float32)


def dot_t(left, right):
    return lax.dot_general(left, right, (((1,), (1,)), ((), ())), preferred_element_type=jnp.float32)


def t_dot(left, right):
    return lax.dot_general(left, right, (((0,), (0,)), ((), ())), preferred_element_type=jnp.float32)


def half(values):
    return values.astype(jnp.bfloat16)


def norm_parts(values):
    center = values - jnp.mean(values, axis=-1, keepdims=True)
    spread = jnp.mean(center * center, axis=-1, keepdims=True)
    inverse = lax.rsqrt(spread + norm_epsilon)
    return center * inverse, inverse


def norm_back(unit, inverse, gain, grad):
    scaled = grad * gain
    first = jnp.mean(scaled, axis=-1, keepdims=True)
    second = jnp.mean(scaled * unit, axis=-1, keepdims=True)
    return inverse * (scaled - first - unit * second)


def adam(owner_grad, adapters, moment_one, moment_two):
    first_moment = beta_first * moment_one + (1.0 - beta_first) * owner_grad
    second_moment = beta_second * moment_two + (1.0 - beta_second) * owner_grad * owner_grad
    first_hat = first_moment / (1.0 - beta_first**STEP)
    second_hat = second_moment / (1.0 - beta_second**STEP)
    updated = adapters - learn_rate * (
        first_hat / (jnp.sqrt(second_hat) + adam_epsilon) + weight_decay * adapters
    )
    return (
        owner_grad,
        updated,
        first_moment,
        second_moment,
        updated.astype(jnp.bfloat16),
    )


def shards(
    tokens,
    cotangent,
    clip_adapter,
    gain_one,
    gain_two,
    w_qkv,
    w_out,
    w_up,
    w_down,
    adapters,
    moment_one,
    moment_two,
):
    groups = lax.axis_size("mp")
    member = lax.axis_index("mp")
    group_index = lax.axis_index("dp")
    micro_count, shard_rows, width = tokens.shape
    hidden_width = w_up.shape[1] * groups
    heads = width // HEAD
    rank_all = adapters.shape[0]
    full_width = adapters.shape[1] * lax.axis_size(("dp", "mp"))
    frames = shard_rows * groups // FRAME
    frames_micro = frames * lax.axis_size("dp")
    scale = 1.0 / math.sqrt(HEAD)
    span = FRAME // shard_rows
    mine = micro_count // span
    part = member % span
    pairs = [[first * span + k for k in range(span)] for first in range(groups // span)]

    def swap(rows):
        return lax.all_to_all(
            rows, "mp", split_axis=0, concat_axis=1, axis_index_groups=pairs, tiled=True
        ).reshape(mine * FRAME, width)

    def swap_back(rows):
        return lax.all_to_all(
            rows.reshape(mine, FRAME, width),
            "mp",
            split_axis=1,
            concat_axis=0,
            axis_index_groups=pairs,
            tiled=True,
        )

    inputs = swap(tokens).astype(jnp.float32)
    dy = swap(cotangent)

    def whole(weight, first, second):
        return lax.all_gather(
            lax.all_gather(weight, first[0], axis=first[1], tiled=True),
            second[0],
            axis=second[1],
            tiled=True,
        )

    qkv_all = whole(w_qkv, ("dp", 0), ("mp", 2)).reshape(width, 3 * width)
    out_all = whole(w_out, ("dp", 1), ("mp", 0))
    up_all = whole(w_up, ("dp", 0), ("mp", 1))
    down_all = whole(w_down, ("dp", 1), ("mp", 0))
    table = lax.all_gather(half(adapters), ("dp", "mp"), axis=1, tiled=True)
    table = table.reshape(rank_all // RANK, RANK, full_width)
    clips = jnp.stack(
        [
            ((part * mine + i) * frames_micro + group_index * frames + member // span)
            // CLIP_FRAMES
            for i in range(mine)
        ]
    )
    chosen = clip_adapter[clips]
    own = table[chosen].reshape(mine * RANK, full_width)
    ends = [0, width, 4 * width, 5 * width, 6 * width, 7 * width]
    ends += [7 * width + hidden_width, 7 * width + 2 * hidden_width, full_width]
    a_qkv, b_qkv, a_out, b_out, a_up, b_up, a_down, b_down = [
        own[:, ends[i] : ends[i + 1]] for i in range(8)
    ]
    rows = mine * FRAME
    row_frame = lax.broadcasted_iota(jnp.int32, (rows, mine * RANK), 0) // FRAME
    column_frame = lax.broadcasted_iota(jnp.int32, (rows, mine * RANK), 1) // RANK
    mask = row_frame == column_frame

    def low(values):
        return half(jnp.where(mask, values, 0.0))

    shape_heads = (mine, FRAME, heads, HEAD)
    unit_one, inverse_one = norm_parts(inputs)
    normed_one = half(unit_one * gain_one)
    low_qkv = low(dot_t(normed_one, a_qkv))
    projected = half(dot(normed_one, qkv_all) + dot(low_qkv, b_qkv))
    queries = projected[:, 0:width].reshape(shape_heads)
    keys = projected[:, width : 2 * width].reshape(shape_heads)
    values = projected[:, 2 * width :].reshape(shape_heads)
    scores = jnp.einsum("fqhd,fkhd->fhqk", queries, keys, preferred_element_type=jnp.float32)
    scores = scores * scale
    exponent = jnp.exp(scores - jnp.max(scores, axis=-1, keepdims=True))
    soft = exponent / jnp.sum(exponent, axis=-1, keepdims=True)
    soft_half = half(soft)
    attended = half(
        jnp.einsum("fhqk,fkhd->fqhd", soft_half, values, preferred_element_type=jnp.float32)
    ).reshape(rows, width)
    low_out = low(dot_t(attended, a_out))
    middle = inputs + dot(attended, out_all) + dot(low_out, b_out)
    unit_two, inverse_two = norm_parts(middle)
    normed_two = half(unit_two * gain_two)
    low_up = low(dot_t(normed_two, a_up))
    hidden = dot(normed_two, up_all) + dot(low_up, b_up)
    phi = 0.5 * (1.0 + lax.erf(hidden * math.sqrt(0.5)))
    active = half(hidden * phi)
    slope = phi + hidden * jnp.exp(-0.5 * hidden * hidden) * (1.0 / math.sqrt(2.0 * math.pi))
    low_down = low(dot_t(active, a_down))
    outputs = half(middle + dot(active, down_all) + dot(low_down, b_down))

    through_down = low(dot_t(dy, b_down))
    d_active = dot_t(dy, down_all) + dot(through_down, a_down)
    d_hidden = half(d_active * slope)
    through_up = low(dot_t(d_hidden, b_up))
    d_normed_two = dot_t(d_hidden, up_all) + dot(through_up, a_up)
    d_middle = dy.astype(jnp.float32) + norm_back(unit_two, inverse_two, gain_two, d_normed_two)
    d_branch = half(d_middle)
    through_out = low(dot_t(d_branch, b_out))
    d_attended = half(dot_t(d_branch, out_all) + dot(through_out, a_out))
    d_heads = d_attended.reshape(shape_heads)
    d_values = jnp.einsum("fhqk,fqhd->fkhd", soft_half, d_heads, preferred_element_type=jnp.float32)
    d_soft = jnp.einsum("fqhd,fkhd->fhqk", d_heads, values, preferred_element_type=jnp.float32)
    inner = jnp.sum(soft * d_soft, axis=-1, keepdims=True)
    d_scores = half(soft * (d_soft - inner))
    d_queries = scale * jnp.einsum(
        "fhqk,fkhd->fqhd", d_scores, keys, preferred_element_type=jnp.float32
    )
    d_keys = scale * jnp.einsum(
        "fhqk,fqhd->fkhd", d_scores, queries, preferred_element_type=jnp.float32
    )
    d_projected = half(
        jnp.concatenate([d.reshape(rows, width) for d in (d_queries, d_keys, d_values)], axis=1)
    )
    through_qkv = low(dot_t(d_projected, b_qkv))
    d_normed_one = dot_t(d_projected, qkv_all) + dot(through_qkv, a_qkv)
    input_grad = half(d_middle + norm_back(unit_one, inverse_one, gain_one, d_normed_one))
    grads = half(jnp.concatenate(
        [
            t_dot(through_qkv, normed_one),
            t_dot(low_qkv, d_projected),
            t_dot(through_out, attended),
            t_dot(low_out, d_branch),
            t_dot(through_up, normed_two),
            t_dot(low_up, d_hidden),
            t_dot(through_down, active),
            t_dot(low_down, dy),
        ],
        axis=1,
    ))
    pick = (
        lax.broadcasted_iota(jnp.int32, (rank_all, mine * RANK), 0)
        == jnp.repeat(chosen, RANK)[None, :] * RANK
        + lax.broadcasted_iota(jnp.int32, (rank_all, mine * RANK), 1) % RANK
    ).astype(jnp.bfloat16)
    owner_grad = lax.psum_scatter(
        dot(pick, grads), ("dp", "mp"), scatter_dimension=1, tiled=True
    )
    return (swap_back(outputs), swap_back(input_grad)) + adam(
        owner_grad, adapters, moment_one, moment_two
    )


MESH = pl.DeviceIdType.MESH
X1, Y1, Y2, X2, C0, C1A, C1B, C2A, C2B = range(9)
HALF_PITCH = 104
HALF_SLOT = 112


def fused_kernel(
    tok_ref,
    cot_ref,
    g1_ref,
    g2_ref,
    wq_ref,
    wo_ref,
    wu_ref,
    wd_ref,
    table_ref,
    clip_ref,
    act_ref,
    ing_ref,
    gr_ref,
    w,
    ad,
    ts,
    cs,
    tr,
    cr,
    xf,
    dyb,
    n1,
    n2,
    proj,
    soft,
    att,
    mid,
    acc,
    dn,
    tmp,
    buf,
    dbr,
    dpj,
    lqh,
    thr,
    bq,
    ao,
    bu,
    an,
    g16,
    gc,
    gs,
    rb,
    osend,
    isend,
    own_act,
    own_ing,
    orecv,
    irecv,
    adp,
    smalls,
    zs,
    zr,
    azs,
    azr,
    ss,
    rs,
    ps,
    pr,
    cxs,
    cxr,
    us,
    ur,
):
    dp = lax.axis_index("dp")
    z = lax.axis_index("mp")
    y = dp // 4
    x = lax.rem(dp // 2, 2)
    c = lax.rem(dp, 2)
    h = lax.rem(z, 2)
    zp = z + 1 - 2 * h
    zn = 4
    shard_rows = tok_ref.shape[0]
    rows = xf.shape[0]
    frame_rows = rows // 2
    width = xf.shape[1]
    local = width // zn
    scale = 1.0 / math.sqrt(HEAD)

    def place(yy, xx, cc, zz):
        return ((yy * 2 + xx) * 2 + cc, zz)

    def order(at_z, k):
        upper = at_z // 2
        near = at_z + upper * (3 - 2 * at_z)
        swapped = jnp.where((near == 1) & (k < 2), 1 - k, k)
        return swapped + upper * (3 - 2 * swapped)

    def rank_of(at_z, block_z):
        upper = at_z // 2
        near = at_z + upper * (3 - 2 * at_z)
        mirrored = block_z + upper * (3 - 2 * block_z)
        return jnp.where((near == 1) & (mirrored < 2), 1 - mirrored, mirrored)

    barrier = pltpu.get_barrier_semaphore()
    for k in range(1, 16):
        yx = lax.rem(y * 2 + x + k // 4, 4)
        target = (yx * 2 + c, lax.rem(z + k % 4, 4))
        pl.semaphore_signal(barrier, inc=1, device_id=target, device_id_type=MESH)
    pl.semaphore_signal(barrier, inc=1, device_id=place(y, x, 1 - c, z), device_id_type=MESH)

    def remote(src, dst, send, recv, target):
        return pltpu.make_async_remote_copy(
            src_ref=src,
            dst_ref=dst,
            send_sem=send,
            recv_sem=recv,
            device_id=target,
            device_id_type=MESH,
        )

    w[z, 0, y, x, c] = jnp.concatenate([wo_ref[...].T] + [wq_ref[i] for i in range(3)], axis=1)
    span = table_ref.shape[1]
    low_columns = pl.ds(pl.multiple_of(lax.rem(z, 2) * span, 128), span)
    for m in range(4):
        clip = jnp.full((RANK, span), clip_ref[m])
        chosen = jnp.zeros((RANK, span), jnp.float32)
        for a in range(table_ref.shape[0] // RANK):
            chosen = jnp.where(clip == a, table_ref[a * RANK : (a + 1) * RANK], chosen)
        adp[m // 2, pl.ds((m % 2) * RANK, RANK)] = chosen.astype(jnp.bfloat16)
    ad[y, x, c, z // 2, :, low_columns] = adp[h]

    def stage(dst, src):
        for m in range(4):
            dst[m, pl.ds(96, 16)] = jnp.zeros((16, width), jnp.bfloat16)
            dst[m, pl.ds(0, shard_rows)] = src[:, m, :]

    def part(kind, zk, yy, xx, cc, first, count):
        return w.at[zk, kind, yy, xx, cc, pl.ds(first, count), :]

    def phase(q):
        if isinstance(q, int):
            return (0, q) if q < 4 else (1 + q % 2, (q - 4) // 2)
        return 1 + lax.rem(q, 2), (q - 4) // 2

    def move(q, what):
        full = 32 if q is None else 96
        n = full // 2
        every = pl.ds(0, 2)
        args, target = {
            X1: ((y, x, c, 0, n), (y, 1 - x, c)),
            Y1: ((y, x, c, n, n), (1 - y, x, c)),
            Y2: ((y, every, c, 0, n), (1 - y, x, c)),
            X2: ((every, x, c, n, n), (y, 1 - x, c)),
            C0: ((y, x, c, 0, full), (y, x, 1 - c)),
            C1A: ((y, 1 - x, c, 0, n), (y, x, 1 - c)),
            C1B: ((1 - y, x, c, n, n), (y, x, 1 - c)),
            C2A: ((1 - y, every, c, 0, n), (y, x, 1 - c)),
            C2B: ((every, 1 - x, c, n, n), (y, x, 1 - c)),
        }[what]
        if q is None:
            yy, xx, cc, first, count = args
            ref = ad.at[yy, xx, cc, :, pl.ds(first, count), :]
            index = 12
        else:
            kind, k = phase(q)
            ref = part(kind, order(z, k), *args)
            index = q
        return remote(ref, ref, ss.at[index, what], rs.at[index, what], place(*target, z))

    def z_move(q):
        kind, k = phase(q)
        ref = part(kind, z, y, x, c, 0, 96)
        other = order(z, k)
        return remote(ref, ref, zs.at[kind, k], zr.at[kind, rank_of(other, z)], (dp, other))

    def z_wait(q):
        kind, k = phase(q)
        ref = part(kind, z, y, x, c, 0, 96)
        remote(ref, ref, zs.at[kind, k], zr.at[kind, k], (dp, zp)).wait_recv()

    def ad_move(j):
        other = lax.rem(z + zn - j, zn)
        dst = ad.at[y, x, c, z // 2, :, low_columns]
        return remote(adp.at[lax.rem(other, 2)], dst, azs.at[j], azr.at[j], (dp, other))

    def t1(q):
        if isinstance(q, int):
            if q is not None and phase(q)[1]:
                z_wait(q)
        elif q is not None:
            z_wait(q)
        for what in (X1, Y1, C0):
            move(q, what).start()

    def t2(q):
        move(q, X1).wait_recv()
        move(q, Y2).start()
        move(q, Y1).wait_recv()
        move(q, X2).start()
        move(q, C1A).start()
        move(q, C1B).start()

    def t3(q):
        move(q, Y2).wait_recv()
        move(q, C2A).start()
        move(q, X2).wait_recv()
        move(q, C2B).start()

    def ready(q):
        for what in (C0, C1A, C1B, C2A, C2B):
            move(q, what).wait_recv()

    tok_move = remote(
        ts.at[pl.ds(2 - 2 * h, 2)], tr, ps.at[0], pr.at[0], (dp, zp)
    )
    cot_move = remote(
        cs.at[pl.ds(2 - 2 * h, 2)], cr, ps.at[1], pr.at[1], (dp, zp)
    )
    act_move = remote(
        osend, orecv, ps.at[2], pr.at[2], (dp, zp)
    )
    ing_moves = [
        remote(isend.at[f], irecv.at[f], ps.at[3 + f], pr.at[3 + f], (dp, zp)) for f in range(2)
    ]

    pl.semaphore_wait(barrier, 16)
    t1(0)
    for j in range(1, 4):
        ad_move(j).start()
    z_move(1).start()
    w[z, 1, y, x, c] = wu_ref[...]
    t1(4)
    stage(ts, tok_ref)
    tok_move.start()
    z_move(2).start()
    z_move(3).start()
    w[z, 2, y, x, c] = wd_ref[...]
    t2(0)
    t1(1)
    for j in range(1, 4):
        ad_move(j).wait_recv()
    t1(None)
    t2(1)
    t1(2)
    t2(None)
    t3(0)
    z_move(6).start()
    z_move(7).start()
    t2(2)
    t1(3)
    t3(1)
    t3(None)
    t2(3)
    t2(4)
    t3(2)
    z_move(8).start()
    z_move(9).start()
    stage(cs, cot_ref)
    cot_move.start()
    t1(5)
    t3(3)
    z_move(10).start()
    z_move(11).start()

    def dot(left, right):
        return jnp.dot(left, right, preferred_element_type=jnp.float32)

    def dot_t(left, right):
        return lax.dot_general(
            left, right, (((1,), (1,)), ((), ())), preferred_element_type=jnp.float32
        )

    def t_dot(left, right):
        return lax.dot_general(
            left, right, (((0,), (0,)), ((), ())), preferred_element_type=jnp.float32
        )

    row_frame = lax.broadcasted_iota(jnp.int32, (rows, 32), 0) // frame_rows
    column_frame = lax.broadcasted_iota(jnp.int32, (rows, 32), 1) // RANK
    mask = row_frame == column_frame

    def low(values):
        return jnp.where(mask, values, 0.0).astype(jnp.bfloat16)

    def tiles(body, step=416):
        @pl.loop(0, rows // step)
        def _(t):
            body(pl.ds(pl.multiple_of(t * step, step), step))

    def norm_parts(values):
        center = values - jnp.mean(values, axis=-1, keepdims=True)
        spread = jnp.mean(center * center, axis=-1, keepdims=True)
        inverse = lax.rsqrt(spread + norm_epsilon)
        return center * inverse, inverse

    def norm_back(values, gain, grad):
        unit, inverse = norm_parts(values)
        scaled = grad * gain
        first = jnp.mean(scaled, axis=-1, keepdims=True)
        second = jnp.mean(scaled * unit, axis=-1, keepdims=True)
        return inverse * (scaled - first - unit * second)

    def group(g):
        return ad[g // 8, (g // 4) % 2, (g // 2) % 2, g % 2]

    def group_ref(g):
        return g16.at[g // 8, (g // 4) % 2, (g // 2) % 2, g % 2]

    def attn_block(zk):
        return w[zk, 0].reshape(width, width)

    def halves(f):
        own = pl.ds(pl.multiple_of(f * frame_rows + h * HALF_PITCH, 8), HALF_PITCH)
        other = pl.ds(pl.multiple_of(f * frame_rows + (1 - h) * HALF_PITCH, 8), HALF_PITCH)
        return own, other

    def join(dst, own_slots, other_slots):
        for f in range(2):
            own, other = halves(f)
            dst[own] = own_slots[2 * h + f][:HALF_PITCH].astype(jnp.float32)
            dst[other] = other_slots[f][:HALF_PITCH].astype(jnp.float32)

    def give(dst, own, received):
        for f in range(2):
            first, second = own[f, pl.ds(0, shard_rows)], received[f, pl.ds(0, shard_rows)]
            dst[:, f, :] = jnp.where(h == 0, first, second)
            dst[:, 2 + f, :] = jnp.where(h == 0, second, first)

    tok_move.wait_recv()
    join(xf, ts, tr)

    def first_norm(at):
        values = xf[at]
        unit, _ = norm_parts(values)
        n1[at] = (unit * g1_ref[...].reshape(1, width)).astype(jnp.bfloat16)
        mid[at] = values

    tiles(first_norm)
    ready(None)
    for k in range(4):
        ready(k)
    for k in range(4):
        bq[k] = jnp.concatenate(
            [jnp.zeros((32, local), jnp.bfloat16)]
            + [group(1 + i)[:, k * local : (k + 1) * local] for i in range(3)],
            axis=1,
        )
        ao[k] = group(4)[:, k * local : (k + 1) * local]
        bu[k] = group(7 + k)
        an[k] = group(11 + k)
    low_wide = jnp.where(mask, dot_t(n1[...], group(0)), 0.0)
    smalls[0] = low_wide.astype(jnp.bfloat16)
    lqh[...] = jnp.zeros_like(lqh)
    for r in range(2):
        for f in range(2):
            first = f * frame_rows + r * HALF_PITCH
            lqh[r, pl.ds(f * HALF_SLOT, HALF_PITCH)] = low_wide[
                first : first + HALF_PITCH
            ].astype(jnp.bfloat16)
    key_pad = (
        lax.rem(lax.broadcasted_iota(jnp.int32, (frame_rows, 1), 0), HALF_PITCH) >= shard_rows
    )
    bias = jnp.where(key_pad, -1e30, 0.0).astype(jnp.float32)

    LOW_QKV, LOW_OUT, LOW_UP, LOW_DOWN, THR_DOWN, THR_UP, THR_OUT, THR_QKV = range(8)

    def attention(i, out_low):
        zk = order(z, i)
        block = attn_block(zk)
        proj[zk] = (dot(n1[...], block) + dot(smalls[LOW_QKV], bq[zk])).astype(jnp.bfloat16)
        for f in range(2):
            at = pl.ds(f * frame_rows, frame_rows)
            for head in range(3):
                first = local + head * HEAD
                q = proj[zk, at, first : first + HEAD]
                k = proj[zk, at, first + local : first + local + HEAD]
                v = proj[zk, at, first + 2 * local : first + 2 * local + HEAD]
                scores = dot_t(k, q) * scale + bias
                exponent = jnp.exp(scores - jnp.max(scores, axis=0, keepdims=True))
                weights = exponent / jnp.sum(exponent, axis=0, keepdims=True)
                weights = weights.astype(jnp.bfloat16)
                soft[zk, f * 3 + head] = weights
                att[zk, at, head * HEAD : (head + 1) * HEAD] = (
                    t_dot(weights, v).astype(jnp.bfloat16)
                )
        gathered = att[zk]
        mid[...] += dot_t(gathered, block[:, :local])
        return out_low + dot_t(gathered, ao[zk])

    def attention_step(i, out_low):
        @pl.when(i == 1)
        def _():
            t1(6)
            t2(5)

        @pl.when(i == 2)
        def _():
            t3(4)

        @pl.when(i == 3)
        def _():
            t1(7)
            t2(6)

        return attention(i, out_low)

    out_low = lax.fori_loop(0, 4, attention_step, jnp.zeros((rows, 32), jnp.float32))
    t3(5)
    ready(4)
    smalls[LOW_OUT] = low(out_low)
    mid[...] += dot(smalls[LOW_OUT], group(5))

    def second_norm(at):
        unit, _ = norm_parts(mid[at])
        n2[at] = (unit * g2_ref[...].reshape(1, width)).astype(jnp.bfloat16)

    tiles(second_norm)
    cot_move.wait_recv()
    join(tmp, cs, cr)
    dyb[...] = tmp[...].astype(jnp.bfloat16)
    smalls[LOW_UP] = low(dot_t(n2[...], group(6)))
    smalls[THR_DOWN] = low(dot_t(dyb[...], group(15)))
    group_ref(15)[...] = jnp.zeros((32, width), jnp.bfloat16)
    t1(8)
    t2(7)
    acc[...] = mid[...]
    dn[...] = jnp.zeros_like(dn)

    def feed(i, lows):
        down_low, up_back = lows
        zk = order(z, i)
        q = 4 + 2 * i

        @pl.when((i > 0) & (i < 3))
        def _():
            t1(q + 3)
            t2(q + 2)

        tmp[...] = dot(n2[...], w[zk, 1].reshape(width, width)) + dot(smalls[LOW_UP], bu[zk])

        def gate(at):
            hidden = tmp[at]
            phi = 0.5 + 0.5 * lax.erf(hidden * math.sqrt(0.5))
            bell = jnp.exp(-0.5 * hidden * hidden) * (1.0 / math.sqrt(2.0 * math.pi))
            buf[0, at] = (hidden * phi).astype(jnp.bfloat16)
            tmp[at] = phi + hidden * bell

        tiles(gate)
        active = buf[0]
        down_low = down_low + dot_t(active, an[zk])
        ga = 11 + zk
        g16[ga // 8, lax.rem(ga // 4, 2), lax.rem(ga // 2, 2), lax.rem(ga, 2)] = t_dot(
            smalls[THR_DOWN], active
        ).astype(jnp.bfloat16)

        @pl.when(i > 0)
        def _():
            t3(q + 1)

        @pl.when(i == 1)
        def _():
            t1(q + 4)

        @pl.when((i > 0) & (i < 3))
        def _():
            t2(q + 3)

        ready(q + 1)
        down = w[zk, 2].reshape(width, width)
        tmp[...] = tmp[...] * (dot(dyb[...], down) + dot(smalls[THR_DOWN], an[zk]))
        buf[1] = tmp[...].astype(jnp.bfloat16)
        d_hidden = buf[1]
        dn[...] += dot_t(d_hidden, w[zk, 1].reshape(width, width))
        acc[...] += dot_t(active, down)
        gu = 7 + zk
        g16[gu // 8, lax.rem(gu // 4, 2), lax.rem(gu // 2, 2), lax.rem(gu, 2)] = t_dot(
            smalls[LOW_UP], d_hidden
        ).astype(jnp.bfloat16)
        up_back = up_back + dot_t(d_hidden, bu[zk])

        @pl.when(i < 3)
        def _():
            t3(q + 2)
            ready(q + 2)

        return down_low, up_back

    empty = jnp.zeros((rows, 32), jnp.float32)
    down_low, up_back = lax.fori_loop(0, 4, feed, (empty, empty))
    smalls[LOW_DOWN] = low(down_low)
    smalls[THR_UP] = low(up_back)
    group_ref(15)[...] = t_dot(smalls[LOW_DOWN], dyb[...]).astype(jnp.bfloat16)

    def core_move(yx):
        src = g16.at[yx // 2, yx % 2, 1 - c]
        return remote(src, gc.at[yx], cxs.at[yx], cxr.at[yx], place(y, x, 1 - c, z))

    def owner_move(yx, zz):
        back_yx = lax.rem(y * 2 + x + 4 - yx, 4)
        back_z = lax.rem(z + 4 - zz, 4)
        slot = back_yx * 4 + back_z
        src = gs.at[yx, zz // 2, :, pl.ds((zz % 2) * span, span)]
        copy = remote(src, rb.at[slot], us.at[yx, zz], ur.at[slot], (yx * 2 + c, zz))
        return copy, slot

    def spread_out(yx):
        core_move(yx).wait_recv()
        for g in range(2):
            gs[yx, g] = (
                g16[yx // 2, yx % 2, c, g].astype(jnp.float32) + gc[yx, g].astype(jnp.float32)
            ).astype(jnp.bfloat16)
        for zz in range(4):
            copy, slot = owner_move(yx, zz)

            @pl.when(slot != 0)
            def _():
                copy.start()

            @pl.when(slot == 0)
            def _():
                rb[0] = gs[yx, zz // 2, :, pl.ds((zz % 2) * span, span)]

    core_move(3).start()
    core_move(2).start()

    group_ref(6)[...] = t_dot(smalls[THR_UP], n2[...]).astype(jnp.bfloat16)
    acc[...] += dot(smalls[LOW_DOWN], group(15))

    def second_back(at):
        grad = dn[at] + dot(smalls[THR_UP, at], group(6))
        value = dyb[at].astype(jnp.float32) + norm_back(
            mid[at], g2_ref[...].reshape(1, width), grad
        )
        dn[at] = value
        dbr[at] = value.astype(jnp.bfloat16)

    tiles(second_back)
    for f in range(2):
        own, other = halves(f)
        osend[f, pl.ds(0, HALF_PITCH)] = acc[other].astype(jnp.bfloat16)
    act_move.start()
    smalls[THR_OUT] = low(dot_t(dbr[...], group(5)))
    group_ref(5)[...] = t_dot(smalls[LOW_OUT], dbr[...]).astype(jnp.bfloat16)
    for r in range(2):
        for k in range(4):
            dpj[r, k, :, 0:local] = jnp.zeros((2 * HALF_SLOT, local), jnp.bfloat16)
            for f in range(2):
                dpj[r, k, pl.ds(f * HALF_SLOT + 96, 16)] = jnp.zeros((16, width), jnp.bfloat16)

    spread_out(3)
    spread_out(2)
    group_ref(4)[...] = jnp.concatenate(
        [t_dot(smalls[THR_OUT], att[k]).astype(jnp.bfloat16) for k in range(4)], axis=1
    )
    core_move(1).start()

    @pl.loop(0, 4)
    def _(zk):
        block = attn_block(zk)
        d_att = (dot(dbr[...], block[:, :local]) + dot(smalls[THR_OUT], ao[zk])).astype(
            jnp.bfloat16
        )
        buf[0, :, 0:local] = d_att

        @pl.when(zk == 1)
        def _():
            spread_out(1)

        for f in range(2):
            at = pl.ds(f * frame_rows, frame_rows)
            for head in range(3):
                first = local + head * HEAD
                q = proj[zk, at, first : first + HEAD]
                k = proj[zk, at, first + local : first + local + HEAD]
                v = proj[zk, at, first + 2 * local : first + 2 * local + HEAD]
                d_out = buf[0, at, head * HEAD : (head + 1) * HEAD]
                weights = soft[zk, f * 3 + head]
                d_values = dot(weights, d_out)
                d_soft = dot_t(v, d_out)
                wide = weights.astype(jnp.float32)
                inner = jnp.sum(wide * d_soft, axis=0, keepdims=True)
                d_scores = (wide * (d_soft - inner)).astype(jnp.bfloat16)
                d_keys = dot(d_scores, q) * scale
                d_queries = t_dot(k, d_scores).T * scale
                for r in range(2):
                    to = pl.ds(f * HALF_SLOT, HALF_PITCH)
                    cut = slice(r * HALF_PITCH, (r + 1) * HALF_PITCH)
                    dpj[r, zk, to, first : first + HEAD] = d_queries[cut].astype(jnp.bfloat16)
                    dpj[r, zk, to, first + local : first + local + HEAD] = d_keys[cut].astype(
                        jnp.bfloat16
                    )
                    dpj[r, zk, to, first + 2 * local : first + 2 * local + HEAD] = d_values[
                        cut
                    ].astype(jnp.bfloat16)

    half_rows = 2 * HALF_SLOT
    half_mask = (
        lax.broadcasted_iota(jnp.int32, (half_rows, 32), 0) // HALF_SLOT
        == lax.broadcasted_iota(jnp.int32, (half_rows, 32), 1) // RANK
    )

    def half_at(f, r):
        return pl.ds(pl.multiple_of(f * frame_rows + r * HALF_PITCH, 8), HALF_PITCH)

    def half_products(r):
        grad = dot_t(dpj[r, 0], attn_block(0))
        back = dot_t(dpj[r, 0], bq[0])
        for k in range(1, 4):
            grad = grad + dot_t(dpj[r, k], attn_block(k))
            back = back + dot_t(dpj[r, k], bq[k])
        back = jnp.where(half_mask, back, 0.0)
        for f in range(2):
            thr[half_at(f, r)] = back[f * HALF_SLOT : f * HALF_SLOT + HALF_PITCH]
        tmp[0:half_rows] = grad + dot(back.astype(jnp.bfloat16), group(0))

    def half_back(f, r):
        at = half_at(f, r)
        grad = tmp[f * HALF_SLOT : f * HALF_SLOT + HALF_PITCH]
        value = dn[at] + norm_back(xf[at], g1_ref[...].reshape(1, width), grad)
        return value.astype(jnp.bfloat16)

    half_products(1 - h)
    isend[0, pl.ds(0, HALF_PITCH)] = half_back(0, 1 - h)
    ing_moves[0].start()
    isend[1, pl.ds(0, HALF_PITCH)] = half_back(1, 1 - h)
    half_products(h)
    smalls[THR_QKV] = thr[...].astype(jnp.bfloat16)
    group_ref(0)[...] = t_dot(smalls[THR_QKV], n1[...]).astype(jnp.bfloat16)
    parts = [
        (t_dot(lqh[0], dpj[0, k]) + t_dot(lqh[1], dpj[1, k])).astype(jnp.bfloat16)
        for k in range(4)
    ]
    for i in range(3):
        first = (1 + i) * local
        group_ref(1 + i)[...] = jnp.concatenate(
            [parts[k][:, first : first + local] for k in range(4)], axis=1
        )
    core_move(0).start()
    spread_out(0)
    ing_moves[1].start()
    own_ing[0] = half_back(0, h)
    own_ing[1] = half_back(1, h)

    for f in range(2):
        own_act[f] = acc[halves(f)[0]].astype(jnp.bfloat16)
    act_move.wait_recv()
    give(act_ref, own_act, orecv)

    for slot in range(1, 16):
        remote(rb.at[slot], rb.at[slot], us.at[0, 0], ur.at[slot], (dp, zp)).wait_recv()
    for parity in range(2):
        total = jnp.zeros((32, span), jnp.float32)
        for slot in range(16):
            if slot % 2 == parity:
                total = total + rb[slot].astype(jnp.float32)
        first = lax.rem(h + parity, 2)
        for a in range(table_ref.shape[0] // RANK):
            chosen = [
                jnp.where(
                    jnp.full((RANK, span), clip_ref[2 * first + i]) == a,
                    total[i * RANK : (i + 1) * RANK],
                    0.0,
                )
                for i in range(2)
            ]
            gr_ref[first, pl.ds(a * RANK, RANK)] = chosen[0] + chosen[1]
    for yx in range(4):
        core_move(yx).wait_send()
        for zz in range(4):
            copy, slot = owner_move(yx, zz)

            @pl.when(slot != 0)
            def _():
                copy.wait_send()

    tok_move.wait_send()
    cot_move.wait_send()
    for j in range(1, 4):
        ad_move(j).wait_send()

    for q in (1, 2, 3, 6, 7, 8, 9, 10, 11):
        z_move(q).wait_send()
    for q in range(4):
        for what in range(9):
            move(q, what).wait_send()

    @pl.loop(4, 12)
    def _(q):
        for what in range(9):
            move(q, what).wait_send()

    for what in range(9):
        move(None, what).wait_send()
    act_move.wait_send()
    for f in range(2):
        ing_moves[f].wait()
    give(ing_ref, own_ing, irecv)


def finish_kernel(
    act_ref, ing_ref, gr_ref, table_ref, one_ref, two_ref, act_out, ing_out, *outs
):
    act_out[...] = act_ref[...]
    ing_out[...] = ing_ref[...]
    results = adam(gr_ref[0] + gr_ref[1], table_ref[...], one_ref[...], two_ref[...])
    for out, result in zip(outs, results):
        out[...] = result


def fused(
    tokens,
    cotangent,
    clip_adapter,
    gain_one,
    gain_two,
    w_qkv,
    w_out,
    w_up,
    w_down,
    adapters,
    moment_one,
    moment_two,
):
    micro_count, shard_rows, width = tokens.shape
    rank_all, span = adapters.shape
    rows = 4 * HALF_PITCH
    frame_rows = 2 * HALF_PITCH
    local = width // 4
    bf, f32 = jnp.bfloat16, jnp.float32
    vmem = pl.BlockSpec(memory_space=pltpu.VMEM)
    smem = pl.BlockSpec(memory_space=pltpu.SMEM)
    scratch = [
        pltpu.VMEM((4, 3, 2, 2, 2, 96, width), bf),
        pltpu.VMEM((2, 2, 2, 2, 32, width), bf),
        pltpu.VMEM((4, HALF_SLOT, width), bf),
        pltpu.VMEM((4, HALF_SLOT, width), bf),
        pltpu.VMEM((2, HALF_SLOT, width), bf),
        pltpu.VMEM((2, HALF_SLOT, width), bf),
        pltpu.VMEM((rows, width), f32),
        pltpu.VMEM((rows, width), bf),
        pltpu.VMEM((rows, width), bf),
        pltpu.VMEM((rows, width), bf),
        pltpu.VMEM((4, rows, width), bf),
        pltpu.VMEM((4, 6, frame_rows, frame_rows), bf),
        pltpu.VMEM((4, rows, local), bf),
        pltpu.VMEM((rows, width), f32),
        pltpu.VMEM((rows, width), f32),
        pltpu.VMEM((rows, width), f32),
        pltpu.VMEM((rows, width), f32),
        pltpu.VMEM((2, rows, width), bf),
        pltpu.VMEM((rows, width), bf),
        pltpu.VMEM((2, 4, 2 * HALF_SLOT, width), bf),
        pltpu.VMEM((2, 2 * HALF_SLOT, 32), bf),
        pltpu.VMEM((rows, 32), f32),
        pltpu.VMEM((4, 32, width), bf),
        pltpu.VMEM((4, 32, local), bf),
        pltpu.VMEM((4, 32, width), bf),
        pltpu.VMEM((4, 32, width), bf),
        pltpu.VMEM((2, 2, 2, 2, 32, width), bf),
        pltpu.VMEM((4, 2, 32, width), bf),
        pltpu.VMEM((4, 2, 32, width), bf),
        pltpu.VMEM((16, 32, span), bf),
        pltpu.VMEM((2, HALF_SLOT, width), bf),
        pltpu.VMEM((2, HALF_SLOT, width), bf),
        pltpu.VMEM((2, HALF_PITCH, width), bf),
        pltpu.VMEM((2, HALF_PITCH, width), bf),
        pltpu.VMEM((2, HALF_SLOT, width), bf),
        pltpu.VMEM((2, HALF_SLOT, width), bf),
        pltpu.VMEM((2, 32, span), bf),
        pltpu.VMEM((8, rows, 32), bf),
        pltpu.SemaphoreType.DMA((3, 4)),
        pltpu.SemaphoreType.DMA((3, 4)),
        pltpu.SemaphoreType.DMA((4,)),
        pltpu.SemaphoreType.DMA((4,)),
        pltpu.SemaphoreType.DMA((13, 9)),
        pltpu.SemaphoreType.DMA((13, 9)),
        pltpu.SemaphoreType.DMA((5,)),
        pltpu.SemaphoreType.DMA((5,)),
        pltpu.SemaphoreType.DMA((4,)),
        pltpu.SemaphoreType.DMA((4,)),
        pltpu.SemaphoreType.DMA((4, 4)),
        pltpu.SemaphoreType.DMA((16,)),
    ]
    act, ing, grads = pl.pallas_call(
        fused_kernel,
        out_shape=(
            jax.ShapeDtypeStruct((shard_rows, micro_count, width), bf),
            jax.ShapeDtypeStruct((shard_rows, micro_count, width), bf),
            jax.ShapeDtypeStruct((2, rank_all, span), f32),
        ),
        in_specs=[vmem] * 9 + [smem],
        out_specs=(vmem, vmem, vmem),
        scratch_shapes=scratch,
        compiler_params=pltpu.CompilerParams(
            collective_id=0, has_side_effects=True, vmem_limit_bytes=60 * 2**20
        ),
    )(
        tokens.transpose(1, 0, 2),
        cotangent.transpose(1, 0, 2),
        gain_one,
        gain_two,
        w_qkv.transpose(1, 0, 2),
        w_out,
        w_up,
        w_down.T,
        adapters,
        clip_adapter,
    )
    plain = jax.ShapeDtypeStruct((rank_all, span), f32)
    rows_spec = pl.BlockSpec((shard_rows // 2, micro_count, width), lambda i: (i, 0, 0))
    plain_spec = pl.BlockSpec((rank_all // 2, span), lambda i: (i, 0))
    act, ing, *others = pl.pallas_call(
        finish_kernel,
        out_shape=(act, ing) + (plain,) * 4 + (jax.ShapeDtypeStruct((rank_all, span), bf),),
        grid=(2,),
        in_specs=[rows_spec] * 2
        + [pl.BlockSpec((2, rank_all // 2, span), lambda i: (0, i, 0))]
        + [plain_spec] * 3,
        out_specs=(rows_spec,) * 2 + (plain_spec,) * 5,
    )(act, ing, grads, adapters, moment_one, moment_two)
    return (act.transpose(1, 0, 2), ing.transpose(1, 0, 2), *others)


def layer(tokens, *others):
    w_up = others[6]
    sizes = lax.axis_size("dp"), lax.axis_size("mp")
    frames_micro = tokens.shape[1] * sizes[0] * sizes[1] // FRAME
    fits = (
        sizes == (8, 4)
        and tokens.shape[0] == 4
        and 2 * tokens.shape[1] == FRAME
        and frames_micro == CLIP_FRAMES
        and w_up.shape == (tokens.shape[2] // 8, tokens.shape[2])
    )
    return (fused if fits else shards)(tokens, *others)


def solution(mesh):
    spread = P(None, ("dp", "mp"))
    rows = P(None, ("dp", "mp"), None)
    return jax.shard_map(
        layer,
        mesh=mesh,
        in_specs=(
            rows,
            rows,
            P(),
            P(),
            P(),
            P("dp", None, "mp"),
            P("mp", "dp"),
            P("dp", "mp"),
            P("mp", "dp"),
            spread,
            spread,
            spread,
        ),
        out_specs=(rows, rows, spread, spread, spread, spread, spread),
        check_vma=False,
    )
```

```python
import functools
import math

import jax
import jax.numpy as jnp
from jax import lax
from jax.experimental import pallas as pl
from jax.experimental.pallas import tpu as pltpu
from jax.sharding import PartitionSpec as P

HEAD = 64
FRAME = 196
RANK = 16
CLIP_FRAMES = 16
STEP = 5

norm_epsilon = 1e-06
beta_first = 0.5
beta_second = 0.5
learn_rate = 0.05
weight_decay = 0.01
adam_epsilon = 1e-08


def dot(left, right):
    return jnp.dot(left, right, preferred_element_type=jnp.float32)


def dot_t(left, right):
    return lax.dot_general(left, right, (((1,), (1,)), ((), ())), preferred_element_type=jnp.float32)


def t_dot(left, right):
    return lax.dot_general(left, right, (((0,), (0,)), ((), ())), preferred_element_type=jnp.float32)


def half(values):
    return values.astype(jnp.bfloat16)


def norm_parts(values):
    center = values - jnp.mean(values, axis=-1, keepdims=True)
    spread = jnp.mean(center * center, axis=-1, keepdims=True)
    inverse = lax.rsqrt(spread + norm_epsilon)
    return center * inverse, inverse


def norm_back(unit, inverse, gain, grad):
    scaled = grad * gain
    first = jnp.mean(scaled, axis=-1, keepdims=True)
    second = jnp.mean(scaled * unit, axis=-1, keepdims=True)
    return inverse * (scaled - first - unit * second)


def adam(owner_grad, adapters, moment_one, moment_two):
    first_moment = beta_first * moment_one + (1.0 - beta_first) * owner_grad
    second_moment = beta_second * moment_two + (1.0 - beta_second) * owner_grad * owner_grad
    first_hat = first_moment / (1.0 - beta_first**STEP)
    second_hat = second_moment / (1.0 - beta_second**STEP)
    updated = adapters - learn_rate * (
        first_hat / (jnp.sqrt(second_hat) + adam_epsilon) + weight_decay * adapters
    )
    return (
        owner_grad,
        updated,
        first_moment,
        second_moment,
        updated.astype(jnp.bfloat16),
    )


def shards(
    tokens,
    cotangent,
    clip_adapter,
    gain_one,
    gain_two,
    w_qkv,
    w_out,
    w_up,
    w_down,
    adapters,
    moment_one,
    moment_two,
):
    groups = lax.axis_size("mp")
    member = lax.axis_index("mp")
    group_index = lax.axis_index("dp")
    micro_count, shard_rows, width = tokens.shape
    hidden_width = w_up.shape[1] * groups
    heads = width // HEAD
    rank_all = adapters.shape[0]
    full_width = adapters.shape[1] * lax.axis_size(("dp", "mp"))
    frames = shard_rows * groups // FRAME
    frames_micro = frames * lax.axis_size("dp")
    scale = 1.0 / math.sqrt(HEAD)
    span = FRAME // shard_rows
    mine = micro_count // span
    part = member % span
    pairs = [[first * span + k for k in range(span)] for first in range(groups // span)]

    def swap(rows):
        return lax.all_to_all(
            rows, "mp", split_axis=0, concat_axis=1, axis_index_groups=pairs, tiled=True
        ).reshape(mine * FRAME, width)

    def swap_back(rows):
        return lax.all_to_all(
            rows.reshape(mine, FRAME, width),
            "mp",
            split_axis=1,
            concat_axis=0,
            axis_index_groups=pairs,
            tiled=True,
        )

    inputs = swap(tokens).astype(jnp.float32)
    dy = swap(cotangent)

    def whole(weight, first, second):
        return lax.all_gather(
            lax.all_gather(weight, first[0], axis=first[1], tiled=True),
            second[0],
            axis=second[1],
            tiled=True,
        )

    qkv_all = whole(w_qkv, ("dp", 0), ("mp", 2)).reshape(width, 3 * width)
    out_all = whole(w_out, ("dp", 1), ("mp", 0))
    up_all = whole(w_up, ("dp", 0), ("mp", 1))
    down_all = whole(w_down, ("dp", 1), ("mp", 0))
    table = lax.all_gather(half(adapters), ("dp", "mp"), axis=1, tiled=True)
    table = table.reshape(rank_all // RANK, RANK, full_width)
    clips = jnp.stack(
        [
            ((part * mine + i) * frames_micro + group_index * frames + member // span)
            // CLIP_FRAMES
            for i in range(mine)
        ]
    )
    chosen = clip_adapter[clips]
    own = table[chosen].reshape(mine * RANK, full_width)
    ends = [0, width, 4 * width, 5 * width, 6 * width, 7 * width]
    ends += [7 * width + hidden_width, 7 * width + 2 * hidden_width, full_width]
    a_qkv, b_qkv, a_out, b_out, a_up, b_up, a_down, b_down = [
        own[:, ends[i] : ends[i + 1]] for i in range(8)
    ]
    rows = mine * FRAME
    row_frame = lax.broadcasted_iota(jnp.int32, (rows, mine * RANK), 0) // FRAME
    column_frame = lax.broadcasted_iota(jnp.int32, (rows, mine * RANK), 1) // RANK
    mask = row_frame == column_frame

    def low(values):
        return half(jnp.where(mask, values, 0.0))

    shape_heads = (mine, FRAME, heads, HEAD)
    unit_one, inverse_one = norm_parts(inputs)
    normed_one = half(unit_one * gain_one)
    low_qkv = low(dot_t(normed_one, a_qkv))
    projected = half(dot(normed_one, qkv_all) + dot(low_qkv, b_qkv))
    queries = projected[:, 0:width].reshape(shape_heads)
    keys = projected[:, width : 2 * width].reshape(shape_heads)
    values = projected[:, 2 * width :].reshape(shape_heads)
    scores = jnp.einsum("fqhd,fkhd->fhqk", queries, keys, preferred_element_type=jnp.float32)
    scores = scores * scale
    exponent = jnp.exp(scores - jnp.max(scores, axis=-1, keepdims=True))
    soft = exponent / jnp.sum(exponent, axis=-1, keepdims=True)
    soft_half = half(soft)
    attended = half(
        jnp.einsum("fhqk,fkhd->fqhd", soft_half, values, preferred_element_type=jnp.float32)
    ).reshape(rows, width)
    low_out = low(dot_t(attended, a_out))
    middle = inputs + dot(attended, out_all) + dot(low_out, b_out)
    unit_two, inverse_two = norm_parts(middle)
    normed_two = half(unit_two * gain_two)
    low_up = low(dot_t(normed_two, a_up))
    hidden = dot(normed_two, up_all) + dot(low_up, b_up)
    phi = 0.5 * (1.0 + lax.erf(hidden * math.sqrt(0.5)))
    active = half(hidden * phi)
    slope = phi + hidden * jnp.exp(-0.5 * hidden * hidden) * (1.0 / math.sqrt(2.0 * math.pi))
    low_down = low(dot_t(active, a_down))
    outputs = half(middle + dot(active, down_all) + dot(low_down, b_down))

    through_down = low(dot_t(dy, b_down))
    d_active = dot_t(dy, down_all) + dot(through_down, a_down)
    d_hidden = half(d_active * slope)
    through_up = low(dot_t(d_hidden, b_up))
    d_normed_two = dot_t(d_hidden, up_all) + dot(through_up, a_up)
    d_middle = dy.astype(jnp.float32) + norm_back(unit_two, inverse_two, gain_two, d_normed_two)
    d_branch = half(d_middle)
    through_out = low(dot_t(d_branch, b_out))
    d_attended = half(dot_t(d_branch, out_all) + dot(through_out, a_out))
    d_heads = d_attended.reshape(shape_heads)
    d_values = jnp.einsum("fhqk,fqhd->fkhd", soft_half, d_heads, preferred_element_type=jnp.float32)
    d_soft = jnp.einsum("fqhd,fkhd->fhqk", d_heads, values, preferred_element_type=jnp.float32)
    inner = jnp.sum(soft * d_soft, axis=-1, keepdims=True)
    d_scores = half(soft * (d_soft - inner))
    d_queries = scale * jnp.einsum(
        "fhqk,fkhd->fqhd", d_scores, keys, preferred_element_type=jnp.float32
    )
    d_keys = scale * jnp.einsum(
        "fhqk,fqhd->fkhd", d_scores, queries, preferred_element_type=jnp.float32
    )
    d_projected = half(
        jnp.concatenate([d.reshape(rows, width) for d in (d_queries, d_keys, d_values)], axis=1)
    )
    through_qkv = low(dot_t(d_projected, b_qkv))
    d_normed_one = dot_t(d_projected, qkv_all) + dot(through_qkv, a_qkv)
    input_grad = half(d_middle + norm_back(unit_one, inverse_one, gain_one, d_normed_one))
    grads = half(jnp.concatenate(
        [
            t_dot(through_qkv, normed_one),
            t_dot(low_qkv, d_projected),
            t_dot(through_out, attended),
            t_dot(low_out, d_branch),
            t_dot(through_up, normed_two),
            t_dot(low_up, d_hidden),
            t_dot(through_down, active),
            t_dot(low_down, dy),
        ],
        axis=1,
    ))
    pick = (
        lax.broadcasted_iota(jnp.int32, (rank_all, mine * RANK), 0)
        == jnp.repeat(chosen, RANK)[None, :] * RANK
        + lax.broadcasted_iota(jnp.int32, (rank_all, mine * RANK), 1) % RANK
    ).astype(jnp.bfloat16)
    owner_grad = lax.psum_scatter(
        dot(pick, grads), ("dp", "mp"), scatter_dimension=1, tiled=True
    )
    return (swap_back(outputs), swap_back(input_grad)) + adam(
        owner_grad, adapters, moment_one, moment_two
    )


MESH = pl.DeviceIdType.MESH
X1, Y1, Y2, X2, C0, C1A, C1B, C2A, C2B = range(9)
HALF_PITCH = 104
HALF_SLOT = 112


def fused_kernel(
    tok_ref,
    cot_ref,
    g1_ref,
    g2_ref,
    wq_ref,
    wo_ref,
    wu_ref,
    wd_ref,
    table_ref,
    clip_ref,
    act_ref,
    ing_ref,
    gr_ref,
    w,
    ad,
    ts,
    cs,
    tr,
    cr,
    xf,
    dyb,
    n1,
    n2,
    proj,
    soft,
    att,
    mid,
    acc,
    dn,
    tmp,
    buf,
    dbr,
    dpj,
    lqh,
    thr,
    bq,
    ao,
    bu,
    an,
    g16,
    gc,
    gs,
    rb,
    osend,
    isend,
    own_act,
    own_ing,
    orecv,
    irecv,
    adp,
    smalls,
    zs,
    zr,
    azs,
    azr,
    ss,
    rs,
    ps,
    pr,
    cxs,
    cxr,
    us,
    ur,
):
    dp = lax.axis_index("dp")
    z = lax.axis_index("mp")
    y = dp // 4
    x = lax.rem(dp // 2, 2)
    c = lax.rem(dp, 2)
    h = lax.rem(z, 2)
    zp = z + 1 - 2 * h
    zn = 4
    shard_rows = tok_ref.shape[0]
    rows = xf.shape[0]
    frame_rows = rows // 2
    width = xf.shape[1]
    local = width // zn
    scale = 1.0 / math.sqrt(HEAD)

    def place(yy, xx, cc, zz):
        return ((yy * 2 + xx) * 2 + cc, zz)

    def order(at_z, k):
        upper = at_z // 2
        near = at_z + upper * (3 - 2 * at_z)
        swapped = jnp.where((near == 1) & (k < 2), 1 - k, k)
        return swapped + upper * (3 - 2 * swapped)

    def rank_of(at_z, block_z):
        upper = at_z // 2
        near = at_z + upper * (3 - 2 * at_z)
        mirrored = block_z + upper * (3 - 2 * block_z)
        return jnp.where((near == 1) & (mirrored < 2), 1 - mirrored, mirrored)

    barrier = pltpu.get_barrier_semaphore()
    for k in range(1, 16):
        yx = lax.rem(y * 2 + x + k // 4, 4)
        target = (yx * 2 + c, lax.rem(z + k % 4, 4))
        pl.semaphore_signal(barrier, inc=1, device_id=target, device_id_type=MESH)
    pl.semaphore_signal(barrier, inc=1, device_id=place(y, x, 1 - c, z), device_id_type=MESH)

    def remote(src, dst, send, recv, target):
        return pltpu.make_async_remote_copy(
            src_ref=src,
            dst_ref=dst,
            send_sem=send,
            recv_sem=recv,
            device_id=target,
            device_id_type=MESH,
        )

    w[z, 0, y, x, c] = jnp.concatenate([wo_ref[...].T] + [wq_ref[i] for i in range(3)], axis=1)
    span = table_ref.shape[1]
    low_columns = pl.ds(pl.multiple_of(lax.rem(z, 2) * span, 128), span)
    for m in range(4):
        clip = jnp.full((RANK, span), clip_ref[m])
        chosen = jnp.zeros((RANK, span), jnp.float32)
        for a in range(table_ref.shape[0] // RANK):
            chosen = jnp.where(clip == a, table_ref[a * RANK : (a + 1) * RANK], chosen)
        adp[m // 2, pl.ds((m % 2) * RANK, RANK)] = chosen.astype(jnp.bfloat16)
    ad[y, x, c, z // 2, :, low_columns] = adp[h]

    def stage(dst, src):
        for m in range(4):
            dst[m, pl.ds(96, 16)] = jnp.zeros((16, width), jnp.bfloat16)
            dst[m, pl.ds(0, shard_rows)] = src[:, m, :]

    def part(kind, zk, yy, xx, cc, first, count):
        return w.at[zk, kind, yy, xx, cc, pl.ds(first, count), :]

    def phase(q):
        if isinstance(q, int):
            return (0, q) if q < 4 else (1 + q % 2, (q - 4) // 2)
        return 1 + lax.rem(q, 2), (q - 4) // 2

    def move(q, what):
        full = 32 if q is None else 96
        n = full // 2
        every = pl.ds(0, 2)
        args, target = {
            X1: ((y, x, c, 0, n), (y, 1 - x, c)),
            Y1: ((y, x, c, n, n), (1 - y, x, c)),
            Y2: ((y, every, c, 0, n), (1 - y, x, c)),
            X2: ((every, x, c, n, n), (y, 1 - x, c)),
            C0: ((y, x, c, 0, full), (y, x, 1 - c)),
            C1A: ((y, 1 - x, c, 0, n), (y, x, 1 - c)),
            C1B: ((1 - y, x, c, n, n), (y, x, 1 - c)),
            C2A: ((1 - y, every, c, 0, n), (y, x, 1 - c)),
            C2B: ((every, 1 - x, c, n, n), (y, x, 1 - c)),
        }[what]
        if q is None:
            yy, xx, cc, first, count = args
            ref = ad.at[yy, xx, cc, :, pl.ds(first, count), :]
            index = 12
        else:
            kind, k = phase(q)
            ref = part(kind, order(z, k), *args)
            index = q
        return remote(ref, ref, ss.at[index, what], rs.at[index, what], place(*target, z))

    def z_move(q):
        kind, k = phase(q)
        ref = part(kind, z, y, x, c, 0, 96)
        other = order(z, k)
        return remote(ref, ref, zs.at[kind, k], zr.at[kind, rank_of(other, z)], (dp, other))

    def z_wait(q):
        kind, k = phase(q)
        ref = part(kind, z, y, x, c, 0, 96)
        remote(ref, ref, zs.at[kind, k], zr.at[kind, k], (dp, zp)).wait_recv()

    def ad_move(j):
        other = lax.rem(z + zn - j, zn)
        dst = ad.at[y, x, c, z // 2, :, low_columns]
        return remote(adp.at[lax.rem(other, 2)], dst, azs.at[j], azr.at[j], (dp, other))

    def t1(q):
        if isinstance(q, int):
            if q is not None and phase(q)[1]:
                z_wait(q)
        elif q is not None:
            z_wait(q)
        for what in (X1, Y1, C0):
            move(q, what).start()

    def t2(q):
        move(q, X1).wait_recv()
        move(q, Y2).start()
        move(q, Y1).wait_recv()
        move(q, X2).start()
        move(q, C1A).start()
        move(q, C1B).start()

    def t3(q):
        move(q, Y2).wait_recv()
        move(q, C2A).start()
        move(q, X2).wait_recv()
        move(q, C2B).start()

    def ready(q):
        for what in (C0, C1A, C1B, C2A, C2B):
            move(q, what).wait_recv()

    tok_move = remote(
        ts.at[pl.ds(2 - 2 * h, 2)], tr, ps.at[0], pr.at[0], (dp, zp)
    )
    cot_move = remote(
        cs.at[pl.ds(2 - 2 * h, 2)], cr, ps.at[1], pr.at[1], (dp, zp)
    )
    act_move = remote(
        osend, orecv, ps.at[2], pr.at[2], (dp, zp)
    )
    ing_moves = [
        remote(isend.at[f], irecv.at[f], ps.at[3 + f], pr.at[3 + f], (dp, zp)) for f in range(2)
    ]

    pl.semaphore_wait(barrier, 16)
    t1(0)
    for j in range(1, 4):
        ad_move(j).start()
    z_move(1).start()
    w[z, 1, y, x, c] = wu_ref[...]
    t1(4)
    stage(ts, tok_ref)
    tok_move.start()
    z_move(2).start()
    z_move(3).start()
    w[z, 2, y, x, c] = wd_ref[...]
    t2(0)
    t1(1)
    for j in range(1, 4):
        ad_move(j).wait_recv()
    t1(None)
    t2(1)
    t1(2)
    t2(None)
    t3(0)
    z_move(6).start()
    z_move(7).start()
    t2(2)
    t1(3)
    t3(1)
    t3(None)
    t2(3)
    t2(4)
    t3(2)
    z_move(8).start()
    z_move(9).start()
    stage(cs, cot_ref)
    cot_move.start()
    t1(5)
    t3(3)
    z_move(10).start()
    z_move(11).start()

    def dot(left, right):
        return jnp.dot(left, right, preferred_element_type=jnp.float32)

    def dot_t(left, right):
        return lax.dot_general(
            left, right, (((1,), (1,)), ((), ())), preferred_element_type=jnp.float32
        )

    def t_dot(left, right):
        return lax.dot_general(
            left, right, (((0,), (0,)), ((), ())), preferred_element_type=jnp.float32
        )

    row_frame = lax.broadcasted_iota(jnp.int32, (rows, 32), 0) // frame_rows
    column_frame = lax.broadcasted_iota(jnp.int32, (rows, 32), 1) // RANK
    mask = row_frame == column_frame

    def low(values):
        return jnp.where(mask, values, 0.0).astype(jnp.bfloat16)

    def tiles(body, step=416):
        @pl.loop(0, rows // step)
        def _(t):
            body(pl.ds(pl.multiple_of(t * step, step), step))

    def norm_parts(values):
        center = values - jnp.mean(values, axis=-1, keepdims=True)
        spread = jnp.mean(center * center, axis=-1, keepdims=True)
        inverse = lax.rsqrt(spread + norm_epsilon)
        return center * inverse, inverse

    def norm_back(values, gain, grad):
        unit, inverse = norm_parts(values)
        scaled = grad * gain
        first = jnp.mean(scaled, axis=-1, keepdims=True)
        second = jnp.mean(scaled * unit, axis=-1, keepdims=True)
        return inverse * (scaled - first - unit * second)

    def group(g):
        return ad[g // 8, (g // 4) % 2, (g // 2) % 2, g % 2]

    def group_ref(g):
        return g16.at[g // 8, (g // 4) % 2, (g // 2) % 2, g % 2]

    def attn_block(zk):
        return w[zk, 0].reshape(width, width)

    def halves(f):
        own = pl.ds(pl.multiple_of(f * frame_rows + h * HALF_PITCH, 8), HALF_PITCH)
        other = pl.ds(pl.multiple_of(f * frame_rows + (1 - h) * HALF_PITCH, 8), HALF_PITCH)
        return own, other

    def join(dst, own_slots, other_slots):
        for f in range(2):
            own, other = halves(f)
            dst[own] = own_slots[2 * h + f][:HALF_PITCH].astype(jnp.float32)
            dst[other] = other_slots[f][:HALF_PITCH].astype(jnp.float32)

    def give(dst, own, received):
        for f in range(2):
            first, second = own[f, pl.ds(0, shard_rows)], received[f, pl.ds(0, shard_rows)]
            dst[:, f, :] = jnp.where(h == 0, first, second)
            dst[:, 2 + f, :] = jnp.where(h == 0, second, first)

    tok_move.wait_recv()
    join(xf, ts, tr)

    def first_norm(at):
        values = xf[at]
        unit, _ = norm_parts(values)
        n1[at] = (unit * g1_ref[...].reshape(1, width)).astype(jnp.bfloat16)
        mid[at] = values

    tiles(first_norm)
    ready(None)
    for k in range(4):
        ready(k)
    for k in range(4):
        bq[k] = jnp.concatenate(
            [jnp.zeros((32, local), jnp.bfloat16)]
            + [group(1 + i)[:, k * local : (k + 1) * local] for i in range(3)],
            axis=1,
        )
        ao[k] = group(4)[:, k * local : (k + 1) * local]
        bu[k] = group(7 + k)
        an[k] = group(11 + k)
    low_wide = jnp.where(mask, dot_t(n1[...], group(0)), 0.0)
    smalls[0] = low_wide.astype(jnp.bfloat16)
    lqh[...] = jnp.zeros_like(lqh)
    for r in range(2):
        for f in range(2):
            first = f * frame_rows + r * HALF_PITCH
            lqh[r, pl.ds(f * HALF_SLOT, HALF_PITCH)] = low_wide[
                first : first + HALF_PITCH
            ].astype(jnp.bfloat16)
    key_pad = (
        lax.rem(lax.broadcasted_iota(jnp.int32, (frame_rows, 1), 0), HALF_PITCH) >= shard_rows
    )
    bias = jnp.where(key_pad, -1e30, 0.0).astype(jnp.float32)

    LOW_QKV, LOW_OUT, LOW_UP, LOW_DOWN, THR_DOWN, THR_UP, THR_OUT, THR_QKV = range(8)

    def attention(i, out_low):
        zk = order(z, i)
        block = attn_block(zk)
        proj[zk] = (dot(n1[...], block) + dot(smalls[LOW_QKV], bq[zk])).astype(jnp.bfloat16)
        for f in range(2):
            at = pl.ds(f * frame_rows, frame_rows)
            for head in range(3):
                first = local + head * HEAD
                q = proj[zk, at, first : first + HEAD]
                k = proj[zk, at, first + local : first + local + HEAD]
                v = proj[zk, at, first + 2 * local : first + 2 * local + HEAD]
                scores = dot_t(k, q) * scale + bias
                exponent = jnp.exp(scores - jnp.max(scores, axis=0, keepdims=True))
                weights = exponent / jnp.sum(exponent, axis=0, keepdims=True)
                weights = weights.astype(jnp.bfloat16)
                soft[zk, f * 3 + head] = weights
                att[zk, at, head * HEAD : (head + 1) * HEAD] = (
                    t_dot(weights, v).astype(jnp.bfloat16)
                )
        gathered = att[zk]
        mid[...] += dot_t(gathered, block[:, :local])
        return out_low + dot_t(gathered, ao[zk])

    def attention_step(i, out_low):
        @pl.when(i == 1)
        def _():
            t1(6)
            t2(5)

        @pl.when(i == 2)
        def _():
            t3(4)

        @pl.when(i == 3)
        def _():
            t1(7)
            t2(6)

        return attention(i, out_low)

    out_low = lax.fori_loop(0, 4, attention_step, jnp.zeros((rows, 32), jnp.float32))
    t3(5)
    ready(4)
    smalls[LOW_OUT] = low(out_low)
    mid[...] += dot(smalls[LOW_OUT], group(5))

    def second_norm(at):
        unit, _ = norm_parts(mid[at])
        n2[at] = (unit * g2_ref[...].reshape(1, width)).astype(jnp.bfloat16)

    tiles(second_norm)
    cot_move.wait_recv()
    join(tmp, cs, cr)
    dyb[...] = tmp[...].astype(jnp.bfloat16)
    smalls[LOW_UP] = low(dot_t(n2[...], group(6)))
    smalls[THR_DOWN] = low(dot_t(dyb[...], group(15)))
    group_ref(15)[...] = jnp.zeros((32, width), jnp.bfloat16)
    t1(8)
    t2(7)
    acc[...] = mid[...]
    dn[...] = jnp.zeros_like(dn)

    def feed(i, lows):
        down_low, up_back = lows
        zk = order(z, i)
        q = 4 + 2 * i

        @pl.when((i > 0) & (i < 3))
        def _():
            t1(q + 3)
            t2(q + 2)

        @pl.when(i > 0)
        def _():
            ready(q)

        tmp[...] = dot(n2[...], w[zk, 1].reshape(width, width)) + dot(smalls[LOW_UP], bu[zk])

        def gate(at):
            hidden = tmp[at]
            phi = 0.5 + 0.5 * lax.erf(hidden * math.sqrt(0.5))
            bell = jnp.exp(-0.5 * hidden * hidden) * (1.0 / math.sqrt(2.0 * math.pi))
            buf[0, at] = (hidden * phi).astype(jnp.bfloat16)
            tmp[at] = phi + hidden * bell

        tiles(gate)
        active = buf[0]
        down_low = down_low + dot_t(active, an[zk])
        ga = 11 + zk
        g16[ga // 8, lax.rem(ga // 4, 2), lax.rem(ga // 2, 2), lax.rem(ga, 2)] = t_dot(
            smalls[THR_DOWN], active
        ).astype(jnp.bfloat16)

        @pl.when(i > 0)
        def _():
            t3(q + 1)

        @pl.when(i == 1)
        def _():
            t1(q + 4)

        @pl.when((i > 0) & (i < 3))
        def _():
            t2(q + 3)

        ready(q + 1)
        down = w[zk, 2].reshape(width, width)
        tmp[...] = tmp[...] * (dot(dyb[...], down) + dot(smalls[THR_DOWN], an[zk]))
        buf[1] = tmp[...].astype(jnp.bfloat16)
        d_hidden = buf[1]
        dn[...] += dot_t(d_hidden, w[zk, 1].reshape(width, width))
        acc[...] += dot_t(active, down)
        gu = 7 + zk
        g16[gu // 8, lax.rem(gu // 4, 2), lax.rem(gu // 2, 2), lax.rem(gu, 2)] = t_dot(
            smalls[LOW_UP], d_hidden
        ).astype(jnp.bfloat16)
        up_back = up_back + dot_t(d_hidden, bu[zk])

        @pl.when(i < 3)
        def _():
            t3(q + 2)

        return down_low, up_back

    empty = jnp.zeros((rows, 32), jnp.float32)
    down_low, up_back = lax.fori_loop(0, 4, feed, (empty, empty))
    smalls[LOW_DOWN] = low(down_low)
    smalls[THR_UP] = low(up_back)
    group_ref(15)[...] = t_dot(smalls[LOW_DOWN], dyb[...]).astype(jnp.bfloat16)

    def core_move(yx):
        src = g16.at[yx // 2, yx % 2, 1 - c]
        return remote(src, gc.at[yx], cxs.at[yx], cxr.at[yx], place(y, x, 1 - c, z))

    def owner_move(yx, zz):
        back_yx = lax.rem(y * 2 + x + 4 - yx, 4)
        back_z = lax.rem(z + 4 - zz, 4)
        slot = back_yx * 4 + back_z
        src = gs.at[yx, zz // 2, :, pl.ds((zz % 2) * span, span)]
        copy = remote(src, rb.at[slot], us.at[yx, zz], ur.at[slot], (yx * 2 + c, zz))
        return copy, slot

    def spread_out(yx):
        core_move(yx).wait_recv()
        for g in range(2):
            gs[yx, g] = (
                g16[yx // 2, yx % 2, c, g].astype(jnp.float32) + gc[yx, g].astype(jnp.float32)
            ).astype(jnp.bfloat16)
        for zz in range(4):
            copy, slot = owner_move(yx, zz)

            @pl.when(slot != 0)
            def _():
                copy.start()

            @pl.when(slot == 0)
            def _():
                rb[0] = gs[yx, zz // 2, :, pl.ds((zz % 2) * span, span)]

    core_move(3).start()
    core_move(2).start()

    group_ref(6)[...] = t_dot(smalls[THR_UP], n2[...]).astype(jnp.bfloat16)
    acc[...] += dot(smalls[LOW_DOWN], group(15))

    def second_back(at):
        grad = dn[at] + dot(smalls[THR_UP, at], group(6))
        value = dyb[at].astype(jnp.float32) + norm_back(
            mid[at], g2_ref[...].reshape(1, width), grad
        )
        dn[at] = value
        dbr[at] = value.astype(jnp.bfloat16)

    tiles(second_back)
    for f in range(2):
        own, other = halves(f)
        osend[f, pl.ds(0, HALF_PITCH)] = acc[other].astype(jnp.bfloat16)
    act_move.start()
    smalls[THR_OUT] = low(dot_t(dbr[...], group(5)))
    group_ref(5)[...] = t_dot(smalls[LOW_OUT], dbr[...]).astype(jnp.bfloat16)
    for r in range(2):
        for k in range(4):
            dpj[r, k, :, 0:local] = jnp.zeros((2 * HALF_SLOT, local), jnp.bfloat16)
            for f in range(2):
                dpj[r, k, pl.ds(f * HALF_SLOT + 96, 16)] = jnp.zeros((16, width), jnp.bfloat16)

    spread_out(3)
    spread_out(2)
    group_ref(4)[...] = jnp.concatenate(
        [t_dot(smalls[THR_OUT], att[k]).astype(jnp.bfloat16) for k in range(4)], axis=1
    )
    core_move(1).start()

    @pl.loop(0, 4)
    def _(zk):
        block = attn_block(zk)
        d_att = (dot(dbr[...], block[:, :local]) + dot(smalls[THR_OUT], ao[zk])).astype(
            jnp.bfloat16
        )
        buf[0, :, 0:local] = d_att

        @pl.when(zk == 1)
        def _():
            spread_out(1)

        for f in range(2):
            at = pl.ds(f * frame_rows, frame_rows)
            for head in range(3):
                first = local + head * HEAD
                q = proj[zk, at, first : first + HEAD]
                k = proj[zk, at, first + local : first + local + HEAD]
                v = proj[zk, at, first + 2 * local : first + 2 * local + HEAD]
                d_out = buf[0, at, head * HEAD : (head + 1) * HEAD]
                weights = soft[zk, f * 3 + head]
                d_values = dot(weights, d_out)
                d_soft = dot_t(v, d_out)
                wide = weights.astype(jnp.float32)
                inner = jnp.sum(wide * d_soft, axis=0, keepdims=True)
                d_scores = (wide * (d_soft - inner)).astype(jnp.bfloat16)
                d_keys = dot(d_scores, q) * scale
                d_queries = t_dot(k, d_scores).T * scale
                for r in range(2):
                    to = pl.ds(f * HALF_SLOT, HALF_PITCH)
                    cut = slice(r * HALF_PITCH, (r + 1) * HALF_PITCH)
                    dpj[r, zk, to, first : first + HEAD] = d_queries[cut].astype(jnp.bfloat16)
                    dpj[r, zk, to, first + local : first + local + HEAD] = d_keys[cut].astype(
                        jnp.bfloat16
                    )
                    dpj[r, zk, to, first + 2 * local : first + 2 * local + HEAD] = d_values[
                        cut
                    ].astype(jnp.bfloat16)

    half_rows = 2 * HALF_SLOT
    half_mask = (
        lax.broadcasted_iota(jnp.int32, (half_rows, 32), 0) // HALF_SLOT
        == lax.broadcasted_iota(jnp.int32, (half_rows, 32), 1) // RANK
    )

    def half_at(f, r):
        return pl.ds(pl.multiple_of(f * frame_rows + r * HALF_PITCH, 8), HALF_PITCH)

    def half_products(r, out):
        grad = dot_t(dpj[r, 0], attn_block(0))
        back = dot_t(dpj[r, 0], bq[0])
        for k in range(1, 4):
            grad = grad + dot_t(dpj[r, k], attn_block(k))
            back = back + dot_t(dpj[r, k], bq[k])
        back = jnp.where(half_mask, back, 0.0)
        for f in range(2):
            thr[half_at(f, r)] = back[f * HALF_SLOT : f * HALF_SLOT + HALF_PITCH]
        out[0:half_rows] = grad + dot(back.astype(jnp.bfloat16), group(0))

    def half_back(f, r, products):
        at = half_at(f, r)
        grad = products[f * HALF_SLOT : f * HALF_SLOT + HALF_PITCH]
        value = dn[at] + norm_back(xf[at], g1_ref[...].reshape(1, width), grad)
        return value.astype(jnp.bfloat16)

    half_products(1 - h, tmp)
    isend[0, pl.ds(0, HALF_PITCH)] = half_back(0, 1 - h, tmp)
    ing_moves[0].start()
    half_products(h, mid)
    smalls[THR_QKV] = thr[...].astype(jnp.bfloat16)
    group_ref(0)[...] = t_dot(smalls[THR_QKV], n1[...]).astype(jnp.bfloat16)
    parts = [
        (t_dot(lqh[0], dpj[0, k]) + t_dot(lqh[1], dpj[1, k])).astype(jnp.bfloat16)
        for k in range(4)
    ]
    for i in range(3):
        first = (1 + i) * local
        group_ref(1 + i)[...] = jnp.concatenate(
            [parts[k][:, first : first + local] for k in range(4)], axis=1
        )
    core_move(0).start()
    isend[1, pl.ds(0, HALF_PITCH)] = half_back(1, 1 - h, tmp)
    spread_out(0)
    ing_moves[1].start()
    own_ing[0] = half_back(0, h, mid)
    own_ing[1] = half_back(1, h, mid)

    for f in range(2):
        own_act[f] = acc[halves(f)[0]].astype(jnp.bfloat16)
    act_move.wait_recv()
    give(act_ref, own_act, orecv)

    for slot in range(1, 16):
        remote(rb.at[slot], rb.at[slot], us.at[0, 0], ur.at[slot], (dp, zp)).wait_recv()
    for parity in range(2):
        total = jnp.zeros((32, span), jnp.float32)
        for slot in range(16):
            if slot % 2 == parity:
                total = total + rb[slot].astype(jnp.float32)
        first = lax.rem(h + parity, 2)
        for a in range(table_ref.shape[0] // RANK):
            chosen = [
                jnp.where(
                    jnp.full((RANK, span), clip_ref[2 * first + i]) == a,
                    total[i * RANK : (i + 1) * RANK],
                    0.0,
                )
                for i in range(2)
            ]
            gr_ref[first, pl.ds(a * RANK, RANK)] = chosen[0] + chosen[1]
    for yx in range(4):
        core_move(yx).wait_send()
        for zz in range(4):
            copy, slot = owner_move(yx, zz)

            @pl.when(slot != 0)
            def _():
                copy.wait_send()

    tok_move.wait_send()
    cot_move.wait_send()
    for j in range(1, 4):
        ad_move(j).wait_send()

    for q in (1, 2, 3, 6, 7, 8, 9, 10, 11):
        z_move(q).wait_send()
    for q in range(4):
        for what in range(9):
            move(q, what).wait_send()

    @pl.loop(4, 12)
    def _(q):
        for what in range(9):
            move(q, what).wait_send()

    for what in range(9):
        move(None, what).wait_send()
    act_move.wait_send()
    for f in range(2):
        ing_moves[f].wait()
    give(ing_ref, own_ing, irecv)


def finish_kernel(
    act_ref, ing_ref, gr_ref, table_ref, one_ref, two_ref, act_out, ing_out, *outs
):
    act_out[...] = act_ref[...]
    ing_out[...] = ing_ref[...]
    results = adam(gr_ref[0] + gr_ref[1], table_ref[...], one_ref[...], two_ref[...])
    for out, result in zip(outs, results):
        out[...] = result


def fused(
    tokens,
    cotangent,
    clip_adapter,
    gain_one,
    gain_two,
    w_qkv,
    w_out,
    w_up,
    w_down,
    adapters,
    moment_one,
    moment_two,
):
    micro_count, shard_rows, width = tokens.shape
    rank_all, span = adapters.shape
    rows = 4 * HALF_PITCH
    frame_rows = 2 * HALF_PITCH
    local = width // 4
    bf, f32 = jnp.bfloat16, jnp.float32
    vmem = pl.BlockSpec(memory_space=pltpu.VMEM)
    smem = pl.BlockSpec(memory_space=pltpu.SMEM)
    scratch = [
        pltpu.VMEM((4, 3, 2, 2, 2, 96, width), bf),
        pltpu.VMEM((2, 2, 2, 2, 32, width), bf),
        pltpu.VMEM((4, HALF_SLOT, width), bf),
        pltpu.VMEM((4, HALF_SLOT, width), bf),
        pltpu.VMEM((2, HALF_SLOT, width), bf),
        pltpu.VMEM((2, HALF_SLOT, width), bf),
        pltpu.VMEM((rows, width), f32),
        pltpu.VMEM((rows, width), bf),
        pltpu.VMEM((rows, width), bf),
        pltpu.VMEM((rows, width), bf),
        pltpu.VMEM((4, rows, width), bf),
        pltpu.VMEM((4, 6, frame_rows, frame_rows), bf),
        pltpu.VMEM((4, rows, local), bf),
        pltpu.VMEM((rows, width), f32),
        pltpu.VMEM((rows, width), f32),
        pltpu.VMEM((rows, width), f32),
        pltpu.VMEM((rows, width), f32),
        pltpu.VMEM((2, rows, width), bf),
        pltpu.VMEM((rows, width), bf),
        pltpu.VMEM((2, 4, 2 * HALF_SLOT, width), bf),
        pltpu.VMEM((2, 2 * HALF_SLOT, 32), bf),
        pltpu.VMEM((rows, 32), f32),
        pltpu.VMEM((4, 32, width), bf),
        pltpu.VMEM((4, 32, local), bf),
        pltpu.VMEM((4, 32, width), bf),
        pltpu.VMEM((4, 32, width), bf),
        pltpu.VMEM((2, 2, 2, 2, 32, width), bf),
        pltpu.VMEM((4, 2, 32, width), bf),
        pltpu.VMEM((4, 2, 32, width), bf),
        pltpu.VMEM((16, 32, span), bf),
        pltpu.VMEM((2, HALF_SLOT, width), bf),
        pltpu.VMEM((2, HALF_SLOT, width), bf),
        pltpu.VMEM((2, HALF_PITCH, width), bf),
        pltpu.VMEM((2, HALF_PITCH, width), bf),
        pltpu.VMEM((2, HALF_SLOT, width), bf),
        pltpu.VMEM((2, HALF_SLOT, width), bf),
        pltpu.VMEM((2, 32, span), bf),
        pltpu.VMEM((8, rows, 32), bf),
        pltpu.SemaphoreType.DMA((3, 4)),
        pltpu.SemaphoreType.DMA((3, 4)),
        pltpu.SemaphoreType.DMA((4,)),
        pltpu.SemaphoreType.DMA((4,)),
        pltpu.SemaphoreType.DMA((13, 9)),
        pltpu.SemaphoreType.DMA((13, 9)),
        pltpu.SemaphoreType.DMA((5,)),
        pltpu.SemaphoreType.DMA((5,)),
        pltpu.SemaphoreType.DMA((4,)),
        pltpu.SemaphoreType.DMA((4,)),
        pltpu.SemaphoreType.DMA((4, 4)),
        pltpu.SemaphoreType.DMA((16,)),
    ]
    act, ing, grads = pl.pallas_call(
        fused_kernel,
        out_shape=(
            jax.ShapeDtypeStruct((shard_rows, micro_count, width), bf),
            jax.ShapeDtypeStruct((shard_rows, micro_count, width), bf),
            jax.ShapeDtypeStruct((2, rank_all, span), f32),
        ),
        in_specs=[vmem] * 9 + [smem],
        out_specs=(vmem, vmem, vmem),
        scratch_shapes=scratch,
        compiler_params=pltpu.CompilerParams(
            collective_id=0, has_side_effects=True, vmem_limit_bytes=60 * 2**20
        ),
    )(
        tokens.transpose(1, 0, 2),
        cotangent.transpose(1, 0, 2),
        gain_one,
        gain_two,
        w_qkv.transpose(1, 0, 2),
        w_out,
        w_up,
        w_down.T,
        adapters,
        clip_adapter,
    )
    plain = jax.ShapeDtypeStruct((rank_all, span), f32)
    rows_spec = pl.BlockSpec((shard_rows // 2, micro_count, width), lambda i: (i, 0, 0))
    plain_spec = pl.BlockSpec((rank_all // 2, span), lambda i: (i, 0))
    act, ing, *others = pl.pallas_call(
        finish_kernel,
        out_shape=(act, ing) + (plain,) * 4 + (jax.ShapeDtypeStruct((rank_all, span), bf),),
        grid=(2,),
        in_specs=[rows_spec] * 2
        + [pl.BlockSpec((2, rank_all // 2, span), lambda i: (0, i, 0))]
        + [plain_spec] * 3,
        out_specs=(rows_spec,) * 2 + (plain_spec,) * 5,
    )(act, ing, grads, adapters, moment_one, moment_two)
    return (act.transpose(1, 0, 2), ing.transpose(1, 0, 2), *others)


def layer(tokens, *others):
    w_up = others[6]
    sizes = lax.axis_size("dp"), lax.axis_size("mp")
    frames_micro = tokens.shape[1] * sizes[0] * sizes[1] // FRAME
    fits = (
        sizes == (8, 4)
        and tokens.shape[0] == 4
        and 2 * tokens.shape[1] == FRAME
        and frames_micro == CLIP_FRAMES
        and w_up.shape == (tokens.shape[2] // 8, tokens.shape[2])
    )
    return (fused if fits else shards)(tokens, *others)


def solution(mesh):
    spread = P(None, ("dp", "mp"))
    rows = P(None, ("dp", "mp"), None)
    return jax.shard_map(
        layer,
        mesh=mesh,
        in_specs=(
            rows,
            rows,
            P(),
            P(),
            P(),
            P("dp", None, "mp"),
            P("mp", "dp"),
            P("dp", "mp"),
            P("mp", "dp"),
            spread,
            spread,
            spread,
        ),
        out_specs=(rows, rows, spread, spread, spread, spread, spread),
        check_vma=False,
    )
```

```python
import functools
import math

import jax
import jax.numpy as jnp
from jax import lax
from jax.experimental import pallas as pl
from jax.experimental.pallas import tpu as pltpu
from jax.sharding import PartitionSpec as P

HEAD = 64
FRAME = 196
RANK = 16
CLIP_FRAMES = 16
STEP = 5

norm_epsilon = 1e-06
beta_first = 0.5
beta_second = 0.5
learn_rate = 0.05
weight_decay = 0.01
adam_epsilon = 1e-08


def dot(left, right):
    return jnp.dot(left, right, preferred_element_type=jnp.float32)


def dot_t(left, right):
    return lax.dot_general(left, right, (((1,), (1,)), ((), ())), preferred_element_type=jnp.float32)


def t_dot(left, right):
    return lax.dot_general(left, right, (((0,), (0,)), ((), ())), preferred_element_type=jnp.float32)


def half(values):
    return values.astype(jnp.bfloat16)


def norm_parts(values):
    center = values - jnp.mean(values, axis=-1, keepdims=True)
    spread = jnp.mean(center * center, axis=-1, keepdims=True)
    inverse = lax.rsqrt(spread + norm_epsilon)
    return center * inverse, inverse


def norm_back(unit, inverse, gain, grad):
    scaled = grad * gain
    first = jnp.mean(scaled, axis=-1, keepdims=True)
    second = jnp.mean(scaled * unit, axis=-1, keepdims=True)
    return inverse * (scaled - first - unit * second)


def adam(owner_grad, adapters, moment_one, moment_two):
    first_moment = beta_first * moment_one + (1.0 - beta_first) * owner_grad
    second_moment = beta_second * moment_two + (1.0 - beta_second) * owner_grad * owner_grad
    first_hat = first_moment / (1.0 - beta_first**STEP)
    second_hat = second_moment / (1.0 - beta_second**STEP)
    updated = adapters - learn_rate * (
        first_hat / (jnp.sqrt(second_hat) + adam_epsilon) + weight_decay * adapters
    )
    return (
        owner_grad,
        updated,
        first_moment,
        second_moment,
        updated.astype(jnp.bfloat16),
    )


def shards(
    tokens,
    cotangent,
    clip_adapter,
    gain_one,
    gain_two,
    w_qkv,
    w_out,
    w_up,
    w_down,
    adapters,
    moment_one,
    moment_two,
):
    groups = lax.axis_size("mp")
    member = lax.axis_index("mp")
    group_index = lax.axis_index("dp")
    micro_count, shard_rows, width = tokens.shape
    hidden_width = w_up.shape[1] * groups
    heads = width // HEAD
    rank_all = adapters.shape[0]
    full_width = adapters.shape[1] * lax.axis_size(("dp", "mp"))
    frames = shard_rows * groups // FRAME
    frames_micro = frames * lax.axis_size("dp")
    scale = 1.0 / math.sqrt(HEAD)
    span = FRAME // shard_rows
    mine = micro_count // span
    part = member % span
    pairs = [[first * span + k for k in range(span)] for first in range(groups // span)]

    def swap(rows):
        return lax.all_to_all(
            rows, "mp", split_axis=0, concat_axis=1, axis_index_groups=pairs, tiled=True
        ).reshape(mine * FRAME, width)

    def swap_back(rows):
        return lax.all_to_all(
            rows.reshape(mine, FRAME, width),
            "mp",
            split_axis=1,
            concat_axis=0,
            axis_index_groups=pairs,
            tiled=True,
        )

    inputs = swap(tokens).astype(jnp.float32)
    dy = swap(cotangent)

    def whole(weight, first, second):
        return lax.all_gather(
            lax.all_gather(weight, first[0], axis=first[1], tiled=True),
            second[0],
            axis=second[1],
            tiled=True,
        )

    qkv_all = whole(w_qkv, ("dp", 0), ("mp", 2)).reshape(width, 3 * width)
    out_all = whole(w_out, ("dp", 1), ("mp", 0))
    up_all = whole(w_up, ("dp", 0), ("mp", 1))
    down_all = whole(w_down, ("dp", 1), ("mp", 0))
    table = lax.all_gather(half(adapters), ("dp", "mp"), axis=1, tiled=True)
    table = table.reshape(rank_all // RANK, RANK, full_width)
    clips = jnp.stack(
        [
            ((part * mine + i) * frames_micro + group_index * frames + member // span)
            // CLIP_FRAMES
            for i in range(mine)
        ]
    )
    chosen = clip_adapter[clips]
    own = table[chosen].reshape(mine * RANK, full_width)
    ends = [0, width, 4 * width, 5 * width, 6 * width, 7 * width]
    ends += [7 * width + hidden_width, 7 * width + 2 * hidden_width, full_width]
    a_qkv, b_qkv, a_out, b_out, a_up, b_up, a_down, b_down = [
        own[:, ends[i] : ends[i + 1]] for i in range(8)
    ]
    rows = mine * FRAME
    row_frame = lax.broadcasted_iota(jnp.int32, (rows, mine * RANK), 0) // FRAME
    column_frame = lax.broadcasted_iota(jnp.int32, (rows, mine * RANK), 1) // RANK
    mask = row_frame == column_frame

    def low(values):
        return half(jnp.where(mask, values, 0.0))

    shape_heads = (mine, FRAME, heads, HEAD)
    unit_one, inverse_one = norm_parts(inputs)
    normed_one = half(unit_one * gain_one)
    low_qkv = low(dot_t(normed_one, a_qkv))
    projected = half(dot(normed_one, qkv_all) + dot(low_qkv, b_qkv))
    queries = projected[:, 0:width].reshape(shape_heads)
    keys = projected[:, width : 2 * width].reshape(shape_heads)
    values = projected[:, 2 * width :].reshape(shape_heads)
    scores = jnp.einsum("fqhd,fkhd->fhqk", queries, keys, preferred_element_type=jnp.float32)
    scores = scores * scale
    exponent = jnp.exp(scores - jnp.max(scores, axis=-1, keepdims=True))
    soft = exponent / jnp.sum(exponent, axis=-1, keepdims=True)
    soft_half = half(soft)
    attended = half(
        jnp.einsum("fhqk,fkhd->fqhd", soft_half, values, preferred_element_type=jnp.float32)
    ).reshape(rows, width)
    low_out = low(dot_t(attended, a_out))
    middle = inputs + dot(attended, out_all) + dot(low_out, b_out)
    unit_two, inverse_two = norm_parts(middle)
    normed_two = half(unit_two * gain_two)
    low_up = low(dot_t(normed_two, a_up))
    hidden = dot(normed_two, up_all) + dot(low_up, b_up)
    phi = 0.5 * (1.0 + lax.erf(hidden * math.sqrt(0.5)))
    active = half(hidden * phi)
    slope = phi + hidden * jnp.exp(-0.5 * hidden * hidden) * (1.0 / math.sqrt(2.0 * math.pi))
    low_down = low(dot_t(active, a_down))
    outputs = half(middle + dot(active, down_all) + dot(low_down, b_down))

    through_down = low(dot_t(dy, b_down))
    d_active = dot_t(dy, down_all) + dot(through_down, a_down)
    d_hidden = half(d_active * slope)
    through_up = low(dot_t(d_hidden, b_up))
    d_normed_two = dot_t(d_hidden, up_all) + dot(through_up, a_up)
    d_middle = dy.astype(jnp.float32) + norm_back(unit_two, inverse_two, gain_two, d_normed_two)
    d_branch = half(d_middle)
    through_out = low(dot_t(d_branch, b_out))
    d_attended = half(dot_t(d_branch, out_all) + dot(through_out, a_out))
    d_heads = d_attended.reshape(shape_heads)
    d_values = jnp.einsum("fhqk,fqhd->fkhd", soft_half, d_heads, preferred_element_type=jnp.float32)
    d_soft = jnp.einsum("fqhd,fkhd->fhqk", d_heads, values, preferred_element_type=jnp.float32)
    inner = jnp.sum(soft * d_soft, axis=-1, keepdims=True)
    d_scores = half(soft * (d_soft - inner))
    d_queries = scale * jnp.einsum(
        "fhqk,fkhd->fqhd", d_scores, keys, preferred_element_type=jnp.float32
    )
    d_keys = scale * jnp.einsum(
        "fhqk,fqhd->fkhd", d_scores, queries, preferred_element_type=jnp.float32
    )
    d_projected = half(
        jnp.concatenate([d.reshape(rows, width) for d in (d_queries, d_keys, d_values)], axis=1)
    )
    through_qkv = low(dot_t(d_projected, b_qkv))
    d_normed_one = dot_t(d_projected, qkv_all) + dot(through_qkv, a_qkv)
    input_grad = half(d_middle + norm_back(unit_one, inverse_one, gain_one, d_normed_one))
    grads = half(jnp.concatenate(
        [
            t_dot(through_qkv, normed_one),
            t_dot(low_qkv, d_projected),
            t_dot(through_out, attended),
            t_dot(low_out, d_branch),
            t_dot(through_up, normed_two),
            t_dot(low_up, d_hidden),
            t_dot(through_down, active),
            t_dot(low_down, dy),
        ],
        axis=1,
    ))
    pick = (
        lax.broadcasted_iota(jnp.int32, (rank_all, mine * RANK), 0)
        == jnp.repeat(chosen, RANK)[None, :] * RANK
        + lax.broadcasted_iota(jnp.int32, (rank_all, mine * RANK), 1) % RANK
    ).astype(jnp.bfloat16)
    owner_grad = lax.psum_scatter(
        dot(pick, grads), ("dp", "mp"), scatter_dimension=1, tiled=True
    )
    return (swap_back(outputs), swap_back(input_grad)) + adam(
        owner_grad, adapters, moment_one, moment_two
    )


MESH = pl.DeviceIdType.MESH
X1, Y1, Y2, X2, C0, C1A, C1B, C2A, C2B = range(9)
HALF_PITCH = 104
HALF_SLOT = 112


def fused_kernel(
    tok_ref,
    cot_ref,
    g1_ref,
    g2_ref,
    wq_ref,
    wo_ref,
    wu_ref,
    wd_ref,
    table_ref,
    clip_ref,
    act_ref,
    ing_ref,
    gr_ref,
    w,
    ad,
    ts,
    cs,
    tr,
    cr,
    xf,
    dyb,
    n1,
    n2,
    proj,
    soft,
    att,
    mid,
    acc,
    dn,
    tmp,
    buf,
    dbr,
    dpj,
    lqh,
    thr,
    bq,
    ao,
    bu,
    an,
    g16,
    gc,
    gs,
    rb,
    osend,
    isend,
    own_act,
    own_ing,
    orecv,
    irecv,
    adp,
    smalls,
    zs,
    zr,
    azs,
    azr,
    ss,
    rs,
    ps,
    pr,
    cxs,
    cxr,
    us,
    ur,
):
    dp = lax.axis_index("dp")
    z = lax.axis_index("mp")
    y = dp // 4
    x = lax.rem(dp // 2, 2)
    c = lax.rem(dp, 2)
    h = lax.rem(z, 2)
    zp = z + 1 - 2 * h
    zn = 4
    shard_rows = tok_ref.shape[0]
    rows = xf.shape[0]
    frame_rows = rows // 2
    width = xf.shape[1]
    local = width // zn
    scale = 1.0 / math.sqrt(HEAD)

    def place(yy, xx, cc, zz):
        return ((yy * 2 + xx) * 2 + cc, zz)

    def order(at_z, k):
        upper = at_z // 2
        near = at_z + upper * (3 - 2 * at_z)
        swapped = jnp.where((near == 1) & (k < 2), 1 - k, k)
        return swapped + upper * (3 - 2 * swapped)

    def rank_of(at_z, block_z):
        upper = at_z // 2
        near = at_z + upper * (3 - 2 * at_z)
        mirrored = block_z + upper * (3 - 2 * block_z)
        return jnp.where((near == 1) & (mirrored < 2), 1 - mirrored, mirrored)

    barrier = pltpu.get_barrier_semaphore()
    for k in range(1, 16):
        yx = lax.rem(y * 2 + x + k // 4, 4)
        target = (yx * 2 + c, lax.rem(z + k % 4, 4))
        pl.semaphore_signal(barrier, inc=1, device_id=target, device_id_type=MESH)
    pl.semaphore_signal(barrier, inc=1, device_id=place(y, x, 1 - c, z), device_id_type=MESH)

    def remote(src, dst, send, recv, target):
        return pltpu.make_async_remote_copy(
            src_ref=src,
            dst_ref=dst,
            send_sem=send,
            recv_sem=recv,
            device_id=target,
            device_id_type=MESH,
        )

    w[z, 0, y, x, c] = jnp.concatenate([wo_ref[...].T] + [wq_ref[i] for i in range(3)], axis=1)
    span = table_ref.shape[1]
    low_columns = pl.ds(pl.multiple_of(lax.rem(z, 2) * span, 128), span)
    for m in range(4):
        clip = jnp.full((RANK, span), clip_ref[m])
        chosen = jnp.zeros((RANK, span), jnp.float32)
        for a in range(table_ref.shape[0] // RANK):
            chosen = jnp.where(clip == a, table_ref[a * RANK : (a + 1) * RANK], chosen)
        adp[m // 2, pl.ds((m % 2) * RANK, RANK)] = chosen.astype(jnp.bfloat16)
    ad[y, x, c, z // 2, :, low_columns] = adp[h]

    def stage(dst, src):
        for m in range(4):
            dst[m, pl.ds(96, 16)] = jnp.zeros((16, width), jnp.bfloat16)
            dst[m, pl.ds(0, shard_rows)] = src[:, m, :]

    def part(kind, zk, yy, xx, cc, first, count):
        return w.at[zk, kind, yy, xx, cc, pl.ds(first, count), :]

    def phase(q):
        if isinstance(q, int):
            return (0, q) if q < 4 else (1 + q % 2, (q - 4) // 2)
        return 1 + lax.rem(q, 2), (q - 4) // 2

    def move(q, what):
        full = 32 if q is None else 96
        n = full // 2
        every = pl.ds(0, 2)
        args, target = {
            X1: ((y, x, c, 0, n), (y, 1 - x, c)),
            Y1: ((y, x, c, n, n), (1 - y, x, c)),
            Y2: ((y, every, c, 0, n), (1 - y, x, c)),
            X2: ((every, x, c, n, n), (y, 1 - x, c)),
            C0: ((y, x, c, 0, full), (y, x, 1 - c)),
            C1A: ((y, 1 - x, c, 0, n), (y, x, 1 - c)),
            C1B: ((1 - y, x, c, n, n), (y, x, 1 - c)),
            C2A: ((1 - y, every, c, 0, n), (y, x, 1 - c)),
            C2B: ((every, 1 - x, c, n, n), (y, x, 1 - c)),
        }[what]
        if q is None:
            yy, xx, cc, first, count = args
            ref = ad.at[yy, xx, cc, :, pl.ds(first, count), :]
            index = 12
        else:
            kind, k = phase(q)
            ref = part(kind, order(z, k), *args)
            index = q
        return remote(ref, ref, ss.at[index, what], rs.at[index, what], place(*target, z))

    def z_move(q):
        kind, k = phase(q)
        ref = part(kind, z, y, x, c, 0, 96)
        other = order(z, k)
        return remote(ref, ref, zs.at[kind, k], zr.at[kind, rank_of(other, z)], (dp, other))

    def z_wait(q):
        kind, k = phase(q)
        ref = part(kind, z, y, x, c, 0, 96)
        remote(ref, ref, zs.at[kind, k], zr.at[kind, k], (dp, zp)).wait_recv()

    def ad_move(j):
        other = lax.rem(z + zn - j, zn)
        dst = ad.at[y, x, c, z // 2, :, low_columns]
        return remote(adp.at[lax.rem(other, 2)], dst, azs.at[j], azr.at[j], (dp, other))

    def t1(q):
        if isinstance(q, int):
            if q is not None and phase(q)[1]:
                z_wait(q)
        elif q is not None:
            z_wait(q)
        for what in (X1, Y1, C0):
            move(q, what).start()

    def t2(q):
        move(q, X1).wait_recv()
        move(q, Y2).start()
        move(q, Y1).wait_recv()
        move(q, X2).start()
        move(q, C1A).start()
        move(q, C1B).start()

    def t3(q):
        move(q, Y2).wait_recv()
        move(q, C2A).start()
        move(q, X2).wait_recv()
        move(q, C2B).start()

    def ready(q):
        for what in (C0, C1A, C1B, C2A, C2B):
            move(q, what).wait_recv()

    tok_move = remote(
        ts.at[pl.ds(2 - 2 * h, 2)], tr, ps.at[0], pr.at[0], (dp, zp)
    )
    cot_move = remote(
        cs.at[pl.ds(2 - 2 * h, 2)], cr, ps.at[1], pr.at[1], (dp, zp)
    )
    act_move = remote(
        osend, orecv, ps.at[2], pr.at[2], (dp, zp)
    )
    ing_moves = [
        remote(isend.at[f], irecv.at[f], ps.at[3 + f], pr.at[3 + f], (dp, zp)) for f in range(2)
    ]

    pl.semaphore_wait(barrier, 16)
    t1(0)
    for j in range(1, 4):
        ad_move(j).start()
    z_move(1).start()
    w[z, 1, y, x, c] = wu_ref[...]
    t1(4)
    stage(ts, tok_ref)
    tok_move.start()
    z_move(2).start()
    z_move(3).start()
    w[z, 2, y, x, c] = wd_ref[...]
    t2(0)
    t1(1)
    for j in range(1, 4):
        ad_move(j).wait_recv()
    t1(None)
    t2(1)
    t1(2)
    t2(None)
    t3(0)
    z_move(6).start()
    z_move(7).start()
    t2(2)
    t1(3)
    t3(1)
    t3(None)
    t2(3)
    t2(4)
    t3(2)
    z_move(8).start()
    z_move(9).start()
    stage(cs, cot_ref)
    cot_move.start()
    t1(5)
    t3(3)
    z_move(10).start()
    z_move(11).start()

    def dot(left, right):
        return jnp.dot(left, right, preferred_element_type=jnp.float32)

    def dot_t(left, right):
        return lax.dot_general(
            left, right, (((1,), (1,)), ((), ())), preferred_element_type=jnp.float32
        )

    def t_dot(left, right):
        return lax.dot_general(
            left, right, (((0,), (0,)), ((), ())), preferred_element_type=jnp.float32
        )

    row_frame = lax.broadcasted_iota(jnp.int32, (rows, 32), 0) // frame_rows
    column_frame = lax.broadcasted_iota(jnp.int32, (rows, 32), 1) // RANK
    mask = row_frame == column_frame

    def low(values):
        return jnp.where(mask, values, 0.0).astype(jnp.bfloat16)

    def tiles(body, step=416):
        @pl.loop(0, rows // step)
        def _(t):
            body(pl.ds(pl.multiple_of(t * step, step), step))

    def norm_parts(values):
        center = values - jnp.mean(values, axis=-1, keepdims=True)
        spread = jnp.mean(center * center, axis=-1, keepdims=True)
        inverse = lax.rsqrt(spread + norm_epsilon)
        return center * inverse, inverse

    def norm_back(values, gain, grad):
        unit, inverse = norm_parts(values)
        scaled = grad * gain
        first = jnp.mean(scaled, axis=-1, keepdims=True)
        second = jnp.mean(scaled * unit, axis=-1, keepdims=True)
        return inverse * (scaled - first - unit * second)

    def group(g):
        return ad[g // 8, (g // 4) % 2, (g // 2) % 2, g % 2]

    def group_ref(g):
        return g16.at[g // 8, (g // 4) % 2, (g // 2) % 2, g % 2]

    def attn_block(zk):
        return w[zk, 0].reshape(width, width)

    def halves(f):
        own = pl.ds(pl.multiple_of(f * frame_rows + h * HALF_PITCH, 8), HALF_PITCH)
        other = pl.ds(pl.multiple_of(f * frame_rows + (1 - h) * HALF_PITCH, 8), HALF_PITCH)
        return own, other

    def join(dst, own_slots, other_slots):
        for f in range(2):
            own, other = halves(f)
            dst[own] = own_slots[2 * h + f][:HALF_PITCH].astype(jnp.float32)
            dst[other] = other_slots[f][:HALF_PITCH].astype(jnp.float32)

    def give(dst, own, received):
        for f in range(2):
            first, second = own[f, pl.ds(0, shard_rows)], received[f, pl.ds(0, shard_rows)]
            dst[:, f, :] = jnp.where(h == 0, first, second)
            dst[:, 2 + f, :] = jnp.where(h == 0, second, first)

    tok_move.wait_recv()
    join(xf, ts, tr)

    def first_norm(at):
        values = xf[at]
        unit, _ = norm_parts(values)
        n1[at] = (unit * g1_ref[...].reshape(1, width)).astype(jnp.bfloat16)
        mid[at] = values

    tiles(first_norm)
    ready(None)
    for k in range(4):
        bq[k] = jnp.concatenate(
            [jnp.zeros((32, local), jnp.bfloat16)]
            + [group(1 + i)[:, k * local : (k + 1) * local] for i in range(3)],
            axis=1,
        )
        ao[k] = group(4)[:, k * local : (k + 1) * local]
        bu[k] = group(7 + k)
        an[k] = group(11 + k)
    low_wide = jnp.where(mask, dot_t(n1[...], group(0)), 0.0)
    smalls[0] = low_wide.astype(jnp.bfloat16)
    lqh[...] = jnp.zeros_like(lqh)
    for r in range(2):
        for f in range(2):
            first = f * frame_rows + r * HALF_PITCH
            lqh[r, pl.ds(f * HALF_SLOT, HALF_PITCH)] = low_wide[
                first : first + HALF_PITCH
            ].astype(jnp.bfloat16)
    key_pad = (
        lax.rem(lax.broadcasted_iota(jnp.int32, (frame_rows, 1), 0), HALF_PITCH) >= shard_rows
    )
    bias = jnp.where(key_pad, -1e30, 0.0).astype(jnp.float32)

    LOW_QKV, LOW_OUT, LOW_UP, LOW_DOWN, THR_DOWN, THR_UP, THR_OUT, THR_QKV = range(8)

    def attention(i, out_low):
        zk = order(z, i)
        block = attn_block(zk)
        proj[zk] = (dot(n1[...], block) + dot(smalls[LOW_QKV], bq[zk])).astype(jnp.bfloat16)
        for f in range(2):
            at = pl.ds(f * frame_rows, frame_rows)
            for head in range(3):
                first = local + head * HEAD
                q = proj[zk, at, first : first + HEAD]
                k = proj[zk, at, first + local : first + local + HEAD]
                v = proj[zk, at, first + 2 * local : first + 2 * local + HEAD]
                scores = dot_t(k, q) * scale + bias
                exponent = jnp.exp(scores - jnp.max(scores, axis=0, keepdims=True))
                weights = exponent / jnp.sum(exponent, axis=0, keepdims=True)
                weights = weights.astype(jnp.bfloat16)
                soft[zk, f * 3 + head] = weights
                att[zk, at, head * HEAD : (head + 1) * HEAD] = (
                    t_dot(weights, v).astype(jnp.bfloat16)
                )
        gathered = att[zk]
        mid[...] += dot_t(gathered, block[:, :local])
        return out_low + dot_t(gathered, ao[zk])

    def attention_step(i, out_low):
        @pl.when(i == 1)
        def _():
            t1(6)
            t2(5)

        @pl.when(i == 2)
        def _():
            t3(4)

        @pl.when(i == 3)
        def _():
            t1(7)
            t2(6)

        for k in range(4):

            @pl.when(i == k)
            def _():
                ready(k)

        return attention(i, out_low)

    out_low = lax.fori_loop(0, 4, attention_step, jnp.zeros((rows, 32), jnp.float32))
    t3(5)
    ready(4)
    smalls[LOW_OUT] = low(out_low)
    mid[...] += dot(smalls[LOW_OUT], group(5))

    def second_norm(at):
        unit, _ = norm_parts(mid[at])
        n2[at] = (unit * g2_ref[...].reshape(1, width)).astype(jnp.bfloat16)

    tiles(second_norm)
    cot_move.wait_recv()
    join(tmp, cs, cr)
    dyb[...] = tmp[...].astype(jnp.bfloat16)
    smalls[LOW_UP] = low(dot_t(n2[...], group(6)))
    smalls[THR_DOWN] = low(dot_t(dyb[...], group(15)))
    group_ref(15)[...] = jnp.zeros((32, width), jnp.bfloat16)
    t1(8)
    t2(7)
    acc[...] = mid[...]
    dn[...] = jnp.zeros_like(dn)

    def feed(i, lows):
        down_low, up_back = lows
        zk = order(z, i)
        q = 4 + 2 * i

        @pl.when((i > 0) & (i < 3))
        def _():
            t1(q + 3)
            t2(q + 2)

        @pl.when(i > 0)
        def _():
            ready(q)

        tmp[...] = dot(n2[...], w[zk, 1].reshape(width, width)) + dot(smalls[LOW_UP], bu[zk])

        def gate(at):
            hidden = tmp[at]
            phi = 0.5 + 0.5 * lax.erf(hidden * math.sqrt(0.5))
            bell = jnp.exp(-0.5 * hidden * hidden) * (1.0 / math.sqrt(2.0 * math.pi))
            buf[0, at] = (hidden * phi).astype(jnp.bfloat16)
            tmp[at] = phi + hidden * bell

        tiles(gate)
        active = buf[0]
        down_low = down_low + dot_t(active, an[zk])
        ga = 11 + zk
        g16[ga // 8, lax.rem(ga // 4, 2), lax.rem(ga // 2, 2), lax.rem(ga, 2)] = t_dot(
            smalls[THR_DOWN], active
        ).astype(jnp.bfloat16)

        @pl.when(i > 0)
        def _():
            t3(q + 1)

        @pl.when(i == 1)
        def _():
            t1(q + 4)

        @pl.when((i > 0) & (i < 3))
        def _():
            t2(q + 3)

        ready(q + 1)
        down = w[zk, 2].reshape(width, width)
        tmp[...] = tmp[...] * (dot(dyb[...], down) + dot(smalls[THR_DOWN], an[zk]))
        buf[1] = tmp[...].astype(jnp.bfloat16)
        d_hidden = buf[1]
        dn[...] += dot_t(d_hidden, w[zk, 1].reshape(width, width))
        acc[...] += dot_t(active, down)
        gu = 7 + zk
        g16[gu // 8, lax.rem(gu // 4, 2), lax.rem(gu // 2, 2), lax.rem(gu, 2)] = t_dot(
            smalls[LOW_UP], d_hidden
        ).astype(jnp.bfloat16)
        up_back = up_back + dot_t(d_hidden, bu[zk])

        @pl.when(i < 3)
        def _():
            t3(q + 2)

        return down_low, up_back

    empty = jnp.zeros((rows, 32), jnp.float32)
    down_low, up_back = lax.fori_loop(0, 4, feed, (empty, empty))
    smalls[LOW_DOWN] = low(down_low)
    smalls[THR_UP] = low(up_back)
    group_ref(15)[...] = t_dot(smalls[LOW_DOWN], dyb[...]).astype(jnp.bfloat16)

    def core_move(yx):
        src = g16.at[yx // 2, yx % 2, 1 - c]
        return remote(src, gc.at[yx], cxs.at[yx], cxr.at[yx], place(y, x, 1 - c, z))

    def owner_move(yx, zz):
        back_yx = lax.rem(y * 2 + x + 4 - yx, 4)
        back_z = lax.rem(z + 4 - zz, 4)
        slot = back_yx * 4 + back_z
        src = gs.at[yx, zz // 2, :, pl.ds((zz % 2) * span, span)]
        copy = remote(src, rb.at[slot], us.at[yx, zz], ur.at[slot], (yx * 2 + c, zz))
        return copy, slot

    def spread_out(yx):
        core_move(yx).wait_recv()
        for g in range(2):
            gs[yx, g] = (
                g16[yx // 2, yx % 2, c, g].astype(jnp.float32) + gc[yx, g].astype(jnp.float32)
            ).astype(jnp.bfloat16)
        for zz in range(4):
            copy, slot = owner_move(yx, zz)

            @pl.when(slot != 0)
            def _():
                copy.start()

            @pl.when(slot == 0)
            def _():
                rb[0] = gs[yx, zz // 2, :, pl.ds((zz % 2) * span, span)]

    core_move(3).start()
    core_move(2).start()

    group_ref(6)[...] = t_dot(smalls[THR_UP], n2[...]).astype(jnp.bfloat16)
    acc[...] += dot(smalls[LOW_DOWN], group(15))

    def second_back(at):
        grad = dn[at] + dot(smalls[THR_UP, at], group(6))
        value = dyb[at].astype(jnp.float32) + norm_back(
            mid[at], g2_ref[...].reshape(1, width), grad
        )
        dn[at] = value
        dbr[at] = value.astype(jnp.bfloat16)

    tiles(second_back)
    for f in range(2):
        own, other = halves(f)
        osend[f, pl.ds(0, HALF_PITCH)] = acc[other].astype(jnp.bfloat16)
    act_move.start()
    smalls[THR_OUT] = low(dot_t(dbr[...], group(5)))
    group_ref(5)[...] = t_dot(smalls[LOW_OUT], dbr[...]).astype(jnp.bfloat16)
    for r in range(2):
        for k in range(4):
            dpj[r, k, :, 0:local] = jnp.zeros((2 * HALF_SLOT, local), jnp.bfloat16)
            for f in range(2):
                dpj[r, k, pl.ds(f * HALF_SLOT + 96, 16)] = jnp.zeros((16, width), jnp.bfloat16)

    spread_out(3)
    spread_out(2)
    group_ref(4)[...] = jnp.concatenate(
        [t_dot(smalls[THR_OUT], att[k]).astype(jnp.bfloat16) for k in range(4)], axis=1
    )
    core_move(1).start()

    @pl.loop(0, 4)
    def _(zk):
        block = attn_block(zk)
        d_att = (dot(dbr[...], block[:, :local]) + dot(smalls[THR_OUT], ao[zk])).astype(
            jnp.bfloat16
        )
        buf[0, :, 0:local] = d_att

        @pl.when(zk == 1)
        def _():
            spread_out(1)

        for f in range(2):
            at = pl.ds(f * frame_rows, frame_rows)
            for head in range(3):
                first = local + head * HEAD
                q = proj[zk, at, first : first + HEAD]
                k = proj[zk, at, first + local : first + local + HEAD]
                v = proj[zk, at, first + 2 * local : first + 2 * local + HEAD]
                d_out = buf[0, at, head * HEAD : (head + 1) * HEAD]
                weights = soft[zk, f * 3 + head]
                d_values = dot(weights, d_out)
                d_soft = dot_t(v, d_out)
                wide = weights.astype(jnp.float32)
                inner = jnp.sum(wide * d_soft, axis=0, keepdims=True)
                d_scores = (wide * (d_soft - inner)).astype(jnp.bfloat16)
                d_keys = dot(d_scores, q) * scale
                d_queries = t_dot(k, d_scores).T * scale
                for r in range(2):
                    to = pl.ds(f * HALF_SLOT, HALF_PITCH)
                    cut = slice(r * HALF_PITCH, (r + 1) * HALF_PITCH)
                    dpj[r, zk, to, first : first + HEAD] = d_queries[cut].astype(jnp.bfloat16)
                    dpj[r, zk, to, first + local : first + local + HEAD] = d_keys[cut].astype(
                        jnp.bfloat16
                    )
                    dpj[r, zk, to, first + 2 * local : first + 2 * local + HEAD] = d_values[
                        cut
                    ].astype(jnp.bfloat16)

    half_rows = 2 * HALF_SLOT
    half_mask = (
        lax.broadcasted_iota(jnp.int32, (half_rows, 32), 0) // HALF_SLOT
        == lax.broadcasted_iota(jnp.int32, (half_rows, 32), 1) // RANK
    )

    def half_at(f, r):
        return pl.ds(pl.multiple_of(f * frame_rows + r * HALF_PITCH, 8), HALF_PITCH)

    def half_products(r, out):
        grad = dot_t(dpj[r, 0], attn_block(0))
        back = dot_t(dpj[r, 0], bq[0])
        for k in range(1, 4):
            grad = grad + dot_t(dpj[r, k], attn_block(k))
            back = back + dot_t(dpj[r, k], bq[k])
        back = jnp.where(half_mask, back, 0.0)
        for f in range(2):
            thr[half_at(f, r)] = back[f * HALF_SLOT : f * HALF_SLOT + HALF_PITCH]
        out[0:half_rows] = grad + dot(back.astype(jnp.bfloat16), group(0))

    def half_back(f, r, products):
        at = half_at(f, r)
        grad = products[f * HALF_SLOT : f * HALF_SLOT + HALF_PITCH]
        value = dn[at] + norm_back(xf[at], g1_ref[...].reshape(1, width), grad)
        return value.astype(jnp.bfloat16)

    half_products(1 - h, tmp)
    isend[0, pl.ds(0, HALF_PITCH)] = half_back(0, 1 - h, tmp)
    ing_moves[0].start()
    half_products(h, mid)
    smalls[THR_QKV] = thr[...].astype(jnp.bfloat16)
    group_ref(0)[...] = t_dot(smalls[THR_QKV], n1[...]).astype(jnp.bfloat16)
    parts = [
        (t_dot(lqh[0], dpj[0, k]) + t_dot(lqh[1], dpj[1, k])).astype(jnp.bfloat16)
        for k in range(4)
    ]
    for i in range(3):
        first = (1 + i) * local
        group_ref(1 + i)[...] = jnp.concatenate(
            [parts[k][:, first : first + local] for k in range(4)], axis=1
        )
    core_move(0).start()
    isend[1, pl.ds(0, HALF_PITCH)] = half_back(1, 1 - h, tmp)
    spread_out(0)
    ing_moves[1].start()
    own_ing[0] = half_back(0, h, mid)
    own_ing[1] = half_back(1, h, mid)

    for f in range(2):
        own_act[f] = acc[halves(f)[0]].astype(jnp.bfloat16)
    act_move.wait_recv()
    give(act_ref, own_act, orecv)

    for slot in range(1, 16):
        remote(rb.at[slot], rb.at[slot], us.at[0, 0], ur.at[slot], (dp, zp)).wait_recv()
    for parity in range(2):
        total = jnp.zeros((32, span), jnp.float32)
        for slot in range(16):
            if slot % 2 == parity:
                total = total + rb[slot].astype(jnp.float32)
        first = lax.rem(h + parity, 2)
        for a in range(table_ref.shape[0] // RANK):
            chosen = [
                jnp.where(
                    jnp.full((RANK, span), clip_ref[2 * first + i]) == a,
                    total[i * RANK : (i + 1) * RANK],
                    0.0,
                )
                for i in range(2)
            ]
            gr_ref[first, pl.ds(a * RANK, RANK)] = chosen[0] + chosen[1]
    for yx in range(4):
        core_move(yx).wait_send()
        for zz in range(4):
            copy, slot = owner_move(yx, zz)

            @pl.when(slot != 0)
            def _():
                copy.wait_send()

    tok_move.wait_send()
    cot_move.wait_send()
    for j in range(1, 4):
        ad_move(j).wait_send()

    for q in (1, 2, 3, 6, 7, 8, 9, 10, 11):
        z_move(q).wait_send()
    for q in range(4):
        for what in range(9):
            move(q, what).wait_send()

    @pl.loop(4, 12)
    def _(q):
        for what in range(9):
            move(q, what).wait_send()

    for what in range(9):
        move(None, what).wait_send()
    act_move.wait_send()
    for f in range(2):
        ing_moves[f].wait()
    give(ing_ref, own_ing, irecv)


def finish_kernel(
    act_ref, ing_ref, gr_ref, table_ref, one_ref, two_ref, act_out, ing_out, *outs
):
    act_out[...] = act_ref[...]
    ing_out[...] = ing_ref[...]
    results = adam(gr_ref[0] + gr_ref[1], table_ref[...], one_ref[...], two_ref[...])
    for out, result in zip(outs, results):
        out[...] = result


def fused(
    tokens,
    cotangent,
    clip_adapter,
    gain_one,
    gain_two,
    w_qkv,
    w_out,
    w_up,
    w_down,
    adapters,
    moment_one,
    moment_two,
):
    micro_count, shard_rows, width = tokens.shape
    rank_all, span = adapters.shape
    rows = 4 * HALF_PITCH
    frame_rows = 2 * HALF_PITCH
    local = width // 4
    bf, f32 = jnp.bfloat16, jnp.float32
    vmem = pl.BlockSpec(memory_space=pltpu.VMEM)
    smem = pl.BlockSpec(memory_space=pltpu.SMEM)
    scratch = [
        pltpu.VMEM((4, 3, 2, 2, 2, 96, width), bf),
        pltpu.VMEM((2, 2, 2, 2, 32, width), bf),
        pltpu.VMEM((4, HALF_SLOT, width), bf),
        pltpu.VMEM((4, HALF_SLOT, width), bf),
        pltpu.VMEM((2, HALF_SLOT, width), bf),
        pltpu.VMEM((2, HALF_SLOT, width), bf),
        pltpu.VMEM((rows, width), f32),
        pltpu.VMEM((rows, width), bf),
        pltpu.VMEM((rows, width), bf),
        pltpu.VMEM((rows, width), bf),
        pltpu.VMEM((4, rows, width), bf),
        pltpu.VMEM((4, 6, frame_rows, frame_rows), bf),
        pltpu.VMEM((4, rows, local), bf),
        pltpu.VMEM((rows, width), f32),
        pltpu.VMEM((rows, width), f32),
        pltpu.VMEM((rows, width), f32),
        pltpu.VMEM((rows, width), f32),
        pltpu.VMEM((2, rows, width), bf),
        pltpu.VMEM((rows, width), bf),
        pltpu.VMEM((2, 4, 2 * HALF_SLOT, width), bf),
        pltpu.VMEM((2, 2 * HALF_SLOT, 32), bf),
        pltpu.VMEM((rows, 32), f32),
        pltpu.VMEM((4, 32, width), bf),
        pltpu.VMEM((4, 32, local), bf),
        pltpu.VMEM((4, 32, width), bf),
        pltpu.VMEM((4, 32, width), bf),
        pltpu.VMEM((2, 2, 2, 2, 32, width), bf),
        pltpu.VMEM((4, 2, 32, width), bf),
        pltpu.VMEM((4, 2, 32, width), bf),
        pltpu.VMEM((16, 32, span), bf),
        pltpu.VMEM((2, HALF_SLOT, width), bf),
        pltpu.VMEM((2, HALF_SLOT, width), bf),
        pltpu.VMEM((2, HALF_PITCH, width), bf),
        pltpu.VMEM((2, HALF_PITCH, width), bf),
        pltpu.VMEM((2, HALF_SLOT, width), bf),
        pltpu.VMEM((2, HALF_SLOT, width), bf),
        pltpu.VMEM((2, 32, span), bf),
        pltpu.VMEM((8, rows, 32), bf),
        pltpu.SemaphoreType.DMA((3, 4)),
        pltpu.SemaphoreType.DMA((3, 4)),
        pltpu.SemaphoreType.DMA((4,)),
        pltpu.SemaphoreType.DMA((4,)),
        pltpu.SemaphoreType.DMA((13, 9)),
        pltpu.SemaphoreType.DMA((13, 9)),
        pltpu.SemaphoreType.DMA((5,)),
        pltpu.SemaphoreType.DMA((5,)),
        pltpu.SemaphoreType.DMA((4,)),
        pltpu.SemaphoreType.DMA((4,)),
        pltpu.SemaphoreType.DMA((4, 4)),
        pltpu.SemaphoreType.DMA((16,)),
    ]
    act, ing, grads = pl.pallas_call(
        fused_kernel,
        out_shape=(
            jax.ShapeDtypeStruct((shard_rows, micro_count, width), bf),
            jax.ShapeDtypeStruct((shard_rows, micro_count, width), bf),
            jax.ShapeDtypeStruct((2, rank_all, span), f32),
        ),
        in_specs=[vmem] * 9 + [smem],
        out_specs=(vmem, vmem, vmem),
        scratch_shapes=scratch,
        compiler_params=pltpu.CompilerParams(
            collective_id=0, has_side_effects=True, vmem_limit_bytes=60 * 2**20
        ),
    )(
        tokens.transpose(1, 0, 2),
        cotangent.transpose(1, 0, 2),
        gain_one,
        gain_two,
        w_qkv.transpose(1, 0, 2),
        w_out,
        w_up,
        w_down.T,
        adapters,
        clip_adapter,
    )
    plain = jax.ShapeDtypeStruct((rank_all, span), f32)
    rows_spec = pl.BlockSpec((shard_rows // 2, micro_count, width), lambda i: (i, 0, 0))
    plain_spec = pl.BlockSpec((rank_all // 2, span), lambda i: (i, 0))
    act, ing, *others = pl.pallas_call(
        finish_kernel,
        out_shape=(act, ing) + (plain,) * 4 + (jax.ShapeDtypeStruct((rank_all, span), bf),),
        grid=(2,),
        in_specs=[rows_spec] * 2
        + [pl.BlockSpec((2, rank_all // 2, span), lambda i: (0, i, 0))]
        + [plain_spec] * 3,
        out_specs=(rows_spec,) * 2 + (plain_spec,) * 5,
    )(act, ing, grads, adapters, moment_one, moment_two)
    return (act.transpose(1, 0, 2), ing.transpose(1, 0, 2), *others)


def layer(tokens, *others):
    w_up = others[6]
    sizes = lax.axis_size("dp"), lax.axis_size("mp")
    frames_micro = tokens.shape[1] * sizes[0] * sizes[1] // FRAME
    fits = (
        sizes == (8, 4)
        and tokens.shape[0] == 4
        and 2 * tokens.shape[1] == FRAME
        and frames_micro == CLIP_FRAMES
        and w_up.shape == (tokens.shape[2] // 8, tokens.shape[2])
    )
    return (fused if fits else shards)(tokens, *others)


def solution(mesh):
    spread = P(None, ("dp", "mp"))
    rows = P(None, ("dp", "mp"), None)
    return jax.shard_map(
        layer,
        mesh=mesh,
        in_specs=(
            rows,
            rows,
            P(),
            P(),
            P(),
            P("dp", None, "mp"),
            P("mp", "dp"),
            P("dp", "mp"),
            P("mp", "dp"),
            spread,
            spread,
            spread,
        ),
        out_specs=(rows, rows, spread, spread, spread, spread, spread),
        check_vma=False,
    )
```

```python
import functools
import math

import jax
import jax.numpy as jnp
from jax import lax
from jax.experimental import pallas as pl
from jax.experimental.pallas import tpu as pltpu
from jax.sharding import PartitionSpec as P

HEAD = 64
FRAME = 196
RANK = 16
CLIP_FRAMES = 16
STEP = 5

norm_epsilon = 1e-06
beta_first = 0.5
beta_second = 0.5
learn_rate = 0.05
weight_decay = 0.01
adam_epsilon = 1e-08


def dot(left, right):
    return jnp.dot(left, right, preferred_element_type=jnp.float32)


def dot_t(left, right):
    return lax.dot_general(left, right, (((1,), (1,)), ((), ())), preferred_element_type=jnp.float32)


def t_dot(left, right):
    return lax.dot_general(left, right, (((0,), (0,)), ((), ())), preferred_element_type=jnp.float32)


def half(values):
    return values.astype(jnp.bfloat16)


def norm_parts(values):
    center = values - jnp.mean(values, axis=-1, keepdims=True)
    spread = jnp.mean(center * center, axis=-1, keepdims=True)
    inverse = lax.rsqrt(spread + norm_epsilon)
    return center * inverse, inverse


def norm_back(unit, inverse, gain, grad):
    scaled = grad * gain
    first = jnp.mean(scaled, axis=-1, keepdims=True)
    second = jnp.mean(scaled * unit, axis=-1, keepdims=True)
    return inverse * (scaled - first - unit * second)


def adam(owner_grad, adapters, moment_one, moment_two):
    first_moment = beta_first * moment_one + (1.0 - beta_first) * owner_grad
    second_moment = beta_second * moment_two + (1.0 - beta_second) * owner_grad * owner_grad
    first_hat = first_moment / (1.0 - beta_first**STEP)
    second_hat = second_moment / (1.0 - beta_second**STEP)
    updated = adapters - learn_rate * (
        first_hat / (jnp.sqrt(second_hat) + adam_epsilon) + weight_decay * adapters
    )
    return (
        owner_grad,
        updated,
        first_moment,
        second_moment,
        updated.astype(jnp.bfloat16),
    )


def shards(
    tokens,
    cotangent,
    clip_adapter,
    gain_one,
    gain_two,
    w_qkv,
    w_out,
    w_up,
    w_down,
    adapters,
    moment_one,
    moment_two,
):
    groups = lax.axis_size("mp")
    member = lax.axis_index("mp")
    group_index = lax.axis_index("dp")
    micro_count, shard_rows, width = tokens.shape
    hidden_width = w_up.shape[1] * groups
    heads = width // HEAD
    rank_all = adapters.shape[0]
    full_width = adapters.shape[1] * lax.axis_size(("dp", "mp"))
    frames = shard_rows * groups // FRAME
    frames_micro = frames * lax.axis_size("dp")
    scale = 1.0 / math.sqrt(HEAD)
    span = FRAME // shard_rows
    mine = micro_count // span
    part = member % span
    pairs = [[first * span + k for k in range(span)] for first in range(groups // span)]

    def swap(rows):
        return lax.all_to_all(
            rows, "mp", split_axis=0, concat_axis=1, axis_index_groups=pairs, tiled=True
        ).reshape(mine * FRAME, width)

    def swap_back(rows):
        return lax.all_to_all(
            rows.reshape(mine, FRAME, width),
            "mp",
            split_axis=1,
            concat_axis=0,
            axis_index_groups=pairs,
            tiled=True,
        )

    inputs = swap(tokens).astype(jnp.float32)
    dy = swap(cotangent)

    def whole(weight, first, second):
        return lax.all_gather(
            lax.all_gather(weight, first[0], axis=first[1], tiled=True),
            second[0],
            axis=second[1],
            tiled=True,
        )

    qkv_all = whole(w_qkv, ("dp", 0), ("mp", 2)).reshape(width, 3 * width)
    out_all = whole(w_out, ("dp", 1), ("mp", 0))
    up_all = whole(w_up, ("dp", 0), ("mp", 1))
    down_all = whole(w_down, ("dp", 1), ("mp", 0))
    table = lax.all_gather(half(adapters), ("dp", "mp"), axis=1, tiled=True)
    table = table.reshape(rank_all // RANK, RANK, full_width)
    clips = jnp.stack(
        [
            ((part * mine + i) * frames_micro + group_index * frames + member // span)
            // CLIP_FRAMES
            for i in range(mine)
        ]
    )
    chosen = clip_adapter[clips]
    own = table[chosen].reshape(mine * RANK, full_width)
    ends = [0, width, 4 * width, 5 * width, 6 * width, 7 * width]
    ends += [7 * width + hidden_width, 7 * width + 2 * hidden_width, full_width]
    a_qkv, b_qkv, a_out, b_out, a_up, b_up, a_down, b_down = [
        own[:, ends[i] : ends[i + 1]] for i in range(8)
    ]
    rows = mine * FRAME
    row_frame = lax.broadcasted_iota(jnp.int32, (rows, mine * RANK), 0) // FRAME
    column_frame = lax.broadcasted_iota(jnp.int32, (rows, mine * RANK), 1) // RANK
    mask = row_frame == column_frame

    def low(values):
        return half(jnp.where(mask, values, 0.0))

    shape_heads = (mine, FRAME, heads, HEAD)
    unit_one, inverse_one = norm_parts(inputs)
    normed_one = half(unit_one * gain_one)
    low_qkv = low(dot_t(normed_one, a_qkv))
    projected = half(dot(normed_one, qkv_all) + dot(low_qkv, b_qkv))
    queries = projected[:, 0:width].reshape(shape_heads)
    keys = projected[:, width : 2 * width].reshape(shape_heads)
    values = projected[:, 2 * width :].reshape(shape_heads)
    scores = jnp.einsum("fqhd,fkhd->fhqk", queries, keys, preferred_element_type=jnp.float32)
    scores = scores * scale
    exponent = jnp.exp(scores - jnp.max(scores, axis=-1, keepdims=True))
    soft = exponent / jnp.sum(exponent, axis=-1, keepdims=True)
    soft_half = half(soft)
    attended = half(
        jnp.einsum("fhqk,fkhd->fqhd", soft_half, values, preferred_element_type=jnp.float32)
    ).reshape(rows, width)
    low_out = low(dot_t(attended, a_out))
    middle = inputs + dot(attended, out_all) + dot(low_out, b_out)
    unit_two, inverse_two = norm_parts(middle)
    normed_two = half(unit_two * gain_two)
    low_up = low(dot_t(normed_two, a_up))
    hidden = dot(normed_two, up_all) + dot(low_up, b_up)
    phi = 0.5 * (1.0 + lax.erf(hidden * math.sqrt(0.5)))
    active = half(hidden * phi)
    slope = phi + hidden * jnp.exp(-0.5 * hidden * hidden) * (1.0 / math.sqrt(2.0 * math.pi))
    low_down = low(dot_t(active, a_down))
    outputs = half(middle + dot(active, down_all) + dot(low_down, b_down))

    through_down = low(dot_t(dy, b_down))
    d_active = dot_t(dy, down_all) + dot(through_down, a_down)
    d_hidden = half(d_active * slope)
    through_up = low(dot_t(d_hidden, b_up))
    d_normed_two = dot_t(d_hidden, up_all) + dot(through_up, a_up)
    d_middle = dy.astype(jnp.float32) + norm_back(unit_two, inverse_two, gain_two, d_normed_two)
    d_branch = half(d_middle)
    through_out = low(dot_t(d_branch, b_out))
    d_attended = half(dot_t(d_branch, out_all) + dot(through_out, a_out))
    d_heads = d_attended.reshape(shape_heads)
    d_values = jnp.einsum("fhqk,fqhd->fkhd", soft_half, d_heads, preferred_element_type=jnp.float32)
    d_soft = jnp.einsum("fqhd,fkhd->fhqk", d_heads, values, preferred_element_type=jnp.float32)
    inner = jnp.sum(soft * d_soft, axis=-1, keepdims=True)
    d_scores = half(soft * (d_soft - inner))
    d_queries = scale * jnp.einsum(
        "fhqk,fkhd->fqhd", d_scores, keys, preferred_element_type=jnp.float32
    )
    d_keys = scale * jnp.einsum(
        "fhqk,fqhd->fkhd", d_scores, queries, preferred_element_type=jnp.float32
    )
    d_projected = half(
        jnp.concatenate([d.reshape(rows, width) for d in (d_queries, d_keys, d_values)], axis=1)
    )
    through_qkv = low(dot_t(d_projected, b_qkv))
    d_normed_one = dot_t(d_projected, qkv_all) + dot(through_qkv, a_qkv)
    input_grad = half(d_middle + norm_back(unit_one, inverse_one, gain_one, d_normed_one))
    grads = half(jnp.concatenate(
        [
            t_dot(through_qkv, normed_one),
            t_dot(low_qkv, d_projected),
            t_dot(through_out, attended),
            t_dot(low_out, d_branch),
            t_dot(through_up, normed_two),
            t_dot(low_up, d_hidden),
            t_dot(through_down, active),
            t_dot(low_down, dy),
        ],
        axis=1,
    ))
    pick = (
        lax.broadcasted_iota(jnp.int32, (rank_all, mine * RANK), 0)
        == jnp.repeat(chosen, RANK)[None, :] * RANK
        + lax.broadcasted_iota(jnp.int32, (rank_all, mine * RANK), 1) % RANK
    ).astype(jnp.bfloat16)
    owner_grad = lax.psum_scatter(
        dot(pick, grads), ("dp", "mp"), scatter_dimension=1, tiled=True
    )
    return (swap_back(outputs), swap_back(input_grad)) + adam(
        owner_grad, adapters, moment_one, moment_two
    )


MESH = pl.DeviceIdType.MESH
X1, Y1, Y2, X2, C0, C1A, C1B, C2A, C2B = range(9)
HALF_PITCH = 104
HALF_SLOT = 112


def fused_kernel(
    tok_ref,
    cot_ref,
    g1_ref,
    g2_ref,
    wq_ref,
    wo_ref,
    wu_ref,
    wd_ref,
    table_ref,
    clip_ref,
    act_ref,
    ing_ref,
    gr_ref,
    w,
    ad,
    ts,
    cs,
    tr,
    cr,
    xf,
    dyb,
    n1,
    n2,
    proj,
    soft,
    att,
    mid,
    acc,
    dn,
    tmp,
    buf,
    dbr,
    dpj,
    lqh,
    thr,
    bq,
    ao,
    bu,
    an,
    g16,
    gc,
    gs,
    rb,
    osend,
    isend,
    own_act,
    own_ing,
    orecv,
    irecv,
    adp,
    smalls,
    zs,
    zr,
    azs,
    azr,
    ss,
    rs,
    ps,
    pr,
    cxs,
    cxr,
    us,
    ur,
):
    dp = lax.axis_index("dp")
    z = lax.axis_index("mp")
    y = dp // 4
    x = lax.rem(dp // 2, 2)
    c = lax.rem(dp, 2)
    h = lax.rem(z, 2)
    zp = z + 1 - 2 * h
    zn = 4
    shard_rows = tok_ref.shape[0]
    rows = xf.shape[0]
    frame_rows = rows // 2
    width = xf.shape[1]
    local = width // zn
    scale = 1.0 / math.sqrt(HEAD)

    def place(yy, xx, cc, zz):
        return ((yy * 2 + xx) * 2 + cc, zz)

    def order(at_z, k):
        upper = at_z // 2
        near = at_z + upper * (3 - 2 * at_z)
        swapped = jnp.where((near == 1) & (k < 2), 1 - k, k)
        return swapped + upper * (3 - 2 * swapped)

    def rank_of(at_z, block_z):
        upper = at_z // 2
        near = at_z + upper * (3 - 2 * at_z)
        mirrored = block_z + upper * (3 - 2 * block_z)
        return jnp.where((near == 1) & (mirrored < 2), 1 - mirrored, mirrored)

    barrier = pltpu.get_barrier_semaphore()
    for k in range(1, 16):
        yx = lax.rem(y * 2 + x + k // 4, 4)
        target = (yx * 2 + c, lax.rem(z + k % 4, 4))
        pl.semaphore_signal(barrier, inc=1, device_id=target, device_id_type=MESH)
    pl.semaphore_signal(barrier, inc=1, device_id=place(y, x, 1 - c, z), device_id_type=MESH)

    def remote(src, dst, send, recv, target):
        return pltpu.make_async_remote_copy(
            src_ref=src,
            dst_ref=dst,
            send_sem=send,
            recv_sem=recv,
            device_id=target,
            device_id_type=MESH,
        )

    w[z, 0, y, x, c] = jnp.concatenate([wo_ref[...].T] + [wq_ref[i] for i in range(3)], axis=1)
    span = table_ref.shape[1]
    low_columns = pl.ds(pl.multiple_of(lax.rem(z, 2) * span, 128), span)
    for m in range(4):
        clip = jnp.full((RANK, span), clip_ref[m])
        chosen = jnp.zeros((RANK, span), jnp.float32)
        for a in range(table_ref.shape[0] // RANK):
            chosen = jnp.where(clip == a, table_ref[a * RANK : (a + 1) * RANK], chosen)
        adp[m // 2, pl.ds((m % 2) * RANK, RANK)] = chosen.astype(jnp.bfloat16)
    ad[y, x, c, z // 2, :, low_columns] = adp[h]

    def stage(dst, src):
        for m in range(4):
            dst[m, pl.ds(96, 16)] = jnp.zeros((16, width), jnp.bfloat16)
            dst[m, pl.ds(0, shard_rows)] = src[:, m, :]

    def part(kind, zk, yy, xx, cc, first, count):
        return w.at[zk, kind, yy, xx, cc, pl.ds(first, count), :]

    def phase(q):
        if isinstance(q, int):
            return (0, q) if q < 4 else (1 + q % 2, (q - 4) // 2)
        return 1 + lax.rem(q, 2), (q - 4) // 2

    def move(q, what):
        full = 32 if q is None else 96
        n = full // 2
        every = pl.ds(0, 2)
        args, target = {
            X1: ((y, x, c, 0, n), (y, 1 - x, c)),
            Y1: ((y, x, c, n, n), (1 - y, x, c)),
            Y2: ((y, every, c, 0, n), (1 - y, x, c)),
            X2: ((every, x, c, n, n), (y, 1 - x, c)),
            C0: ((y, x, c, 0, full), (y, x, 1 - c)),
            C1A: ((y, 1 - x, c, 0, n), (y, x, 1 - c)),
            C1B: ((1 - y, x, c, n, n), (y, x, 1 - c)),
            C2A: ((1 - y, every, c, 0, n), (y, x, 1 - c)),
            C2B: ((every, 1 - x, c, n, n), (y, x, 1 - c)),
        }[what]
        if q is None:
            yy, xx, cc, first, count = args
            ref = ad.at[yy, xx, cc, :, pl.ds(first, count), :]
            index = 12
        else:
            kind, k = phase(q)
            ref = part(kind, order(z, k), *args)
            index = q
        return remote(ref, ref, ss.at[index, what], rs.at[index, what], place(*target, z))

    def z_move(q):
        kind, k = phase(q)
        ref = part(kind, z, y, x, c, 0, 96)
        other = order(z, k)
        return remote(ref, ref, zs.at[kind, k], zr.at[kind, rank_of(other, z)], (dp, other))

    def z_wait(q):
        kind, k = phase(q)
        ref = part(kind, z, y, x, c, 0, 96)
        remote(ref, ref, zs.at[kind, k], zr.at[kind, k], (dp, zp)).wait_recv()

    def ad_move(j):
        other = lax.rem(z + zn - j, zn)
        dst = ad.at[y, x, c, z // 2, :, low_columns]
        return remote(adp.at[lax.rem(other, 2)], dst, azs.at[j], azr.at[j], (dp, other))

    def t1(q):
        if isinstance(q, int):
            if q is not None and phase(q)[1]:
                z_wait(q)
        elif q is not None:
            z_wait(q)
        for what in (X1, Y1, C0):
            move(q, what).start()

    def t2(q):
        move(q, X1).wait_recv()
        move(q, Y2).start()
        move(q, Y1).wait_recv()
        move(q, X2).start()
        move(q, C1A).start()
        move(q, C1B).start()

    def t3(q):
        move(q, Y2).wait_recv()
        move(q, C2A).start()
        move(q, X2).wait_recv()
        move(q, C2B).start()

    def ready(q):
        for what in (C0, C1A, C1B, C2A, C2B):
            move(q, what).wait_recv()

    tok_move = remote(
        ts.at[pl.ds(2 - 2 * h, 2)], tr, ps.at[0], pr.at[0], (dp, zp)
    )
    cot_move = remote(
        cs.at[pl.ds(2 - 2 * h, 2)], cr, ps.at[1], pr.at[1], (dp, zp)
    )
    act_move = remote(
        osend, orecv, ps.at[2], pr.at[2], (dp, zp)
    )
    ing_moves = [
        remote(isend.at[f], irecv.at[f], ps.at[3 + f], pr.at[3 + f], (dp, zp)) for f in range(2)
    ]

    pl.semaphore_wait(barrier, 16)
    t1(0)
    for j in range(1, 4):
        ad_move(j).start()
    z_move(1).start()
    w[z, 1, y, x, c] = wu_ref[...]
    t1(4)
    stage(ts, tok_ref)
    tok_move.start()
    z_move(2).start()
    z_move(3).start()
    w[z, 2, y, x, c] = wd_ref[...]
    t2(0)
    t1(1)
    for j in range(1, 4):
        ad_move(j).wait_recv()
    t1(None)
    t2(1)
    t1(2)
    t2(None)
    t3(0)
    z_move(6).start()
    z_move(7).start()
    t2(2)
    t1(3)
    t3(1)
    t3(None)
    t2(3)
    t2(4)
    t3(2)
    z_move(8).start()
    z_move(9).start()
    t1(5)
    t3(3)
    z_move(10).start()
    z_move(11).start()

    def dot(left, right):
        return jnp.dot(left, right, preferred_element_type=jnp.float32)

    def dot_t(left, right):
        return lax.dot_general(
            left, right, (((1,), (1,)), ((), ())), preferred_element_type=jnp.float32
        )

    def t_dot(left, right):
        return lax.dot_general(
            left, right, (((0,), (0,)), ((), ())), preferred_element_type=jnp.float32
        )

    row_frame = lax.broadcasted_iota(jnp.int32, (rows, 32), 0) // frame_rows
    column_frame = lax.broadcasted_iota(jnp.int32, (rows, 32), 1) // RANK
    mask = row_frame == column_frame

    def low(values):
        return jnp.where(mask, values, 0.0).astype(jnp.bfloat16)

    def tiles(body, step=416):
        @pl.loop(0, rows // step)
        def _(t):
            body(pl.ds(pl.multiple_of(t * step, step), step))

    def norm_parts(values):
        center = values - jnp.mean(values, axis=-1, keepdims=True)
        spread = jnp.mean(center * center, axis=-1, keepdims=True)
        inverse = lax.rsqrt(spread + norm_epsilon)
        return center * inverse, inverse

    def norm_back(values, gain, grad):
        unit, inverse = norm_parts(values)
        scaled = grad * gain
        first = jnp.mean(scaled, axis=-1, keepdims=True)
        second = jnp.mean(scaled * unit, axis=-1, keepdims=True)
        return inverse * (scaled - first - unit * second)

    def group(g):
        return ad[g // 8, (g // 4) % 2, (g // 2) % 2, g % 2]

    def group_ref(g):
        return g16.at[g // 8, (g // 4) % 2, (g // 2) % 2, g % 2]

    def attn_block(zk):
        return w[zk, 0].reshape(width, width)

    def halves(f):
        own = pl.ds(pl.multiple_of(f * frame_rows + h * HALF_PITCH, 8), HALF_PITCH)
        other = pl.ds(pl.multiple_of(f * frame_rows + (1 - h) * HALF_PITCH, 8), HALF_PITCH)
        return own, other

    def join(dst, own_slots, other_slots):
        for f in range(2):
            own, other = halves(f)
            dst[own] = own_slots[2 * h + f][:HALF_PITCH].astype(jnp.float32)
            dst[other] = other_slots[f][:HALF_PITCH].astype(jnp.float32)

    def give(dst, own, received):
        for f in range(2):
            first, second = own[f, pl.ds(0, shard_rows)], received[f, pl.ds(0, shard_rows)]
            dst[:, f, :] = jnp.where(h == 0, first, second)
            dst[:, 2 + f, :] = jnp.where(h == 0, second, first)

    tok_move.wait_recv()
    join(xf, ts, tr)

    def first_norm(at):
        values = xf[at]
        unit, _ = norm_parts(values)
        n1[at] = (unit * g1_ref[...].reshape(1, width)).astype(jnp.bfloat16)
        mid[at] = values

    tiles(first_norm)
    ready(None)
    for k in range(4):
        bq[k] = jnp.concatenate(
            [jnp.zeros((32, local), jnp.bfloat16)]
            + [group(1 + i)[:, k * local : (k + 1) * local] for i in range(3)],
            axis=1,
        )
        ao[k] = group(4)[:, k * local : (k + 1) * local]
        bu[k] = group(7 + k)
        an[k] = group(11 + k)
    low_wide = jnp.where(mask, dot_t(n1[...], group(0)), 0.0)
    smalls[0] = low_wide.astype(jnp.bfloat16)
    lqh[...] = jnp.zeros_like(lqh)
    for r in range(2):
        for f in range(2):
            first = f * frame_rows + r * HALF_PITCH
            lqh[r, pl.ds(f * HALF_SLOT, HALF_PITCH)] = low_wide[
                first : first + HALF_PITCH
            ].astype(jnp.bfloat16)
    key_pad = (
        lax.rem(lax.broadcasted_iota(jnp.int32, (frame_rows, 1), 0), HALF_PITCH) >= shard_rows
    )
    bias = jnp.where(key_pad, -1e30, 0.0).astype(jnp.float32)

    LOW_QKV, LOW_OUT, LOW_UP, LOW_DOWN, THR_DOWN, THR_UP, THR_OUT, THR_QKV = range(8)

    def attention(i, out_low):
        zk = order(z, i)
        block = attn_block(zk)
        proj[zk] = (dot(n1[...], block) + dot(smalls[LOW_QKV], bq[zk])).astype(jnp.bfloat16)
        for f in range(2):
            at = pl.ds(f * frame_rows, frame_rows)
            for head in range(3):
                first = local + head * HEAD
                q = proj[zk, at, first : first + HEAD]
                k = proj[zk, at, first + local : first + local + HEAD]
                v = proj[zk, at, first + 2 * local : first + 2 * local + HEAD]
                scores = dot_t(k, q) * scale + bias
                exponent = jnp.exp(scores - jnp.max(scores, axis=0, keepdims=True))
                weights = exponent / jnp.sum(exponent, axis=0, keepdims=True)
                weights = weights.astype(jnp.bfloat16)
                soft[zk, f * 3 + head] = weights
                att[zk, at, head * HEAD : (head + 1) * HEAD] = (
                    t_dot(weights, v).astype(jnp.bfloat16)
                )
        gathered = att[zk]
        mid[...] += dot_t(gathered, block[:, :local])
        return out_low + dot_t(gathered, ao[zk])

    def attention_step(i, out_low):
        @pl.when(i == 0)
        def _():
            stage(cs, cot_ref)
            cot_move.start()

        @pl.when(i == 1)
        def _():
            t1(6)
            t2(5)

        @pl.when(i == 2)
        def _():
            t3(4)

        @pl.when(i == 3)
        def _():
            t1(7)
            t2(6)

        for k in range(4):

            @pl.when(i == k)
            def _():
                ready(k)

        return attention(i, out_low)

    out_low = lax.fori_loop(0, 4, attention_step, jnp.zeros((rows, 32), jnp.float32))
    t3(5)
    ready(4)
    smalls[LOW_OUT] = low(out_low)
    mid[...] += dot(smalls[LOW_OUT], group(5))

    def second_norm(at):
        unit, _ = norm_parts(mid[at])
        n2[at] = (unit * g2_ref[...].reshape(1, width)).astype(jnp.bfloat16)

    tiles(second_norm)
    cot_move.wait_recv()
    join(tmp, cs, cr)
    dyb[...] = tmp[...].astype(jnp.bfloat16)
    smalls[LOW_UP] = low(dot_t(n2[...], group(6)))
    smalls[THR_DOWN] = low(dot_t(dyb[...], group(15)))
    group_ref(15)[...] = jnp.zeros((32, width), jnp.bfloat16)
    t1(8)
    t2(7)
    acc[...] = mid[...]
    dn[...] = jnp.zeros_like(dn)

    def feed(i, lows):
        down_low, up_back = lows
        zk = order(z, i)
        q = 4 + 2 * i

        @pl.when((i > 0) & (i < 3))
        def _():
            t1(q + 3)
            t2(q + 2)

        @pl.when(i > 0)
        def _():
            ready(q)

        tmp[...] = dot(n2[...], w[zk, 1].reshape(width, width)) + dot(smalls[LOW_UP], bu[zk])

        def gate(at):
            hidden = tmp[at]
            phi = 0.5 + 0.5 * lax.erf(hidden * math.sqrt(0.5))
            bell = jnp.exp(-0.5 * hidden * hidden) * (1.0 / math.sqrt(2.0 * math.pi))
            buf[0, at] = (hidden * phi).astype(jnp.bfloat16)
            tmp[at] = phi + hidden * bell

        tiles(gate)
        active = buf[0]
        down_low = down_low + dot_t(active, an[zk])
        ga = 11 + zk
        g16[ga // 8, lax.rem(ga // 4, 2), lax.rem(ga // 2, 2), lax.rem(ga, 2)] = t_dot(
            smalls[THR_DOWN], active
        ).astype(jnp.bfloat16)

        @pl.when(i > 0)
        def _():
            t3(q + 1)

        @pl.when(i == 1)
        def _():
            t1(q + 4)

        @pl.when((i > 0) & (i < 3))
        def _():
            t2(q + 3)

        ready(q + 1)
        down = w[zk, 2].reshape(width, width)
        tmp[...] = tmp[...] * (dot(dyb[...], down) + dot(smalls[THR_DOWN], an[zk]))
        buf[1] = tmp[...].astype(jnp.bfloat16)
        d_hidden = buf[1]
        dn[...] += dot_t(d_hidden, w[zk, 1].reshape(width, width))
        acc[...] += dot_t(active, down)
        gu = 7 + zk
        g16[gu // 8, lax.rem(gu // 4, 2), lax.rem(gu // 2, 2), lax.rem(gu, 2)] = t_dot(
            smalls[LOW_UP], d_hidden
        ).astype(jnp.bfloat16)
        up_back = up_back + dot_t(d_hidden, bu[zk])

        @pl.when(i < 3)
        def _():
            t3(q + 2)

        return down_low, up_back

    empty = jnp.zeros((rows, 32), jnp.float32)
    down_low, up_back = lax.fori_loop(0, 4, feed, (empty, empty))
    smalls[LOW_DOWN] = low(down_low)
    smalls[THR_UP] = low(up_back)
    group_ref(15)[...] = t_dot(smalls[LOW_DOWN], dyb[...]).astype(jnp.bfloat16)

    def core_move(yx):
        src = g16.at[yx // 2, yx % 2, 1 - c]
        return remote(src, gc.at[yx], cxs.at[yx], cxr.at[yx], place(y, x, 1 - c, z))

    def owner_move(yx, zz):
        back_yx = lax.rem(y * 2 + x + 4 - yx, 4)
        back_z = lax.rem(z + 4 - zz, 4)
        slot = back_yx * 4 + back_z
        src = gs.at[yx, zz // 2, :, pl.ds((zz % 2) * span, span)]
        copy = remote(src, rb.at[slot], us.at[yx, zz], ur.at[slot], (yx * 2 + c, zz))
        return copy, slot

    def spread_out(yx):
        core_move(yx).wait_recv()
        for g in range(2):
            gs[yx, g] = (
                g16[yx // 2, yx % 2, c, g].astype(jnp.float32) + gc[yx, g].astype(jnp.float32)
            ).astype(jnp.bfloat16)
        for zz in range(4):
            copy, slot = owner_move(yx, zz)

            @pl.when(slot != 0)
            def _():
                copy.start()

            @pl.when(slot == 0)
            def _():
                rb[0] = gs[yx, zz // 2, :, pl.ds((zz % 2) * span, span)]

    core_move(3).start()
    core_move(2).start()

    group_ref(6)[...] = t_dot(smalls[THR_UP], n2[...]).astype(jnp.bfloat16)
    acc[...] += dot(smalls[LOW_DOWN], group(15))

    def second_back(at):
        grad = dn[at] + dot(smalls[THR_UP, at], group(6))
        value = dyb[at].astype(jnp.float32) + norm_back(
            mid[at], g2_ref[...].reshape(1, width), grad
        )
        dn[at] = value
        dbr[at] = value.astype(jnp.bfloat16)

    tiles(second_back)
    for f in range(2):
        own, other = halves(f)
        osend[f, pl.ds(0, HALF_PITCH)] = acc[other].astype(jnp.bfloat16)
    act_move.start()
    smalls[THR_OUT] = low(dot_t(dbr[...], group(5)))
    group_ref(5)[...] = t_dot(smalls[LOW_OUT], dbr[...]).astype(jnp.bfloat16)
    for r in range(2):
        for k in range(4):
            dpj[r, k, :, 0:local] = jnp.zeros((2 * HALF_SLOT, local), jnp.bfloat16)
            for f in range(2):
                dpj[r, k, pl.ds(f * HALF_SLOT + 96, 16)] = jnp.zeros((16, width), jnp.bfloat16)

    spread_out(3)
    spread_out(2)
    group_ref(4)[...] = jnp.concatenate(
        [t_dot(smalls[THR_OUT], att[k]).astype(jnp.bfloat16) for k in range(4)], axis=1
    )
    core_move(1).start()

    @pl.loop(0, 4)
    def _(zk):
        block = attn_block(zk)
        d_att = (dot(dbr[...], block[:, :local]) + dot(smalls[THR_OUT], ao[zk])).astype(
            jnp.bfloat16
        )
        buf[0, :, 0:local] = d_att

        @pl.when(zk == 1)
        def _():
            spread_out(1)

        for f in range(2):
            at = pl.ds(f * frame_rows, frame_rows)
            for head in range(3):
                first = local + head * HEAD
                q = proj[zk, at, first : first + HEAD]
                k = proj[zk, at, first + local : first + local + HEAD]
                v = proj[zk, at, first + 2 * local : first + 2 * local + HEAD]
                d_out = buf[0, at, head * HEAD : (head + 1) * HEAD]
                weights = soft[zk, f * 3 + head]
                d_values = dot(weights, d_out)
                d_soft = dot_t(v, d_out)
                wide = weights.astype(jnp.float32)
                inner = jnp.sum(wide * d_soft, axis=0, keepdims=True)
                d_scores = (wide * (d_soft - inner)).astype(jnp.bfloat16)
                d_keys = dot(d_scores, q) * scale
                d_queries = t_dot(k, d_scores).T * scale
                for r in range(2):
                    to = pl.ds(f * HALF_SLOT, HALF_PITCH)
                    cut = slice(r * HALF_PITCH, (r + 1) * HALF_PITCH)
                    dpj[r, zk, to, first : first + HEAD] = d_queries[cut].astype(jnp.bfloat16)
                    dpj[r, zk, to, first + local : first + local + HEAD] = d_keys[cut].astype(
                        jnp.bfloat16
                    )
                    dpj[r, zk, to, first + 2 * local : first + 2 * local + HEAD] = d_values[
                        cut
                    ].astype(jnp.bfloat16)

    half_rows = 2 * HALF_SLOT
    half_mask = (
        lax.broadcasted_iota(jnp.int32, (half_rows, 32), 0) // HALF_SLOT
        == lax.broadcasted_iota(jnp.int32, (half_rows, 32), 1) // RANK
    )

    def half_at(f, r):
        return pl.ds(pl.multiple_of(f * frame_rows + r * HALF_PITCH, 8), HALF_PITCH)

    def half_products(r, out):
        grad = dot_t(dpj[r, 0], attn_block(0))
        back = dot_t(dpj[r, 0], bq[0])
        for k in range(1, 4):
            grad = grad + dot_t(dpj[r, k], attn_block(k))
            back = back + dot_t(dpj[r, k], bq[k])
        back = jnp.where(half_mask, back, 0.0)
        for f in range(2):
            thr[half_at(f, r)] = back[f * HALF_SLOT : f * HALF_SLOT + HALF_PITCH]
        out[0:half_rows] = grad + dot(back.astype(jnp.bfloat16), group(0))

    def half_back(f, r, products):
        at = half_at(f, r)
        grad = products[f * HALF_SLOT : f * HALF_SLOT + HALF_PITCH]
        value = dn[at] + norm_back(xf[at], g1_ref[...].reshape(1, width), grad)
        return value.astype(jnp.bfloat16)

    half_products(1 - h, tmp)
    isend[0, pl.ds(0, HALF_PITCH)] = half_back(0, 1 - h, tmp)
    ing_moves[0].start()
    half_products(h, mid)
    smalls[THR_QKV] = thr[...].astype(jnp.bfloat16)
    group_ref(0)[...] = t_dot(smalls[THR_QKV], n1[...]).astype(jnp.bfloat16)
    parts = [
        (t_dot(lqh[0], dpj[0, k]) + t_dot(lqh[1], dpj[1, k])).astype(jnp.bfloat16)
        for k in range(4)
    ]
    for i in range(3):
        first = (1 + i) * local
        group_ref(1 + i)[...] = jnp.concatenate(
            [parts[k][:, first : first + local] for k in range(4)], axis=1
        )
    core_move(0).start()
    isend[1, pl.ds(0, HALF_PITCH)] = half_back(1, 1 - h, tmp)
    spread_out(0)
    ing_moves[1].start()
    own_ing[0] = half_back(0, h, mid)
    own_ing[1] = half_back(1, h, mid)

    for f in range(2):
        own_act[f] = acc[halves(f)[0]].astype(jnp.bfloat16)
    act_move.wait_recv()
    give(act_ref, own_act, orecv)

    for slot in range(1, 16):
        remote(rb.at[slot], rb.at[slot], us.at[0, 0], ur.at[slot], (dp, zp)).wait_recv()
    for parity in range(2):
        total = jnp.zeros((32, span), jnp.float32)
        for slot in range(16):
            if slot % 2 == parity:
                total = total + rb[slot].astype(jnp.float32)
        first = lax.rem(h + parity, 2)
        for a in range(table_ref.shape[0] // RANK):
            chosen = [
                jnp.where(
                    jnp.full((RANK, span), clip_ref[2 * first + i]) == a,
                    total[i * RANK : (i + 1) * RANK],
                    0.0,
                )
                for i in range(2)
            ]
            gr_ref[first, pl.ds(a * RANK, RANK)] = chosen[0] + chosen[1]
    for yx in range(4):
        core_move(yx).wait_send()
        for zz in range(4):
            copy, slot = owner_move(yx, zz)

            @pl.when(slot != 0)
            def _():
                copy.wait_send()

    tok_move.wait_send()
    cot_move.wait_send()
    for j in range(1, 4):
        ad_move(j).wait_send()

    for q in (1, 2, 3, 6, 7, 8, 9, 10, 11):
        z_move(q).wait_send()
    for q in range(4):
        for what in range(9):
            move(q, what).wait_send()

    @pl.loop(4, 12)
    def _(q):
        for what in range(9):
            move(q, what).wait_send()

    for what in range(9):
        move(None, what).wait_send()
    act_move.wait_send()
    for f in range(2):
        ing_moves[f].wait()
    give(ing_ref, own_ing, irecv)


def finish_kernel(
    act_ref, ing_ref, gr_ref, table_ref, one_ref, two_ref, act_out, ing_out, *outs
):
    act_out[...] = act_ref[...]
    ing_out[...] = ing_ref[...]
    results = adam(gr_ref[0] + gr_ref[1], table_ref[...], one_ref[...], two_ref[...])
    for out, result in zip(outs, results):
        out[...] = result


def fused(
    tokens,
    cotangent,
    clip_adapter,
    gain_one,
    gain_two,
    w_qkv,
    w_out,
    w_up,
    w_down,
    adapters,
    moment_one,
    moment_two,
):
    micro_count, shard_rows, width = tokens.shape
    rank_all, span = adapters.shape
    rows = 4 * HALF_PITCH
    frame_rows = 2 * HALF_PITCH
    local = width // 4
    bf, f32 = jnp.bfloat16, jnp.float32
    vmem = pl.BlockSpec(memory_space=pltpu.VMEM)
    smem = pl.BlockSpec(memory_space=pltpu.SMEM)
    scratch = [
        pltpu.VMEM((4, 3, 2, 2, 2, 96, width), bf),
        pltpu.VMEM((2, 2, 2, 2, 32, width), bf),
        pltpu.VMEM((4, HALF_SLOT, width), bf),
        pltpu.VMEM((4, HALF_SLOT, width), bf),
        pltpu.VMEM((2, HALF_SLOT, width), bf),
        pltpu.VMEM((2, HALF_SLOT, width), bf),
        pltpu.VMEM((rows, width), f32),
        pltpu.VMEM((rows, width), bf),
        pltpu.VMEM((rows, width), bf),
        pltpu.VMEM((rows, width), bf),
        pltpu.VMEM((4, rows, width), bf),
        pltpu.VMEM((4, 6, frame_rows, frame_rows), bf),
        pltpu.VMEM((4, rows, local), bf),
        pltpu.VMEM((rows, width), f32),
        pltpu.VMEM((rows, width), f32),
        pltpu.VMEM((rows, width), f32),
        pltpu.VMEM((rows, width), f32),
        pltpu.VMEM((2, rows, width), bf),
        pltpu.VMEM((rows, width), bf),
        pltpu.VMEM((2, 4, 2 * HALF_SLOT, width), bf),
        pltpu.VMEM((2, 2 * HALF_SLOT, 32), bf),
        pltpu.VMEM((rows, 32), f32),
        pltpu.VMEM((4, 32, width), bf),
        pltpu.VMEM((4, 32, local), bf),
        pltpu.VMEM((4, 32, width), bf),
        pltpu.VMEM((4, 32, width), bf),
        pltpu.VMEM((2, 2, 2, 2, 32, width), bf),
        pltpu.VMEM((4, 2, 32, width), bf),
        pltpu.VMEM((4, 2, 32, width), bf),
        pltpu.VMEM((16, 32, span), bf),
        pltpu.VMEM((2, HALF_SLOT, width), bf),
        pltpu.VMEM((2, HALF_SLOT, width), bf),
        pltpu.VMEM((2, HALF_PITCH, width), bf),
        pltpu.VMEM((2, HALF_PITCH, width), bf),
        pltpu.VMEM((2, HALF_SLOT, width), bf),
        pltpu.VMEM((2, HALF_SLOT, width), bf),
        pltpu.VMEM((2, 32, span), bf),
        pltpu.VMEM((8, rows, 32), bf),
        pltpu.SemaphoreType.DMA((3, 4)),
        pltpu.SemaphoreType.DMA((3, 4)),
        pltpu.SemaphoreType.DMA((4,)),
        pltpu.SemaphoreType.DMA((4,)),
        pltpu.SemaphoreType.DMA((13, 9)),
        pltpu.SemaphoreType.DMA((13, 9)),
        pltpu.SemaphoreType.DMA((5,)),
        pltpu.SemaphoreType.DMA((5,)),
        pltpu.SemaphoreType.DMA((4,)),
        pltpu.SemaphoreType.DMA((4,)),
        pltpu.SemaphoreType.DMA((4, 4)),
        pltpu.SemaphoreType.DMA((16,)),
    ]
    act, ing, grads = pl.pallas_call(
        fused_kernel,
        out_shape=(
            jax.ShapeDtypeStruct((shard_rows, micro_count, width), bf),
            jax.ShapeDtypeStruct((shard_rows, micro_count, width), bf),
            jax.ShapeDtypeStruct((2, rank_all, span), f32),
        ),
        in_specs=[vmem] * 9 + [smem],
        out_specs=(vmem, vmem, vmem),
        scratch_shapes=scratch,
        compiler_params=pltpu.CompilerParams(
            collective_id=0, has_side_effects=True, vmem_limit_bytes=60 * 2**20
        ),
    )(
        tokens.transpose(1, 0, 2),
        cotangent.transpose(1, 0, 2),
        gain_one,
        gain_two,
        w_qkv.transpose(1, 0, 2),
        w_out,
        w_up,
        w_down.T,
        adapters,
        clip_adapter,
    )
    plain = jax.ShapeDtypeStruct((rank_all, span), f32)
    rows_spec = pl.BlockSpec((shard_rows // 2, micro_count, width), lambda i: (i, 0, 0))
    plain_spec = pl.BlockSpec((rank_all // 2, span), lambda i: (i, 0))
    act, ing, *others = pl.pallas_call(
        finish_kernel,
        out_shape=(act, ing) + (plain,) * 4 + (jax.ShapeDtypeStruct((rank_all, span), bf),),
        grid=(2,),
        in_specs=[rows_spec] * 2
        + [pl.BlockSpec((2, rank_all // 2, span), lambda i: (0, i, 0))]
        + [plain_spec] * 3,
        out_specs=(rows_spec,) * 2 + (plain_spec,) * 5,
    )(act, ing, grads, adapters, moment_one, moment_two)
    return (act.transpose(1, 0, 2), ing.transpose(1, 0, 2), *others)


def layer(tokens, *others):
    w_up = others[6]
    sizes = lax.axis_size("dp"), lax.axis_size("mp")
    frames_micro = tokens.shape[1] * sizes[0] * sizes[1] // FRAME
    fits = (
        sizes == (8, 4)
        and tokens.shape[0] == 4
        and 2 * tokens.shape[1] == FRAME
        and frames_micro == CLIP_FRAMES
        and w_up.shape == (tokens.shape[2] // 8, tokens.shape[2])
    )
    return (fused if fits else shards)(tokens, *others)


def solution(mesh):
    spread = P(None, ("dp", "mp"))
    rows = P(None, ("dp", "mp"), None)
    return jax.shard_map(
        layer,
        mesh=mesh,
        in_specs=(
            rows,
            rows,
            P(),
            P(),
            P(),
            P("dp", None, "mp"),
            P("mp", "dp"),
            P("dp", "mp"),
            P("mp", "dp"),
            spread,
            spread,
            spread,
        ),
        out_specs=(rows, rows, spread, spread, spread, spread, spread),
        check_vma=False,
    )
```
